32 devices in a mesh: rep: 8 (over z, y), kv: 4 (over x, core).
Axes of the slice: x: 2, y: 2, z: 4, core: 2. Of those that a mesh axis runs over, the one named last changes fastest.
Arguments:
- tokens: bfloat16 [12288, 1024], P('rep'), may hold values from -6 to 6
- cotangent: bfloat16 [12288, 1024], P('rep'), may hold values from -6 to 6
- lengths: int32 [8, 6], P('rep'), may hold values from 1 to 1024, 1536 in all within a row
- block_gains: float32 [2, 1024], replicated, may hold values from 0.5 to 1.5
- block_velocity: float32 [2, 1024], replicated, may hold values from -64 to 64
- head_gains: float32 [2, 128], replicated, may hold values from 0.5 to 1.5
- head_velocity: float32 [2, 128], replicated, may hold values from -224 to 224
- weight_query: float32 [1024, 2048], P('rep', 'kv'), may hold values from -0.1875 to 0.1875
- velocity_query: float32 [1024, 2048], P('rep', 'kv'), may hold values from -6 to 6
- error_query: float32 [8, 1024, 2048], P('rep', None, 'kv'), may hold values from -48 to 48
- factor_query: float32 [2048, 8], P('kv'), may hold values from -6 to 6
- weight_keyval: float32 [2, 1024, 1024], P(None, 'rep', 'kv'), may hold values from -0.1875 to 0.1875
- velocity_keyval: float32 [2, 1024, 1024], P(None, 'rep', 'kv'), may hold values from -6 to 6
- error_keyval: float32 [8, 2, 1024, 1024], P('rep', None, None, 'kv'), may hold values from -48 to 48
- factor_keyval: float32 [2, 1024, 8], P(None, 'kv'), may hold values from -6 to 6
- weight_out: float32 [2048, 1024], P(('kv', 'rep')), may hold values from -2 to 2
- velocity_out: float32 [2048, 1024], P(('kv', 'rep')), may hold values from -6 to 6
- error_out: float32 [8, 2048, 1024], P('rep', 'kv'), may hold values from -48 to 48
- factor_out: float32 [4, 1024, 8], P('kv'), may hold values from -6 to 6
- weight_gateup: float32 [2, 1024, 3072], P(None, 'rep', 'kv'), may hold values from -0.1875 to 0.1875
- velocity_gateup: float32 [2, 1024, 3072], P(None, 'rep', 'kv'), may hold values from -6 to 6
- error_gateup: float32 [8, 2, 1024, 3072], P('rep', None, None, 'kv'), may hold values from -48 to 48
- factor_gateup: float32 [2, 3072, 8], P(None, 'kv'), may hold values from -6 to 6
- weight_down: float32 [3072, 1024], P(('kv', 'rep')), may hold values from -0.109375 to 0.109375
- velocity_down: float32 [3072, 1024], P(('kv', 'rep')), may hold values from -6 to 6
- error_down: float32 [8, 3072, 1024], P('rep', 'kv'), may hold values from -48 to 48
- factor_down: float32 [4, 1024, 8], P('kv'), may hold values from -6 to 6
Outputs:
- layer_out: bfloat16 [12288, 1024], P(('rep', 'kv'))
- input_grad: float32 [12288, 1024], P(('rep', 'kv'))
- new_block_gains: float32 [2, 1024], replicated
- new_block_velocity: float32 [2, 1024], replicated
- new_head_gains: float32 [2, 128], replicated
- new_head_velocity: float32 [2, 128], replicated
- new_weight_query: float32 [1024, 2048], P('rep', 'kv')
- new_velocity_query: float32 [1024, 2048], P('rep', 'kv')
- new_error_query: float32 [8, 1024, 2048], P('rep', None, 'kv')
- left_query: float32 [4, 1024, 8], P('kv')
- right_query: float32 [2048, 8], P('kv')
- new_weight_keyval: float32 [2, 1024, 1024], P(None, 'rep', 'kv')
- new_velocity_keyval: float32 [2, 1024, 1024], P(None, 'rep', 'kv')
- new_error_keyval: float32 [8, 2, 1024, 1024], P('rep', None, None, 'kv')
- left_keyval: float32 [2, 4, 1024, 8], P(None, 'kv')
- right_keyval: float32 [2, 1024, 8], P(None, 'kv')
- new_weight_out: float32 [2048, 1024], P(('kv', 'rep'))
- new_velocity_out: float32 [2048, 1024], P(('kv', 'rep'))
- new_error_out: float32 [8, 2048, 1024], P('rep', 'kv')
- left_out: float32 [2048, 8], P('kv')
- right_out: float32 [4, 1024, 8], P('kv')
- new_weight_gateup: float32 [2, 1024, 3072], P(None, 'rep', 'kv')
- new_velocity_gateup: float32 [2, 1024, 3072], P(None, 'rep', 'kv')
- new_error_gateup: float32 [8, 2, 1024, 3072], P('rep', None, None, 'kv')
- left_gateup: float32 [2, 4, 1024, 8], P(None, 'kv')
- right_gateup: float32 [2, 3072, 8], P(None, 'kv')
- new_weight_down: float32 [3072, 1024], P(('kv', 'rep'))
- new_velocity_down: float32 [3072, 1024], P(('kv', 'rep'))
- new_error_down: float32 [8, 3072, 1024], P('rep', 'kv')
- left_down: float32 [3072, 8], P('kv')
- right_down: float32 [4, 1024, 8], P('kv')
The draws below stay inside these ranges and needn't reach their ends.
Inputs may be any that keep to these rules, and one draw needn't show every extreme that they name: Each row of lengths sums to 1536, and its largest entry is 1024.
All inputs are finite; a program needn't handle non-finite values.
Results may differ from the reference program's by a relative error of at most 0.023.
Values may be sent and summed in bfloat16 or wider, within the bound.
No kernel may reach another device: no remote copies, remote signals or barrier semaphores. Data moves between devices by JAX's collectives and lax.ppermute only.
A program may use at most 256 MiB of HBM per device.

```python
import math
import jax
import jax.numpy as jnp
import numpy as np
from jax import lax

D = 1024
NH = 16
KVH = 8
HD = 128
FF = 3072
RANK = 8
TOK_DEV = 1536
DOCS = 6
MOST = 1024
QD = 2048
KD = 1024
REPS = 8
SHARDS = 4
TOKENS = 12288


def level_of(key, shape, split, low, largest):
    loudness = 1.0
    for axis_at, shards_of in split:
        draws = jax.random.uniform(jax.random.fold_in(jax.random.fold_in(key, 6), axis_at), (shards_of,), jnp.float32, low / len(split), largest / len(split))
        loudness = loudness * jnp.repeat(jnp.exp(draws), shape[axis_at] // shards_of).reshape((-1,) + (1,) * (len(shape) - 1 - axis_at))
    return loudness


def profile(number_of, total, reach, skew):
    portions = [(1 << 20) // math.isqrt(rank ** skew) + 1 for rank in range(2, number_of + 1)]
    spare, counts = total - reach - (number_of - 1), [1] * (number_of - 1)
    while spare > 0:
        free = [i for i in range(number_of - 1) if counts[i] < reach]
        whole, budget = sum([portions[i] for i in free]), spare
        for i in free:
            more = min(reach - counts[i], max(1, budget * portions[i] // whole), spare)
            counts[i] = counts[i] + more
            spare = spare - more
    return np.array([reach] + counts)


def ragged_sizes(rng, count, total, bound, slope):
    if count == 2:
        one = jax.random.randint(rng, (), max(1, total - bound), min(bound, total - 1) + 1)
        return jnp.stack([one, total - one])
    tallies = jnp.asarray(profile(count, total, bound, slope), jnp.int32)
    couples = (count - 1) // 2
    donor, sink = tallies[1:1 + 2 * couples:2], tallies[2:2 + 2 * couples:2]
    room = jnp.minimum(donor - 1, bound - sink)
    shifted = jax.random.randint(jax.random.fold_in(rng, 1), (couples,), 0, 1 << 20) % (room + 1)
    tallies = tallies.at[1:1 + 2 * couples:2].set(donor - shifted).at[2:2 + 2 * couples:2].set(sink + shifted)
    return tallies[jax.random.permutation(jax.random.fold_in(rng, 2), count)]


def normal_values(key, dims, scale, most, cuts=(), held_as=jnp.bfloat16):
    array = jax.random.normal(key, dims, jnp.float32) * scale
    if len(cuts) > 0:
        array = level_of(key, dims, cuts, -0.22, 0.18) * array
    return jnp.clip(array, min=-most, max=most).astype(held_as)


def setup_inputs(seed: int = 0) -> dict:
    key_of = jax.random.split(jax.random.key(seed), 28)
    tokens = normal_values(key_of[0], (TOKENS, D), 1.0, 6.0, ((0, 8),))
    cotangent = normal_values(key_of[1], (TOKENS, D), 1.0, 6.0, ((0, 8),))
    lengths = jax.vmap(lambda own: ragged_sizes(own, DOCS, TOK_DEV, MOST, 2))(jax.random.split(key_of[2], REPS)).reshape((REPS, DOCS)).astype(jnp.int32)
    block_gains = jnp.clip(1.0 + 0.1 * jax.random.normal(key_of[3], (2, D), jnp.float32), 0.5, 1.5)
    block_velocity = normal_values(key_of[4], (2, D), (0.3 * TOK_DEV ** 0.5), 64.0, (), jnp.float32)
    head_gains = jnp.clip(1.0 + 0.1 * jax.random.normal(key_of[5], (2, HD), jnp.float32), 0.5, 1.5)
    head_velocity = normal_values(key_of[6], (2, HD), (1.0 * TOK_DEV ** 0.5), 224.0, (), jnp.float32)
    weight_query = normal_values(key_of[7], (D, QD), D ** -0.5, 0.1875, ((0, 8), (1, 4)), jnp.float32)
    velocity_query = normal_values(key_of[8], (D, QD), (0.02 * TOK_DEV ** 0.5), 6.0, ((0, 8), (1, 4)), jnp.float32)
    error_query = normal_values(key_of[9], (REPS, D, QD), (0.2 * TOK_DEV ** 0.5), 48.0, ((0, 8), (2, 4)), jnp.float32)
    factor_query = normal_values(key_of[10], (QD, RANK), 1.0, 6.0, ((0, 4),), jnp.float32)
    weight_keyval = normal_values(key_of[11], (2, D, KD), D ** -0.5, 0.1875, ((1, 8), (2, 4)), jnp.float32)
    velocity_keyval = normal_values(key_of[12], (2, D, KD), (0.02 * TOK_DEV ** 0.5), 6.0, ((1, 8), (2, 4)), jnp.float32)
    error_keyval = normal_values(key_of[13], (REPS, 2, D, KD), (0.2 * TOK_DEV ** 0.5), 48.0, ((0, 8), (3, 4)), jnp.float32)
    factor_keyval = normal_values(key_of[14], (2, KD, RANK), 1.0, 6.0, ((1, 4),), jnp.float32)
    weight_out = normal_values(key_of[15], (QD, D), (max(QD * 8 // TOK_DEV, 1)) ** -0.5, 2.0, ((0, 32),), jnp.float32)
    velocity_out = normal_values(key_of[16], (QD, D), (0.02 * TOK_DEV ** 0.5), 6.0, ((0, 32),), jnp.float32)
    error_out = normal_values(key_of[17], (REPS, QD, D), (0.2 * TOK_DEV ** 0.5), 48.0, ((0, 8), (1, 4)), jnp.float32)
    factor_out = normal_values(key_of[18], (SHARDS, D, RANK), 1.0, 6.0, ((0, 4),), jnp.float32)
    weight_gateup = normal_values(key_of[19], (2, D, FF), D ** -0.5, 0.1875, ((1, 8), (2, 4)), jnp.float32)
    velocity_gateup = normal_values(key_of[20], (2, D, FF), (0.02 * TOK_DEV ** 0.5), 6.0, ((1, 8), (2, 4)), jnp.float32)
    error_gateup = normal_values(key_of[21], (REPS, 2, D, FF), (0.2 * TOK_DEV ** 0.5), 48.0, ((0, 8), (3, 4)), jnp.float32)
    factor_gateup = normal_values(key_of[22], (2, FF, RANK), 1.0, 6.0, ((1, 4),), jnp.float32)
    weight_down = normal_values(key_of[23], (FF, D), FF ** -0.5, 0.109375, ((0, 32),), jnp.float32)
    velocity_down = normal_values(key_of[24], (FF, D), (0.02 * TOK_DEV ** 0.5), 6.0, ((0, 32),), jnp.float32)
    error_down = normal_values(key_of[25], (REPS, FF, D), (0.2 * TOK_DEV ** 0.5), 48.0, ((0, 8), (1, 4)), jnp.float32)
    factor_down = normal_values(key_of[26], (SHARDS, D, RANK), 1.0, 6.0, ((0, 4),), jnp.float32)
    return dict(tokens=tokens, cotangent=cotangent, lengths=lengths, block_gains=block_gains, block_velocity=block_velocity, head_gains=head_gains, head_velocity=head_velocity, weight_query=weight_query, velocity_query=velocity_query, error_query=error_query, factor_query=factor_query, weight_keyval=weight_keyval, velocity_keyval=velocity_keyval, error_keyval=error_keyval, factor_keyval=factor_keyval, weight_out=weight_out, velocity_out=velocity_out, error_out=error_out, factor_out=factor_out, weight_gateup=weight_gateup, velocity_gateup=velocity_gateup, error_gateup=error_gateup, factor_gateup=factor_gateup, weight_down=weight_down, velocity_down=velocity_down, error_down=error_down, factor_down=factor_down)


@jax.custom_vjp
def low(v):
    return lax.optimization_barrier(v.astype(jnp.bfloat16)).astype(jnp.float32)

@jax.custom_vjp
def low_back(v):
    return v

def low_keep(v):
    return (low(v), None)

def low_pass(kept, grad):
    return (grad,)

def back_keep(v):
    return (v, None)

def back_low(kept, grad):
    return (low(grad),)
low.defvjp(low_keep, low_pass)
low_back.defvjp(back_keep, back_low)
EPSILON = 1e-06
ROPE_BASE = 1000000.0
MOMENTUM = 0.9
STEP_RATE = 0.04
GAIN_RATE = 0.005
NEGATIVE = -1e+30
HIGHEST = lax.Precision.HIGHEST

def dense_high(left_side, right_side):
    return jnp.dot(left_side, right_side, precision=HIGHEST, preferred_element_type=jnp.float32)

def precise(form, left_side, right_side):
    return jnp.einsum(form, left_side, right_side, precision=HIGHEST, preferred_element_type=jnp.float32)

def norm_scale(values, gain):
    return values * lax.rsqrt(lax.optimization_barrier(jnp.mean(values * values, axis=-1, keepdims=True)) + EPSILON) * gain

def turned(values):
    half_width = values.shape[-1] // 2
    return jnp.concatenate([-values[..., half_width:], values[..., :half_width]], axis=-1)

def rotate(values, cosine, sine):
    return values * cosine + turned(values) * sine

def doc_layout(lengths_row, row_count):
    doc_ends = jnp.cumsum(lengths_row, dtype=jnp.int32)
    places = jnp.arange(row_count, dtype=jnp.int32)
    passed = (places[:, None] >= doc_ends[None, :]).astype(jnp.int32)
    document = lax.optimization_barrier(jnp.sum(passed, axis=1, dtype=jnp.int32))
    doc_start = lax.optimization_barrier(jnp.sum(passed * lengths_row[None, :], axis=1, dtype=jnp.int32))
    return (document, places - doc_start)

def rope_tables(position, head_width):
    half_index = jnp.arange(head_width // 2, dtype=jnp.float32)
    frequency = ROPE_BASE ** (-2.0 * half_index / head_width)
    angles = position.astype(jnp.float32)[:, None] * frequency[None, :]
    angles = jnp.concatenate([angles, angles], axis=1)
    return (jnp.cos(angles), jnp.sin(angles))

def forward(row_block, weights, gains, document, cosine, sine):
    weight_query, weight_keyval, weight_out, weight_gateup, weight_down = weights
    block_gains, head_gains = gains
    row_count = row_block.shape[0]
    hidden_first = low(norm_scale(row_block, block_gains[0]))
    query_heads = low_back(dense_high(hidden_first, low(weight_query))).reshape(row_count, NH, HD)
    key_heads = low_back(dense_high(hidden_first, low(weight_keyval[0]))).reshape(row_count, KVH, HD)
    value_heads = low_back(dense_high(hidden_first, low(weight_keyval[1]))).reshape(row_count, KVH, HD)
    query_heads = low(rotate(norm_scale(query_heads, head_gains[0]), cosine[:, None, :], sine[:, None, :]))
    key_heads = low(rotate(norm_scale(key_heads, head_gains[1]), cosine[:, None, :], sine[:, None, :]))
    value_heads = low(value_heads)
    key_heads = jnp.repeat(key_heads, NH // KVH, axis=1)
    value_heads = jnp.repeat(value_heads, NH // KVH, axis=1)
    scores = low_back(jnp.einsum('qhd,khd->hqk', query_heads, key_heads, precision=HIGHEST) / math.sqrt(HD))
    places = jnp.arange(row_count, dtype=jnp.int32)
    allowed = (document[:, None] == document[None, :]) & (places[:, None] >= places[None, :])
    scores = jnp.where(allowed[None], scores, NEGATIVE)
    score_top = lax.optimization_barrier(jnp.max(scores, axis=-1, keepdims=True))
    weights_soft = jnp.exp(scores - score_top)
    weights_soft = weights_soft / lax.optimization_barrier(jnp.sum(weights_soft, axis=-1, keepdims=True))
    mixed_heads = low_back(jnp.einsum('hqk,khd->qhd', low(weights_soft), value_heads, precision=HIGHEST))
    mixed_heads = low(mixed_heads).reshape(row_count, NH * HD)
    middle = row_block + low_back(dense_high(mixed_heads, low(weight_out)))
    hidden_second = low(norm_scale(middle, block_gains[1]))
    gate_values = low_back(dense_high(hidden_second, low(weight_gateup[0])))
    up_values = low_back(dense_high(hidden_second, low(weight_gateup[1])))
    active = low(jax.nn.silu(gate_values) * up_values)
    return middle + dense_high(active, low(weight_down))

def merge_rows(parts):
    return parts.reshape(parts.shape[:-3] + (parts.shape[-3] * parts.shape[-2], parts.shape[-1]))

def blocked(matrix, split_cols):
    if split_cols:
        parts = matrix.reshape(matrix.shape[:-1] + (SHARDS, matrix.shape[-1] // SHARDS))
        return jnp.moveaxis(parts, -2, -3)
    return matrix.reshape(matrix.shape[:-2] + (SHARDS, matrix.shape[-2] // SHARDS, matrix.shape[-1]))

def unblocked(parts, split_cols):
    if split_cols:
        joined = jnp.moveaxis(parts, -3, -2)
        return joined.reshape(joined.shape[:-2] + (joined.shape[-2] * joined.shape[-1],))
    return merge_rows(parts)

def start_blocks(start, split_cols):
    if split_cols:
        return start.reshape(start.shape[:-2] + (SHARDS, start.shape[-2] // SHARDS, start.shape[-1]))
    return start

def orthonormal(panel):
    columns = []
    for column_index in range(panel.shape[-1]):
        column = panel[..., column_index]
        for earlier in columns:
            column = column - lax.optimization_barrier(jnp.sum(earlier * column, axis=-1, keepdims=True)) * earlier
        column = column * lax.rsqrt(lax.optimization_barrier(jnp.sum(column * column, axis=-1, keepdims=True)) + EPSILON)
        columns.append(column)
    return jnp.stack(columns, axis=-1)

def reference(tokens, cotangent, lengths, block_gains, block_velocity, head_gains, head_velocity, weight_query, velocity_query, error_query, factor_query, weight_keyval, velocity_keyval, error_keyval, factor_keyval, weight_out, velocity_out, error_out, factor_out, weight_gateup, velocity_gateup, error_gateup, factor_gateup, weight_down, velocity_down, error_down, factor_down):
    masters = (weight_query, weight_keyval, weight_out, weight_gateup, weight_down)
    velocities = (velocity_query, velocity_keyval, velocity_out, velocity_gateup, velocity_down)
    errors = (error_query, error_keyval, error_out, error_gateup, error_down)
    starts = (factor_query, factor_keyval, factor_out, factor_gateup, factor_down)
    splits = (True, True, False, True, False)
    start_parts = tuple((start_blocks(start, split_cols) for start, split_cols in zip(starts, splits)))
    inputs = tokens.astype(jnp.float32).reshape(REPS, TOK_DEV, D)
    backs = cotangent.astype(jnp.float32).reshape(REPS, TOK_DEV, D)

    def replica_step(state_now, item):
        row_block, back_block, lengths_row, error_items = item
        document, position = doc_layout(lengths_row, TOK_DEV)
        cosine, sine = rope_tables(position, HD)

        def run_layer(inputs_now, weights_now, gains_now):
            return forward(inputs_now, weights_now, gains_now, document, cosine, sine)
        result, pull = jax.vjp(run_layer, row_block, masters, (block_gains, head_gains))
        grad_rows, grad_weights, grad_gains = pull(back_block)
        moments = tuple((grad_now + error_now for grad_now, error_now in zip(grad_weights, error_items)))
        left_sums = tuple((total + precise('...ij,...jk->...ik', blocked(moment, split_cols), start) for total, moment, start, split_cols in zip(state_now[1], moments, start_parts, splits)))
        gain_sums = (state_now[0][0] + grad_gains[0], state_now[0][1] + grad_gains[1])
        return ((gain_sums, left_sums), (result, grad_rows, moments))
    zero_lefts = tuple((jnp.zeros(blocked(master, split_cols).shape[:-1] + (RANK,), jnp.float32) for master, split_cols in zip(masters, splits)))
    zero_gains = (jnp.zeros((2, D), jnp.float32), jnp.zeros((2, HD), jnp.float32))
    (gain_sums, left_sums), (results, grad_inputs, moments) = lax.scan(replica_step, (zero_gains, zero_lefts), (inputs, backs, lengths, errors))
    new_block_velocity = MOMENTUM * block_velocity + gain_sums[0] / REPS
    new_block_gains = block_gains - GAIN_RATE * new_block_velocity
    new_head_velocity = MOMENTUM * head_velocity + gain_sums[1] / REPS
    new_head_gains = head_gains - GAIN_RATE * new_head_velocity
    outputs = [results.reshape(TOKENS, D).astype(jnp.bfloat16), grad_inputs.reshape(TOKENS, D), new_block_gains, new_block_velocity, new_head_gains, new_head_velocity]
    for kind_index in range(5):
        split_cols = splits[kind_index]
        left_part = orthonormal(left_sums[kind_index])
        stacked = blocked(moments[kind_index], split_cols)
        right_part = precise('n...ji,...jk->...ik', stacked, left_part) / REPS
        approx = precise('...ik,...jk->...ij', left_part, right_part)
        new_errors = unblocked(stacked - approx, split_cols)
        new_velocity = MOMENTUM * velocities[kind_index] + unblocked(approx, split_cols)
        new_weight = masters[kind_index] - STEP_RATE * new_velocity
        left_final = left_part if split_cols else merge_rows(left_part)
        right_final = merge_rows(right_part) if split_cols else right_part
        outputs.extend([new_weight, new_velocity, new_errors, left_final, right_final])
    return tuple(outputs)
```

```python
import functools
import math

import jax
import jax.numpy as jnp
from jax import lax
from jax.experimental import pallas as pl
from jax.experimental.pallas import tpu as pltpu
from jax.sharding import PartitionSpec as P

EPSILON = 1e-06
ROPE_BASE = 1000000.0
MOMENTUM = 0.9
STEP_RATE = 0.04
GAIN_RATE = 0.005
PIECE = 128
QUERIES = 256
KEYS = 512
F32 = jnp.float32
BF16 = jnp.bfloat16
VMEM_LIMIT = 56 * 1024 * 1024


def nn(left, right):
    return lax.dot_general(left, right, (((1,), (0,)), ((), ())), preferred_element_type=F32)


def nt(left, right):
    return lax.dot_general(left, right, (((1,), (1,)), ((), ())), preferred_element_type=F32)


def tn(left, right):
    return lax.dot_general(left, right, (((0,), (0,)), ((), ())), preferred_element_type=F32)


def params(limit=VMEM_LIMIT):
    return pltpu.CompilerParams(vmem_limit_bytes=limit)


def cost(flops, moved, exps=0):
    return pl.CostEstimate(flops=int(flops / 8), bytes_accessed=int(moved / 8), transcendentals=0)


def sds(shape, dtype):
    return jax.ShapeDtypeStruct(shape, dtype)


VM = pl.BlockSpec(memory_space=pltpu.VMEM)
SM = pl.BlockSpec(memory_space=pltpu.SMEM)
ANY = pl.BlockSpec(memory_space=pl.ANY)


def flip_kv(value, bit):
    size = lax.axis_size("kv")
    return lax.ppermute(value, "kv", [(i, i ^ bit) for i in range(size)])


def flip_rep(value, bit):
    size = lax.axis_size("rep")
    return lax.ppermute(value, "rep", [(i, i ^ bit) for i in range(size)])


def after(value, *earlier):
    return lax.optimization_barrier((value, *earlier))[0]


def rounded(value):
    return lax.reduce_precision(value, exponent_bits=8, mantissa_bits=7)


def sum_rep_low(value):
    bit = 1
    while bit < lax.axis_size("rep"):
        held = rounded(value)
        value = held + flip_rep(held.astype(BF16), bit).astype(F32)
        bit *= 2
    return value


def xor_codes(bits):
    codes = (0,)
    for bit in bits:
        codes = codes + tuple(code ^ bit for code in codes)
    return codes


def spread(value, bits):
    for bit in bits[:-1]:
        value = jnp.concatenate([value, flip_rep(value, bit)], axis=0)
    codes = xor_codes(bits)
    middle = len(codes) // 2
    return [(value, codes[:middle]), (flip_rep(value, bits[-1]), codes[middle:])]


def gather_halves(chunk):
    replicas = lax.axis_size("rep")
    falling = [1 << i for i in range(replicas.bit_length() - 2, -1, -1)]
    rows = chunk.shape[0]
    if rows % 32 != 0:
        return [part + (0,) for part in spread(chunk, falling)]
    rising = falling[-1:] + falling[:-1]
    first = [part + (0,) for part in spread(chunk[: rows // 2], falling)]
    return first + [part + (rows // 2,) for part in spread(chunk[rows // 2 :], rising)]


def piece_copies(rep, layout, refs, target, sems):
    share = target.shape[0] // sum(len(codes) for codes, offset in layout if offset == 0)
    copies = []
    for (codes, offset), ref in zip(layout, refs):
        rows = ref.shape[0] // len(codes)
        for at, code in enumerate(codes):
            first = pl.multiple_of(lax.bitwise_xor(rep, code) * share + offset, 8)
            copies.append(
                pltpu.make_async_copy(
                    ref.at[pl.ds(at * rows, rows), :], target.at[pl.ds(first, rows), :], sems.at[len(copies)]
                )
            )
    return copies


def pack_feed(gateup, down):
    depth = down.shape[1]
    rows = gateup.shape[0]
    rest = gateup[:, depth:]
    rest = jnp.concatenate([rest[: rows // 2], rest[rows // 2 :]], axis=1)
    return jnp.concatenate([gateup[:, :depth], rest, down], axis=0)


def feed_copies(packed, gateup, down, sems):
    replicas = packed.shape[0]
    depth = down.shape[1]
    rows, low_rows = gateup.shape[0] // replicas, down.shape[0] // replicas
    half = rows // 2
    rest = gateup.shape[1] - depth
    first, second = [], []
    for at in range(replicas):
        top = at * rows
        pairs = [
            (packed.at[at, 0:rows, :], gateup.at[top : top + rows, 0:depth]),
            (packed.at[at, rows : rows + half, 0:rest], gateup.at[top : top + half, depth : depth + rest]),
            (packed.at[at, rows : rows + half, rest : 2 * rest], gateup.at[top + half : top + rows, depth : depth + rest]),
        ]
        first += [pltpu.make_async_copy(x, y, sems.at[at * 4 + i]) for i, (x, y) in enumerate(pairs)]
        second.append(
            pltpu.make_async_copy(
                packed.at[at, rows + half : rows + half + low_rows, :],
                down.at[at * low_rows : (at + 1) * low_rows, :],
                sems.at[at * 4 + 3],
            )
        )
    return first, second


def start_all(copies):
    for copy in copies:
        copy.start()


def wait_all(copies):
    for copy in copies:
        copy.wait()


def unit_of(values):
    scale = lax.rsqrt(jnp.mean(values * values, axis=-1, keepdims=True) + EPSILON)
    return values * scale, scale


def norm_back(grad, unit, scale, gain):
    weighted = grad * gain
    return scale * (weighted - unit * jnp.mean(weighted * unit, axis=-1, keepdims=True))


def forward_kernel(layout, rep, meta, tok_ref, gain_ref, head_ref, cos_ref, sin_ref, start_ref, *refs):
    pieces = refs[: len(layout)]
    hid_out, q_out, raw_out, k_out, kt_out, v_out, mixed_out, log_ref = refs[len(layout) : len(layout) + 8]
    (tok_s, w_s, hid_s, q_s, raw_s, k_s, kt_s, v_s, vt_s, mixed_s, out_acc, sum_acc) = refs[len(layout) + 8 : -3]
    in_sems, w_sems, out_sems = refs[-3:]
    heads, total, width = q_s.shape
    groups = k_s.shape[0]
    pairs = heads // groups
    blocks = total // QUERIES
    factor = math.log2(math.e) / math.sqrt(width)

    def token_copy(block):
        here = pl.ds(pl.multiple_of(block * QUERIES, QUERIES), QUERIES)
        return pltpu.make_async_copy(tok_ref.at[here, :], tok_s.at[here, :], in_sems.at[block])

    def sent(block):
        here = pl.ds(pl.multiple_of(block * QUERIES, QUERIES), QUERIES)
        pairs_of = [
            (hid_s.at[here, :], hid_out.at[here, :]),
            (q_s.at[:, here, :], q_out.at[:, here, :]),
            (raw_s.at[:, here, :], raw_out.at[:, here, :]),
            (k_s.at[:, here, :], k_out.at[:, here, :]),
            (kt_s.at[:, :, here], kt_out.at[:, :, here]),
            (v_s.at[:, here, :], v_out.at[:, here, :]),
            (mixed_s.at[here, :], mixed_out.at[here, :]),
        ]
        return [pltpu.make_async_copy(x, y, out_sems.at[i, block]) for i, (x, y) in enumerate(pairs_of)]

    weights = piece_copies(rep[0], layout, pieces, w_s, w_sems)
    token_copy(0).start()
    start_all(weights)
    for block in range(1, blocks):
        token_copy(block).start()
    log_ref[...] = jnp.zeros_like(log_ref)
    vt_s[...] = jnp.zeros_like(vt_s)
    wait_all(weights)

    @pl.loop(0, blocks)
    def _(block):
        low, count = meta[block], meta[blocks + block]
        here = pl.ds(pl.multiple_of(block * QUERIES, QUERIES), QUERIES)
        token_copy(block).wait()
        unit, _ = unit_of(tok_s[here, :].astype(F32))
        hidden = (unit * gain_ref[...]).astype(BF16)
        hid_s[here, :] = hidden
        projected = nn(hidden, w_s[...])
        cosine, sine = cos_ref[here, :], sin_ref[here, :]
        means = jnp.full((width, width), 1.0 / width, BF16)
        for index in range(heads + groups):
            one = projected[:, index * width : (index + 1) * width]
            raw_s[index, here, :] = one.astype(BF16)
            gain = head_ref[0:1, :] if index < heads else head_ref[1:2, :]
            normed = one * lax.rsqrt(nn((one * one).astype(BF16), means) + EPSILON) * gain
            turned = normed * cosine + pltpu.roll(normed, width // 2, 1) * sine
            if index < heads:
                q_s[index, here, :] = turned.astype(BF16)
            else:
                k_s[index - heads, here, :] = turned.astype(BF16)
                kt_s[index - heads, :, here] = turned.T.astype(BF16)
        for index in range(groups):
            first = (heads + groups + index) * width
            one = projected[:, first : first + width]
            v_s[index, here, :] = one.astype(BF16)
            vt_s[index, :, here] = one.T.astype(BF16)

        start = jnp.concatenate([start_ref[:, here]] * pairs, axis=1)
        place = block * QUERIES + lax.broadcasted_iota(jnp.int32, (1, QUERIES), 1)
        place = jnp.concatenate([place] * pairs, axis=1)
        queries = [
            jnp.concatenate([q_s[g * pairs + j, here, :] for j in range(pairs)], axis=0) for g in range(groups)
        ]
        out_acc[...] = jnp.zeros_like(out_acc)
        sum_acc[...] = jnp.zeros_like(sum_acc)

        @pl.loop(0, count)
        def _(turn):
            base = pl.multiple_of(low + turn * KEYS, PIECE)
            key_place = base + lax.broadcasted_iota(jnp.int32, (KEYS, 1), 0)
            allowed = (key_place >= start) & (key_place <= place)
            for g in range(groups):
                scores = nt(k_s[g, pl.ds(base, KEYS), :], queries[g])
                weights = jnp.where(allowed, jnp.exp2(scores * factor), 0.0)
                sum_acc[g] += jnp.sum(weights, axis=0, keepdims=True)
                out_acc[g] += nn(vt_s[g, :, pl.ds(base, KEYS)], weights.astype(BF16))

        for g in range(groups):
            total_weight = sum_acc[g]
            mixed = out_acc[g] / total_weight
            logs = jnp.log2(total_weight)
            for j in range(pairs):
                head = g * pairs + j
                mixed_s[here, head * width : (head + 1) * width] = mixed[:, j * QUERIES : (j + 1) * QUERIES].T.astype(BF16)
                log_ref[head : head + 1, here] = logs[:, j * QUERIES : (j + 1) * QUERIES]
        start_all(sent(block))

    @pl.loop(0, blocks)
    def _(block):
        wait_all(sent(block))


def layout_of(pieces):
    return tuple((codes, offset) for _, codes, offset in pieces), [piece for piece, _, _ in pieces]


def slots(layout):
    return sum(len(codes) for codes, _ in layout)


def forward(rep, meta, tokens, gain, head_gains, cosine, sine, doc_start, pieces, heads, groups):
    total, depth = tokens.shape
    width = head_gains.shape[1]
    cols = pieces[0][0].shape[1]
    layout, arrays = layout_of(pieces)
    wide = heads // groups * QUERIES
    blocks = total // QUERIES
    outs = [
        (total, depth),
        (heads, total, width),
        (heads + groups, total, width),
        (groups, total, width),
        (groups, width, total),
        (groups, total, width),
        (total, heads * width),
    ]
    return pl.pallas_call(
        functools.partial(forward_kernel, layout),
        in_specs=[SM, SM, ANY] + [VM] * 5 + [ANY] * len(arrays),
        out_specs=[ANY] * 7 + [VM],
        out_shape=[sds(shape, BF16) for shape in outs] + [sds((8, total), F32)],
        scratch_shapes=[pltpu.VMEM((total, depth), BF16), pltpu.VMEM((depth, cols), BF16)]
        + [pltpu.VMEM(shape, BF16) for shape in outs[:6]]
        + [
            pltpu.VMEM((groups, width, total), BF16),
            pltpu.VMEM((total, heads * width), BF16),
            pltpu.VMEM((groups, width, wide), F32),
            pltpu.VMEM((groups, 1, wide), F32),
            pltpu.SemaphoreType.DMA((blocks,)),
            pltpu.SemaphoreType.DMA((slots(layout),)),
            pltpu.SemaphoreType.DMA((7, blocks)),
        ],
        compiler_params=params(),
        cost_estimate=cost(12e9, 20e6),
        name="attention_forward",
    )(rep, meta, tokens, gain, head_gains, cosine, sine, doc_start, *arrays)


def branch_kernel(layout, rep, core, mixed_ref, *refs):
    pieces = refs[: len(layout)]
    mine_out, other_out, w_s, mixed_s, out_s, sems, w_sems, out_sems = refs[len(layout) :]
    quarter = mixed_s.shape[1]
    loads = [
        pltpu.make_async_copy(mixed_ref.at[pl.ds(at * quarter, quarter), :], mixed_s.at[at], sems.at[at]) for at in range(4)
    ]
    weights = piece_copies(rep[0], layout, pieces, w_s, w_sems)
    start_all(weights + loads)
    wait_all(weights)
    lasts = []
    for step in range(4):
        spot = step % 2
        side = 1 - step // 2
        at = 2 * spot + lax.rem(core[0] + side, 2)
        if step == 0:
            wait_all(loads)
        out_s[step] = nn(mixed_s[at], w_s[...]).astype(BF16).reshape(out_s.shape[1:])
        lasts.append(
            pltpu.make_async_copy(out_s.at[step], (mine_out, other_out)[side].at[:, spot], out_sems.at[step])
        )
        lasts[-1].start()
    wait_all(lasts)


def branch(rep, core, mixed, pieces, depth):
    total, cols = mixed.shape
    layout, arrays = layout_of(pieces)
    parts = total // 4 // PIECE
    return pl.pallas_call(
        functools.partial(branch_kernel, layout),
        in_specs=[SM, SM] + [ANY] * (1 + len(arrays)),
        out_specs=[ANY, ANY],
        out_shape=[sds((parts, 2, PIECE, depth), BF16)] * 2,
        scratch_shapes=[
            pltpu.VMEM((cols, depth), BF16),
            pltpu.VMEM((4, total // 4, cols), BF16),
            pltpu.VMEM((4, parts, PIECE, depth), BF16),
            pltpu.SemaphoreType.DMA((4,)),
            pltpu.SemaphoreType.DMA((slots(layout),)),
            pltpu.SemaphoreType.DMA((4,)),
        ],
        compiler_params=params(),
        cost_estimate=cost(2 * total * cols * depth, 6e6),
        name="branch",
    )(rep, core, mixed, *arrays)


def feed_kernel(part, core, gain_ref, fgu_ref, fd_ref, here_ref, there_ref, tok_ref, cot_ref, packed_ref, *refs):
    mine_out, other_out, sum_ref, gu_left, d_left, down_out, hid_out, act_out, dgu_out = refs[-20:-11]
    mid_s, tok_s, cot_s, wgu_s, wd_s, terms_s, down_s, hid_s, act_s, dgu_s, sems = refs[-11:]
    units = wd_s.shape[0]
    spots = [(side, spot) for side in (1, 0) for spot in range(2)]
    spare = 4 * packed_ref.shape[0]

    def natural(ref, side, spot):
        return ref.at[spot, lax.rem(core[0] + side, 2), part]

    def rows(index):
        return pl.ds(index * PIECE, PIECE)

    first, cots, lasts = [], [], []
    for index, (side, spot) in enumerate(spots):
        at = spare + 8 * index
        source = (here_ref, there_ref)[side].at[spot]
        first.append(pltpu.make_async_copy(source, mid_s.at[rows(index), :], sems.at[at]))
        first.append(pltpu.make_async_copy(natural(tok_ref, side, spot), tok_s.at[rows(index), :], sems.at[at + 1]))
        cots.append(pltpu.make_async_copy(natural(cot_ref, side, spot), cot_s.at[rows(index), :], sems.at[at + 2]))
    gateups, downs = feed_copies(packed_ref, wgu_s, wd_s, sems)
    start_all(first + gateups + cots + downs)

    def send(scratch, target_of, kind):
        for index, (side, spot) in enumerate(spots):
            lasts.append(
                pltpu.make_async_copy(
                    scratch.at[rows(index), :], target_of(side, spot), sems.at[spare + 8 * index + 3 + kind]
                )
            )
            lasts[-1].start()

    wait_all(first)
    unit, _ = unit_of(tok_s[...].astype(F32) + mid_s[...].astype(F32))
    hid_s[...] = (unit * gain_ref[...]).astype(BF16)
    send(hid_s, lambda side, spot: natural(hid_out, side, spot), 0)
    wait_all(gateups)
    both = nn(hid_s[...], wgu_s[...])
    wait_all(cots + downs)
    grad_active = nt(cot_s[...], wd_s[...])
    gate, up = both[:, :units], both[:, units:]
    sig = jax.nn.sigmoid(gate)
    lit = gate * sig
    act_s[...] = (lit * up).astype(BF16)
    send(act_s, lambda side, spot: natural(act_out, side, spot), 1)
    dgu_s[:, :units] = (grad_active * up * sig * (1.0 + gate * (1.0 - sig))).astype(BF16)
    dgu_s[:, units:] = (grad_active * lit).astype(BF16)
    send(dgu_s, lambda side, spot: natural(dgu_out, side, spot), 2)
    terms = nt(dgu_s[...], wgu_s[...])
    terms_s[...] = terms.astype(BF16)
    send(terms_s, lambda side, spot: (mine_out, other_out)[side].at[spot], 3)
    down_s[...] = nn(act_s[...], wd_s[...]).astype(BF16)
    send(down_s, lambda side, spot: natural(down_out, side, spot), 4)
    sum_ref[...] = jnp.sum(terms * unit, axis=0, keepdims=True)
    gu_left[...] = tn(nn(dgu_s[...], fgu_ref[...]).astype(BF16), hid_s[...])
    d_left[...] = tn(nn(cot_s[...], fd_ref[...]).astype(BF16), act_s[...])
    wait_all(lasts)


def feed(part, parts, core, fgu, fd, here, there, tokens_cut, cot_cut, gain, packed, units, chain):
    depth = gain.shape[1]
    saved = (
        (2, 2, parts, PIECE, depth),
        (2, 2, parts, PIECE, depth),
        (2, 2, parts, PIECE, units),
        (2, 2, parts, PIECE, 2 * units),
    )
    rows = 4 * PIECE
    return pl.pallas_call(
        functools.partial(feed_kernel, part),
        in_specs=[SM, VM, VM, VM] + [ANY] * (5 + len(chain)),
        out_specs=[ANY, ANY, VM, VM, VM] + [ANY] * 4,
        out_shape=[sds((2, PIECE, depth), BF16)] * 2
        + [sds((1, depth), F32), sds((fgu.shape[1], depth), F32), sds((fd.shape[1], units), F32)]
        + [sds(shape, BF16) for shape in saved],
        scratch_shapes=[
            pltpu.VMEM((rows, depth), BF16),
            pltpu.VMEM((rows, depth), BF16),
            pltpu.VMEM((rows, depth), BF16),
            pltpu.VMEM((depth, 2 * units), BF16),
            pltpu.VMEM((units, depth), BF16),
            pltpu.VMEM((rows, depth), BF16),
            pltpu.VMEM((rows, depth), BF16),
            pltpu.VMEM((rows, depth), BF16),
            pltpu.VMEM((rows, units), BF16),
            pltpu.VMEM((rows, 2 * units), BF16),
            pltpu.SemaphoreType.DMA((4 * packed.shape[0] + 32,)),
        ],
        input_output_aliases={9 + i: 5 + i for i in range(len(chain))},
        compiler_params=params(),
        cost_estimate=cost(2 * 4 * PIECE * depth * units * 6, 12e6),
        name=f"feed_{part}",
    )(core, gain, fgu, fd, here, there, tokens_cut, cot_cut, packed, *chain)


def backward_kernel(layout, out_layout, parts, rep, meta, mid_gain, head_ref, cos_ref, sin_ref, start_ref, log_ref, fa_ref, fo_ref, *refs):
    (tok_ref, cot_ref, q_hbm, k_hbm, kt_hbm, v_hbm, raw_hbm, mixed_hbm) = refs[:8]
    mid_parts, grad_parts = refs[8 : 8 + 2 * parts], refs[8 + 2 * parts : 8 + 4 * parts]
    hid_hbm = refs[8 + 4 * parts]
    refs = refs[9 + 4 * parts :]
    pieces, out_pieces = refs[: len(layout)], refs[len(layout) : len(layout) + len(out_layout)]
    rest = refs[len(layout) + len(out_layout) :]
    (own_ref, own_mid, gb_out, grads_out, terms_out, query_sum, key_sum, first_sum, all_left, out_left) = rest[:10]
    (mid_s, grad_s, tok_s, cot_s, w_s, wo_s, q_s, k_s, kt_s, v_s, raw_s, mixed_s, hid_s, gb_s, all_s, terms_s, dk_s, dv_s, dq_acc) = rest[10:-5]
    row_sems, big_sems, w_sems, wo_sems, out_sems = rest[-5:]
    heads, total, width = q_s.shape
    groups = k_s.shape[0]
    pairs = heads // groups
    blocks, cuts = total // QUERIES, total // PIECE
    per = QUERIES // PIECE
    core, half = meta[2 * blocks + 2 * cuts], meta[2 * blocks + 2 * cuts + 1]
    root = 1.0 / math.sqrt(width)
    factor = math.log2(math.e) * root

    def row_copies(cut):
        quarter, part = cut // parts, cut % parts
        spot = quarter // 2
        here = pl.ds(cut * PIECE, PIECE)
        near = lax.rem(core + quarter, 2) == 0

        @pl.when(near)
        def _():
            pltpu.make_async_copy(mid_parts[2 * part].at[spot], mid_s.at[here, :], row_sems.at[0, cut]).start()
            pltpu.make_async_copy(grad_parts[2 * part].at[spot], grad_s.at[here, :], row_sems.at[1, cut]).start()

        @pl.when(jnp.logical_not(near))
        def _():
            pltpu.make_async_copy(mid_parts[2 * part + 1].at[spot], mid_s.at[here, :], row_sems.at[0, cut]).start()
            pltpu.make_async_copy(grad_parts[2 * part + 1].at[spot], grad_s.at[here, :], row_sems.at[1, cut]).start()

        pltpu.make_async_copy(tok_ref.at[here, :], tok_s.at[here, :], row_sems.at[2, cut]).start()
        pltpu.make_async_copy(cot_ref.at[here, :], cot_s.at[here, :], row_sems.at[3, cut]).start()

    big = [
        pltpu.make_async_copy(x, y, big_sems.at[i])
        for i, (x, y) in enumerate(
            [
                (k_hbm, k_s), (v_hbm, v_s), (q_hbm, q_s), (kt_hbm, kt_s), (mixed_hbm, mixed_s),
                (raw_hbm, raw_s), (hid_hbm, hid_s),
            ]
        )
    ]
    weights = piece_copies(rep[0], layout, pieces, w_s, w_sems)
    out_weights = piece_copies(rep[0], out_layout, out_pieces, wo_s, wo_sems)
    for cut in range(cuts - 1, cuts - 1 - per, -1):
        row_copies(cut)
    start_all(out_weights + big + weights)
    for cut in range(cuts - 1 - per, -1, -1):
        row_copies(cut)
    dk_s[...] = jnp.zeros_like(dk_s)
    dv_s[...] = jnp.zeros_like(dv_s)
    query_sum[...] = jnp.zeros_like(query_sum)
    key_sum[...] = jnp.zeros_like(key_sum)
    first_sum[...] = jnp.zeros_like(first_sum)
    all_left[...] = jnp.zeros_like(all_left)
    out_left[...] = jnp.zeros_like(out_left)
    ones = jnp.ones((8, width), F32)
    query_gain, key_gain = head_ref[0:1, :], head_ref[1:2, :]
    means = jnp.full((width, width), 1.0 / width, BF16)

    def mean_of(values):
        return nn(values.astype(BF16), means)

    def head_back(grad, raw, cosine, sine, gain):
        turned = grad * cosine - pltpu.roll(grad, width // 2, 1) * sine
        scale = lax.rsqrt(mean_of(raw * raw) + EPSILON)
        unit = raw * scale
        weighted = turned * gain
        back = scale * (weighted - unit * mean_of(weighted * unit))
        return back.astype(BF16), jnp.sum(turned * unit, axis=0, keepdims=True)

    def out_copies(block):
        here = pl.ds(pl.multiple_of(block * QUERIES, QUERIES), QUERIES)
        pairs_of = [(gb_s, gb_out), (all_s, grads_out), (terms_s, terms_out)]
        return [
            pltpu.make_async_copy(x.at[here, :], y.at[here, :], out_sems.at[i, block]) for i, (x, y) in enumerate(pairs_of)
        ]

    @pl.loop(0, blocks)
    def _(turn_of):
        block = blocks - 1 - turn_of
        low, count = meta[block], meta[blocks + block]
        rows = pl.ds(pl.multiple_of(block * QUERIES, QUERIES), QUERIES)
        for at in range(per):
            cut = block * per + at
            here = pl.ds(pl.multiple_of(cut * PIECE, PIECE), PIECE)
            for kind, target in enumerate((mid_s, grad_s, tok_s, cot_s)):
                pltpu.make_async_copy(tok_ref.at[here, :], target.at[here, :], row_sems.at[kind, cut]).wait()
        middle = tok_s[rows, :].astype(F32) + mid_s[rows, :].astype(F32)
        unit, scale = unit_of(middle)
        result = cot_s[rows, :].astype(F32) + norm_back(grad_s[rows, :].astype(F32), unit, scale, mid_gain[...])
        low_grad = result.astype(BF16)
        gb_s[rows, :] = low_grad
        for at in range(per):
            cut = block * per + at

            @pl.when(cut // parts == 2 * half + core)
            def _():
                own_ref[lax.rem(cut, parts)] = result[at * PIECE : (at + 1) * PIECE]
                own_mid[lax.rem(cut, parts)] = middle[at * PIECE : (at + 1) * PIECE]

        @pl.when(turn_of == 0)
        def _():
            wait_all(out_weights + big)

        grad_mixed = nt(low_grad, wo_s[...]).astype(BF16)
        mixed = mixed_s[rows, :]
        start = jnp.concatenate([start_ref[:, rows]] * pairs, axis=1)
        place = block * QUERIES + lax.broadcasted_iota(jnp.int32, (1, QUERIES), 1)
        place = jnp.concatenate([place] * pairs, axis=1)
        queries, grads, logs, deltas = [], [], [], []
        for g in range(groups):
            members = range(g * pairs, (g + 1) * pairs)
            queries.append(jnp.concatenate([q_s[h, rows, :] for h in members], axis=0))
            grad = jnp.concatenate([grad_mixed[:, h * width : (h + 1) * width] for h in members], axis=0)
            out = jnp.concatenate([mixed[:, h * width : (h + 1) * width] for h in members], axis=0)
            grads.append(grad)
            logs.append(jnp.concatenate([log_ref[h : h + 1, rows] for h in members], axis=1))
            terms = lax.dot_general(
                ones,
                grad.astype(F32) * out.astype(F32),
                (((1,), (1,)), ((), ())),
                precision=lax.Precision.HIGHEST,
                preferred_element_type=F32,
            )
            deltas.append(terms[0:1, :])
        dq_acc[...] = jnp.zeros_like(dq_acc)

        @pl.loop(0, count)
        def _(turn):
            base = pl.multiple_of(low + turn * KEYS, PIECE)
            key_place = base + lax.broadcasted_iota(jnp.int32, (KEYS, 1), 0)
            allowed = (key_place >= start) & (key_place <= place)
            keys = pl.ds(base, KEYS)
            for g in range(groups):
                scores = nt(k_s[g, keys, :], queries[g])
                weights = jnp.where(allowed, jnp.exp2(scores * factor - logs[g]), 0.0)
                grad_weights = nt(v_s[g, keys, :], grads[g])
                grad_scores = (weights * (grad_weights - deltas[g])).astype(BF16)
                dv_s[g, keys, :] += nn(weights.astype(BF16), grads[g])
                dk_s[g, keys, :] += nn(grad_scores, queries[g])
                dq_acc[g] += nn(kt_s[g, :, keys], grad_scores)

        cosine, sine = cos_ref[rows, :], sin_ref[rows, :]
        sums = jnp.zeros((1, width), F32)
        columns = []
        for head in range(heads):
            j = head % pairs
            grad = dq_acc[head // pairs, :, j * QUERIES : (j + 1) * QUERIES].T * root
            back, part_sum = head_back(grad, raw_s[head, rows, :].astype(F32), cosine, sine, query_gain)
            columns.append(back)
            sums = sums + part_sum
        query_sum[...] += sums
        sums = jnp.zeros((1, width), F32)
        for g in range(groups):
            back, part_sum = head_back(
                dk_s[g, rows, :] * root, raw_s[heads + g, rows, :].astype(F32), cosine, sine, key_gain
            )
            columns.append(back)
            sums = sums + part_sum
        key_sum[...] += sums
        for g in range(groups):
            columns.append(dv_s[g, rows, :].astype(BF16))
        everything = jnp.concatenate(columns, axis=1)
        all_s[rows, :] = everything

        @pl.when(turn_of == 0)
        def _():
            wait_all(weights)

        terms = nt(everything, w_s[...])
        first_sum[...] += jnp.sum(terms * unit_of(tok_s[rows, :].astype(F32))[0], axis=0, keepdims=True)
        terms_s[rows, :] = terms.astype(BF16)
        all_left[...] += tn(nn(everything, fa_ref[...]).astype(BF16), hid_s[rows, :])
        out_left[...] += tn(nn(low_grad, fo_ref[...]).astype(BF16), mixed)
        start_all(out_copies(block))

    @pl.loop(0, blocks)
    def _(block):
        wait_all(out_copies(block))


def backward(
    rep, meta, gain, head_gains, cosine, sine, doc_start, logs, tokens, cotangent, q_rot, k_rot, k_turned, v_heads, raw,
    mixed, hidden, fa, fo, mids, grads, pieces, out_pieces
):
    heads, total, width = q_rot.shape
    groups = k_rot.shape[0]
    depth = tokens.shape[1]
    cols = pieces[0][0].shape[1]
    parts = len(grads)
    blocks = total // QUERIES
    layout, arrays = layout_of(pieces)
    out_layout, out_arrays = layout_of(out_pieces)
    flat = [one for pair in mids + grads for one in pair]
    big = (tokens, cotangent, q_rot, k_rot, k_turned, v_heads, raw, mixed)
    rows = pltpu.VMEM((total, depth), BF16)
    return pl.pallas_call(
        functools.partial(backward_kernel, layout, out_layout, parts),
        in_specs=[SM, SM] + [VM] * 8 + [ANY] * (1 + len(big) + len(flat) + len(arrays) + len(out_arrays)),
        out_specs=[VM, VM, ANY, ANY, ANY] + [VM] * 5,
        out_shape=[
            sds((parts, PIECE, depth), F32),
            sds((parts, PIECE, depth), F32),
            sds((total, depth), BF16),
            sds((total, cols), BF16),
            sds((total, depth), BF16),
            sds((1, width), F32),
            sds((1, width), F32),
            sds((1, depth), F32),
            sds((fa.shape[1], depth), F32),
            sds((fo.shape[1], heads * width), F32),
        ],
        scratch_shapes=[rows, rows, rows, rows, pltpu.VMEM((depth, cols), BF16), pltpu.VMEM((heads * width, depth), BF16)]
        + [pltpu.VMEM(one.shape, BF16) for one in (q_rot, k_rot, k_turned, v_heads, raw, mixed, hidden)]
        + [
            rows,
            pltpu.VMEM((total, cols), BF16),
            rows,
            pltpu.VMEM((groups, total, width), F32),
            pltpu.VMEM((groups, total, width), F32),
            pltpu.VMEM((groups, width, heads // groups * QUERIES), F32),
            pltpu.SemaphoreType.DMA((4, total // PIECE)),
            pltpu.SemaphoreType.DMA((7,)),
            pltpu.SemaphoreType.DMA((slots(layout),)),
            pltpu.SemaphoreType.DMA((slots(out_layout),)),
            pltpu.SemaphoreType.DMA((3, blocks)),
        ],
        compiler_params=params(),
        cost_estimate=cost(20e9, 30e6),
        name="attention_backward",
    )(rep, meta, gain, head_gains, cosine, sine, doc_start, logs, fa, fo, *big, *flat, hidden, *arrays, *out_arrays)


def shares_kernel(count, *refs):
    errors, starts, out_ref = refs[:count], refs[count:-1], refs[-1]
    blocks = []
    for error in errors:
        blocks += [error[at] for at in range(error.shape[0])] if len(error.shape) == 3 else [error[...]]
    first = 0
    for block, start in zip(blocks, starts):
        high = start[...].astype(BF16)
        low = (start[...] - high.astype(F32)).astype(BF16)
        both = nt(jnp.concatenate([high, low], axis=0), block.astype(BF16))
        ranks, rows = start.shape[0], block.shape[0]
        out_ref[:, first : first + rows] = both[:ranks] + both[ranks:]
        first += rows


def shares_of(errors, starts, rows):
    return pl.pallas_call(
        functools.partial(shares_kernel, len(errors)),
        in_specs=[VM] * (len(errors) + len(starts)),
        out_specs=VM,
        out_shape=sds((starts[0].shape[0], rows), F32),
        compiler_params=params(),
        cost_estimate=cost(1e9, 16e6),
        name="error_shares",
    )(*errors, *starts)


def orthonormal_kernel(sizes, in_ref, out_ref):
    first = 0
    for size in sizes:
        panel = in_ref[:, first : first + size]
        ranks = panel.shape[0]
        index = lax.broadcasted_iota(jnp.int32, (ranks, 1), 0)
        for at in range(ranks):
            column = panel[at : at + 1, :]
            column = column * lax.rsqrt(jnp.sum(column * column, axis=1, keepdims=True) + EPSILON)
            dots = jnp.sum(panel * column, axis=1, keepdims=True)
            later = panel - dots * column
            panel = jnp.where(index > at, later, jnp.where(index == at, column, panel))
        out_ref[:, first : first + size] = panel
        first += size


def orthonormal(panels, sizes, label):
    return pl.pallas_call(
        functools.partial(orthonormal_kernel, sizes),
        out_shape=sds(panels.shape, F32),
        compiler_params=params(),
        cost_estimate=cost(1e6, 4e5),
        name=f"orthonormal_{label}",
    )(panels)


def split_low(value):
    high = rounded(value)
    return high.astype(BF16), (value - high).astype(BF16)


def right_terms(left_t, moment):
    high, low = split_low(left_t)
    ranks = left_t.shape[0]
    both = nn(jnp.concatenate([high, low], axis=0), moment.astype(BF16))
    return both[:ranks] + both[ranks:]


def outer(left_t, right_t):
    left_high, left_low = split_low(left_t)
    right_high, right_low = split_low(right_t)
    return tn(
        jnp.concatenate([left_high, left_low, left_high], axis=0),
        jnp.concatenate([right_high, right_high, right_low], axis=0),
    )


def cut_columns(value, widths):
    return jnp.split(value, [sum(widths[: i + 1]) for i in range(len(widths) - 1)], axis=1)


def all_rights(moments, lefts):
    return jnp.concatenate([right_terms(l, m) for l, m in zip(lefts, moments)], axis=1)


def settle(moment, left_t, right_t, weight, velocity, rep_index):
    rows = weight.shape[0]
    mine = outer(lax.dynamic_slice_in_dim(left_t, rep_index * rows, rows, 1), right_t)
    new_velocity = MOMENTUM * velocity + mine
    return weight - STEP_RATE * new_velocity, new_velocity, moment - outer(left_t, right_t)


def on_device(
    tokens,
    cotangent,
    lengths,
    block_gains,
    block_velocity,
    head_gains,
    head_velocity,
    weight_query,
    velocity_query,
    error_query,
    factor_query,
    weight_keyval,
    velocity_keyval,
    error_keyval,
    factor_keyval,
    weight_out,
    velocity_out,
    error_out,
    factor_out,
    weight_gateup,
    velocity_gateup,
    error_gateup,
    factor_gateup,
    weight_down,
    velocity_down,
    error_down,
    factor_down,
):
    total, depth = tokens.shape
    width = head_gains.shape[1]
    heads = weight_query.shape[1] // width
    groups = weight_keyval.shape[2] // width
    units = weight_gateup.shape[2]
    quarter = total // 4
    parts = quarter // PIECE
    blocks = total // PIECE
    replicas = lax.axis_size("rep")
    rep_index = lax.axis_index("rep")
    kv_index = lax.axis_index("kv")
    core = lax.rem(kv_index, 2)
    half = kv_index // 2
    rep = rep_index[None].astype(jnp.int32)
    core_at = core[None].astype(jnp.int32)

    pieces_qkv = gather_halves(
        jnp.concatenate([weight_query, weight_keyval[0], weight_keyval[1]], axis=1).astype(BF16)
    )
    pieces_out = gather_halves(weight_out.astype(BF16))
    packed = pack_feed(
        jnp.concatenate([weight_gateup[0], weight_gateup[1]], axis=1).astype(BF16), weight_down.astype(BF16)
    )
    packed = lax.all_gather(packed, "rep", axis=0)

    own_lengths = lengths[0]
    docs = own_lengths.shape[0]
    before = jnp.arange(docs)[:, None] >= jnp.arange(docs)[None, :]
    ends = jnp.sum(jnp.where(before, own_lengths[None, :], 0), axis=1)
    places = jnp.arange(total, dtype=jnp.int32)
    passed = places[None, :] >= ends[:, None]
    doc_start = jnp.sum(jnp.where(passed, own_lengths[:, None], 0), axis=0, keepdims=True).astype(jnp.int32)
    position = (places[None, :] - doc_start)[0]
    meta = []
    for rows in (QUERIES, PIECE):
        block_ends = (jnp.arange(total // rows, dtype=jnp.int32) + 1) * rows
        turns = (block_ends - doc_start[0, ::rows] + KEYS - 1) // KEYS
        meta += [jnp.maximum(block_ends - turns * KEYS, 0), turns]
    meta = jnp.concatenate(meta + [core[None], half[None]]).astype(jnp.int32)

    half_index = jnp.arange(width // 2, dtype=F32)
    frequency = ROPE_BASE ** (-2.0 * half_index / width)
    angles = position.astype(F32)[:, None] * frequency[None, :]
    cosine, sine = jnp.cos(angles), jnp.sin(angles)
    cosine = jnp.concatenate([cosine, cosine], axis=1)
    sine = jnp.concatenate([-sine, sine], axis=1)

    tokens_cut = tokens.reshape(2, 2, parts, PIECE, depth)
    cot_cut = cotangent.reshape(2, 2, parts, PIECE, depth)

    def chip_sum(mine, theirs):
        return (mine.astype(F32) + theirs.astype(F32)).astype(BF16)

    def cross_sum(own, *earlier):
        theirs = flip_kv(own, 2)
        summed = (after(own, *earlier).astype(F32) + theirs.astype(F32)).astype(BF16)
        return summed, flip_kv(summed, 1)

    factors = [factor_query, factor_keyval[0], factor_keyval[1], factor_gateup[0], factor_gateup[1]]
    factors = [one.T for one in factors] + [factor_out[0].T, factor_down[0].T]
    errors = [error_query[0], error_keyval[0, 0], error_keyval[0, 1], error_gateup[0, 0], error_gateup[0, 1]]
    errors += [error_out[0], error_down[0]]
    tied = (error_query[0], error_keyval[0], error_gateup[0], error_out[0], error_down[0])
    tied = lax.optimization_barrier((*tied, pieces_qkv[0][0], pieces_qkv[2 % len(pieces_qkv)][0]))[:5]
    counts = [one.shape[0] for one in errors]
    shares = shares_of(tied, factors, sum(counts))
    doc_start = after(doc_start, shares)
    shares = cut_columns(shares, counts)
    ranks = factor_query.shape[1]

    def laid(parts_of):
        rows = []
        for at, one in enumerate(parts_of):
            pads = (at * ranks, 128 - (at + 1) * ranks)
            rows.append(jnp.pad(one.T, ((0, 0), pads)))
        return jnp.concatenate(rows, axis=0).astype(BF16)

    laid_attn, laid_feed = laid(factors[:3]), laid(factors[3:5])
    laid_out, laid_down = laid(factors[5:6]), laid(factors[6:7])
    doc_start = after(doc_start, laid_attn, laid_feed, laid_out, laid_down)

    hidden_first, q_rot, raw, k_rot, k_turned, v_heads, mixed, logs = forward(
        rep, meta, tokens, block_gains[0:1], head_gains, cosine, sine, doc_start, pieces_qkv, heads, groups
    )
    mine, other = branch(rep, core_at, mixed, pieces_out, depth)
    theirs = flip_kv(other, 1)
    owns = [chip_sum(mine[p], theirs[p]) for p in range(parts)]

    mids, chain, terms_parts, second_parts, left_parts, term_owns = [], [], [], [], [], []
    earlier = ()
    for part in range(parts):
        mids.append(cross_sum(owns[part], *earlier))
        here = mids[part][0]
        if part >= 2:
            mine, theirs = terms_parts[part - 2]
            term_owns.append(chip_sum(mine, after(theirs, terms_parts[part - 1][0])))
            here = after(here, term_owns[-1])
        mine, other, second, gu_left, d_left, *chain = feed(
            part, parts, core_at, laid_feed, laid_down, here, mids[part][1], tokens_cut, cot_cut, block_gains[1:2],
            packed, units, chain,
        )
        earlier = (mine,)
        terms_parts.append((mine, flip_kv(other, 1)))
        second_parts.append(second)
        left_parts.append((gu_left, d_left))
    down_terms = chain[0].reshape(total, depth)

    last = terms_parts[parts - 1][0]
    gu_left = sum(one[0] for one in left_parts[1:]) + left_parts[0][0]
    d_left = sum(one[1] for one in left_parts[1:]) + left_parts[0][1]
    lefts = [gu_left[:ranks] + shares[3], gu_left[ranks : 2 * ranks] + shares[4], d_left[:ranks] + shares[6]]
    lefts = sum_rep_low(jnp.concatenate(lefts, axis=1))
    term_owns.append(chip_sum(terms_parts[1][0], after(terms_parts[1][1], last)))
    grads = [cross_sum(term_owns[0], last)]
    *chain, _, _ = lax.optimization_barrier((*chain[1:], term_owns[1], grads[0][0]))
    hid_full, act_full, dgu_full = [one.reshape(total, -1) for one in chain]
    gate_moment = tn(hid_full, dgu_full[:, :units]) + errors[3]
    term_owns.append(chip_sum(terms_parts[2][0], after(terms_parts[2][1], gate_moment)))
    hid_full, dgu_full, _ = lax.optimization_barrier((hid_full, dgu_full, term_owns[2]))
    up_moment = tn(hid_full, dgu_full[:, units:]) + errors[4]
    grads.append(cross_sum(term_owns[1], up_moment))
    down_moment = tn(after(act_full, grads[1][0]), cotangent) + errors[6]
    moments_feed = [gate_moment, up_moment, down_moment]
    lefts = orthonormal(after(lefts, down_moment), (depth, depth, units), "feed")
    lefts_feed = cut_columns(lefts, (depth, depth, units))
    grads.append(cross_sum(term_owns[2], lefts))
    rights_feed = all_rights(moments_feed, lefts_feed)
    there, rights_feed = lax.optimization_barrier((grads[2][1], rights_feed))
    grads[2] = (grads[2][0], there)
    feed_own = lax.psum_scatter(after(down_terms, there), "kv", scatter_dimension=0, tiled=True)

    own_grad, own_middle, gb_full, grads_qkv, input_terms, head_query, head_key, first_gain, all_left, out_left = backward(
        rep, meta, block_gains[1:2], head_gains, cosine, sine, doc_start, logs, tokens, cotangent, q_rot, k_rot,
        k_turned, v_heads, raw, mixed, hidden_first, laid_attn, laid_out, mids, grads, pieces_qkv, pieces_out,
    )

    second_gain = sum(second_parts[1:], second_parts[0])
    gains = jnp.concatenate([first_gain, second_gain, head_query, head_key], axis=1)
    for bit in (1, 2):
        gains = gains + flip_kv(gains, bit)
    gains = gains.reshape(8, -1)
    lefts = [all_left[at * ranks : (at + 1) * ranks] + shares[at] for at in range(3)] + [out_left[:ranks] + shares[5]]
    lefts = jnp.concatenate(lefts, axis=1)
    summed = sum_rep_low(jnp.concatenate([lefts, rights_feed, gains], axis=1))
    lefts, rights_feed, gains = cut_columns(summed, (lefts.shape[1], rights_feed.shape[1], gains.shape[1]))

    layer_out = (own_middle.reshape(quarter, depth) + feed_own.astype(F32)).astype(BF16)
    grad_first = lax.psum_scatter(input_terms, "kv", scatter_dimension=0, tiled=True).astype(F32)
    own_tokens = lax.dynamic_slice_in_dim(tokens, kv_index * quarter, quarter, 0).astype(F32)
    unit, scale = unit_of(own_tokens)
    input_grad = own_grad.reshape(quarter, depth) + norm_back(grad_first, unit, scale, block_gains[0])

    query_rows = heads * width
    group_cols = groups * width
    moments_attn = [
        tn(hidden_first, grads_qkv[:, :query_rows]) + errors[0],
        tn(hidden_first, grads_qkv[:, query_rows : query_rows + group_cols]) + errors[1],
        tn(hidden_first, grads_qkv[:, query_rows + group_cols :]) + errors[2],
        tn(mixed, gb_full) + errors[5],
    ]
    rights_feed = cut_columns(rights_feed / replicas, (units, units, depth))
    sizes = (depth, depth, depth, query_rows)
    lefts_attn = cut_columns(orthonormal(lefts, sizes, "attn"), sizes)
    rights = sum_rep_low(all_rights(moments_attn, lefts_attn)) / replicas
    rights_attn = cut_columns(rights, (query_rows, group_cols, group_cols, depth))
    gains = gains.reshape(1, -1) / replicas
    block_mean = gains[0, : 2 * depth].reshape(2, depth)
    head_mean = gains[0, 2 * depth :].reshape(2, width)
    new_block_velocity = MOMENTUM * block_velocity + block_mean
    new_head_velocity = MOMENTUM * head_velocity + head_mean


    def settled(moments, lefts, rights, weights, velocities):
        return [
            settle(m, l, r, w, v, rep_index)
            for m, l, r, w, v in zip(moments, lefts, rights, weights, velocities)
        ]

    gate_new, up_new, down_new = settled(
        moments_feed,
        lefts_feed,
        rights_feed,
        [weight_gateup[0], weight_gateup[1], weight_down],
        [velocity_gateup[0], velocity_gateup[1], velocity_down],
    )
    query_new, key_new, value_new, out_new = settled(
        moments_attn,
        lefts_attn,
        rights_attn,
        [weight_query, weight_keyval[0], weight_keyval[1], weight_out],
        [velocity_query, velocity_keyval[0], velocity_keyval[1], velocity_out],
    )

    def pair(first, second):
        return [jnp.stack([one, two]) for one, two in zip(first, second)]

    keyval_new = pair(key_new, value_new)
    gateup_new = pair(gate_new, up_new)
    return (
        layer_out,
        input_grad,
        block_gains - GAIN_RATE * new_block_velocity,
        new_block_velocity,
        head_gains - GAIN_RATE * new_head_velocity,
        new_head_velocity,
        query_new[0],
        query_new[1],
        query_new[2][None],
        lefts_attn[0].T[None],
        rights_attn[0].T,
        keyval_new[0],
        keyval_new[1],
        keyval_new[2][None],
        jnp.stack([lefts_attn[1].T, lefts_attn[2].T])[:, None],
        jnp.stack([rights_attn[1].T, rights_attn[2].T]),
        out_new[0],
        out_new[1],
        out_new[2][None],
        lefts_attn[3].T,
        rights_attn[3].T[None],
        gateup_new[0],
        gateup_new[1],
        gateup_new[2][None],
        jnp.stack([lefts_feed[0].T, lefts_feed[1].T])[:, None],
        jnp.stack([rights_feed[0].T, rights_feed[1].T]),
        down_new[0],
        down_new[1],
        down_new[2][None],
        lefts_feed[2].T,
        rights_feed[2].T[None],
    )


def solution(mesh):
    placed = (
        P("rep", None),
        P("rep", None),
        P("rep", None),
        P(),
        P(),
        P(),
        P(),
        P("rep", "kv"),
        P("rep", "kv"),
        P("rep", None, "kv"),
        P("kv", None),
        P(None, "rep", "kv"),
        P(None, "rep", "kv"),
        P("rep", None, None, "kv"),
        P(None, "kv", None),
        P(("kv", "rep"), None),
        P(("kv", "rep"), None),
        P("rep", "kv", None),
        P("kv", None, None),
        P(None, "rep", "kv"),
        P(None, "rep", "kv"),
        P("rep", None, None, "kv"),
        P(None, "kv", None),
        P(("kv", "rep"), None),
        P(("kv", "rep"), None),
        P("rep", "kv", None),
        P("kv", None, None),
    )
    return jax.shard_map(
        on_device,
        mesh=mesh,
        in_specs=placed,
        out_specs=(
            P(("rep", "kv"), None),
            P(("rep", "kv"), None),
            P(),
            P(),
            P(),
            P(),
            P("rep", "kv"),
            P("rep", "kv"),
            P("rep", None, "kv"),
            P("kv", None, None),
            P("kv", None),
            P(None, "rep", "kv"),
            P(None, "rep", "kv"),
            P("rep", None, None, "kv"),
            P(None, "kv", None, None),
            P(None, "kv", None),
            P(("kv", "rep"), None),
            P(("kv", "rep"), None),
            P("rep", "kv", None),
            P("kv", None),
            P("kv", None, None),
            P(None, "rep", "kv"),
            P(None, "rep", "kv"),
            P("rep", None, None, "kv"),
            P(None, "kv", None, None),
            P(None, "kv", None),
            P(("kv", "rep"), None),
            P(("kv", "rep"), None),
            P("rep", "kv", None),
            P("kv", None),
            P("kv", None, None),
        ),
        check_vma=False,
    )
```

```python
import functools
import math

import jax
import jax.numpy as jnp
from jax import lax
from jax.experimental import pallas as pl
from jax.experimental.pallas import tpu as pltpu
from jax.sharding import PartitionSpec as P

EPSILON = 1e-06
ROPE_BASE = 1000000.0
MOMENTUM = 0.9
STEP_RATE = 0.04
GAIN_RATE = 0.005
PIECE = 128
QUERIES = 256
KEYS = 512
F32 = jnp.float32
BF16 = jnp.bfloat16
VMEM_LIMIT = 56 * 1024 * 1024


def nn(left, right):
    return lax.dot_general(left, right, (((1,), (0,)), ((), ())), preferred_element_type=F32)


def nt(left, right):
    return lax.dot_general(left, right, (((1,), (1,)), ((), ())), preferred_element_type=F32)


def tn(left, right):
    return lax.dot_general(left, right, (((0,), (0,)), ((), ())), preferred_element_type=F32)


def params(limit=VMEM_LIMIT):
    return pltpu.CompilerParams(vmem_limit_bytes=limit)


def cost(flops, moved, exps=0):
    return pl.CostEstimate(flops=int(flops / 8), bytes_accessed=int(moved / 8), transcendentals=0)


def sds(shape, dtype):
    return jax.ShapeDtypeStruct(shape, dtype)


VM = pl.BlockSpec(memory_space=pltpu.VMEM)
SM = pl.BlockSpec(memory_space=pltpu.SMEM)
ANY = pl.BlockSpec(memory_space=pl.ANY)


def flip_kv(value, bit):
    size = lax.axis_size("kv")
    return lax.ppermute(value, "kv", [(i, i ^ bit) for i in range(size)])


def flip_rep(value, bit):
    size = lax.axis_size("rep")
    return lax.ppermute(value, "rep", [(i, i ^ bit) for i in range(size)])


def after(value, *earlier):
    return lax.optimization_barrier((value, *earlier))[0]


def rounded(value):
    return lax.reduce_precision(value, exponent_bits=8, mantissa_bits=7)


def rep_bits():
    return [1 << i for i in range(lax.axis_size("rep").bit_length() - 1)]


def begin_sum(value, bit):
    held = rounded(value.astype(F32))
    return held, flip_rep(held.astype(BF16), bit)


def end_sum(pair, *earlier):
    return after(pair[0], *earlier) + pair[1].astype(F32)


def xor_codes(bits):
    codes = (0,)
    for bit in bits:
        codes = codes + tuple(code ^ bit for code in codes)
    return codes


def spread(value, bits):
    for bit in bits[:-1]:
        value = jnp.concatenate([value, flip_rep(value, bit)], axis=0)
    codes = xor_codes(bits)
    middle = len(codes) // 2
    return [(value, codes[:middle]), (flip_rep(value, bits[-1]), codes[middle:])]


def gather_halves(chunk):
    replicas = lax.axis_size("rep")
    falling = [1 << i for i in range(replicas.bit_length() - 2, -1, -1)]
    rows = chunk.shape[0]
    if rows % 32 != 0:
        return [part + (0,) for part in spread(chunk, falling)]
    rising = falling[-1:] + falling[:-1]
    first = [part + (0,) for part in spread(chunk[: rows // 2], falling)]
    return first + [part + (rows // 2,) for part in spread(chunk[rows // 2 :], rising)]


def piece_copies(rep, layout, refs, target, sems):
    share = target.shape[0] // sum(len(codes) for codes, offset in layout if offset == 0)
    copies = []
    for (codes, offset), ref in zip(layout, refs):
        rows = ref.shape[0] // len(codes)
        for at, code in enumerate(codes):
            first = pl.multiple_of(lax.bitwise_xor(rep, code) * share + offset, 8)
            copies.append(
                pltpu.make_async_copy(
                    ref.at[pl.ds(at * rows, rows), :], target.at[pl.ds(first, rows), :], sems.at[len(copies)]
                )
            )
    return copies


def pack_feed(gateup, down):
    depth = down.shape[1]
    rows = gateup.shape[0]
    rest = gateup[:, depth:]
    rest = jnp.concatenate([rest[: rows // 2], rest[rows // 2 :]], axis=1)
    return jnp.concatenate([gateup[:, :depth], rest, down], axis=0)


def feed_copies(packed, gateup, down, sems):
    replicas = packed.shape[0]
    depth = down.shape[1]
    rows, low_rows = gateup.shape[0] // replicas, down.shape[0] // replicas
    half = rows // 2
    rest = gateup.shape[1] - depth
    first, second = [], []
    for at in range(replicas):
        top = at * rows
        pairs = [
            (packed.at[at, 0:rows, :], gateup.at[top : top + rows, 0:depth]),
            (packed.at[at, rows : rows + half, 0:rest], gateup.at[top : top + half, depth : depth + rest]),
            (packed.at[at, rows : rows + half, rest : 2 * rest], gateup.at[top + half : top + rows, depth : depth + rest]),
        ]
        first += [pltpu.make_async_copy(x, y, sems.at[at * 4 + i]) for i, (x, y) in enumerate(pairs)]
        second.append(
            pltpu.make_async_copy(
                packed.at[at, rows + half : rows + half + low_rows, :],
                down.at[at * low_rows : (at + 1) * low_rows, :],
                sems.at[at * 4 + 3],
            )
        )
    return first, second


def start_all(copies):
    for copy in copies:
        copy.start()


def wait_all(copies):
    for copy in copies:
        copy.wait()


def unit_of(values):
    scale = lax.rsqrt(jnp.mean(values * values, axis=-1, keepdims=True) + EPSILON)
    return values * scale, scale


def norm_back(grad, unit, scale, gain):
    weighted = grad * gain
    return scale * (weighted - unit * jnp.mean(weighted * unit, axis=-1, keepdims=True))


def forward_kernel(layout, rep, meta, tok_ref, gain_ref, head_ref, cos_ref, sin_ref, start_ref, *refs):
    pieces = refs[: len(layout)]
    hid_out, q_out, raw_out, k_out, kt_out, v_out, mixed_out, log_ref = refs[len(layout) : len(layout) + 8]
    (tok_s, w_s, hid_s, q_s, raw_s, k_s, kt_s, v_s, vt_s, mixed_s, out_acc, sum_acc) = refs[len(layout) + 8 : -3]
    in_sems, w_sems, out_sems = refs[-3:]
    heads, total, width = q_s.shape
    groups = k_s.shape[0]
    pairs = heads // groups
    blocks = total // QUERIES
    factor = math.log2(math.e) / math.sqrt(width)

    def token_copy(block):
        here = pl.ds(pl.multiple_of(block * QUERIES, QUERIES), QUERIES)
        return pltpu.make_async_copy(tok_ref.at[here, :], tok_s.at[here, :], in_sems.at[block])

    def sent(block):
        here = pl.ds(pl.multiple_of(block * QUERIES, QUERIES), QUERIES)
        pairs_of = [
            (hid_s.at[here, :], hid_out.at[here, :]),
            (q_s.at[:, here, :], q_out.at[:, here, :]),
            (raw_s.at[:, here, :], raw_out.at[:, here, :]),
            (k_s.at[:, here, :], k_out.at[:, here, :]),
            (kt_s.at[:, :, here], kt_out.at[:, :, here]),
            (v_s.at[:, here, :], v_out.at[:, here, :]),
            (mixed_s.at[here, :], mixed_out.at[here, :]),
        ]
        return [pltpu.make_async_copy(x, y, out_sems.at[i, block]) for i, (x, y) in enumerate(pairs_of)]

    weights = piece_copies(rep[0], layout, pieces, w_s, w_sems)
    token_copy(0).start()
    start_all(weights)
    for block in range(1, blocks):
        token_copy(block).start()
    log_ref[...] = jnp.zeros_like(log_ref)
    vt_s[...] = jnp.zeros_like(vt_s)
    wait_all(weights)

    @pl.loop(0, blocks)
    def _(block):
        low, count = meta[block], meta[blocks + block]
        here = pl.ds(pl.multiple_of(block * QUERIES, QUERIES), QUERIES)
        token_copy(block).wait()
        unit, _ = unit_of(tok_s[here, :].astype(F32))
        hidden = (unit * gain_ref[...]).astype(BF16)
        hid_s[here, :] = hidden
        projected = nn(hidden, w_s[...])
        cosine, sine = cos_ref[here, :], sin_ref[here, :]
        means = jnp.full((width, width), 1.0 / width, BF16)
        for index in range(heads + groups):
            one = projected[:, index * width : (index + 1) * width]
            raw_s[index, here, :] = one.astype(BF16)
            gain = head_ref[0:1, :] if index < heads else head_ref[1:2, :]
            normed = one * lax.rsqrt(nn((one * one).astype(BF16), means) + EPSILON) * gain
            turned = normed * cosine + pltpu.roll(normed, width // 2, 1) * sine
            if index < heads:
                q_s[index, here, :] = turned.astype(BF16)
            else:
                k_s[index - heads, here, :] = turned.astype(BF16)
                kt_s[index - heads, :, here] = turned.T.astype(BF16)
        for index in range(groups):
            first = (heads + groups + index) * width
            one = projected[:, first : first + width]
            v_s[index, here, :] = one.astype(BF16)
            vt_s[index, :, here] = one.T.astype(BF16)

        start = jnp.concatenate([start_ref[:, here]] * pairs, axis=1)
        place = block * QUERIES + lax.broadcasted_iota(jnp.int32, (1, QUERIES), 1)
        place = jnp.concatenate([place] * pairs, axis=1)
        queries = [
            jnp.concatenate([q_s[g * pairs + j, here, :] for j in range(pairs)], axis=0) for g in range(groups)
        ]
        out_acc[...] = jnp.zeros_like(out_acc)
        sum_acc[...] = jnp.zeros_like(sum_acc)

        @pl.loop(0, count)
        def _(turn):
            base = pl.multiple_of(low + turn * KEYS, PIECE)
            key_place = base + lax.broadcasted_iota(jnp.int32, (KEYS, 1), 0)
            allowed = (key_place >= start) & (key_place <= place)
            for g in range(groups):
                scores = nt(k_s[g, pl.ds(base, KEYS), :], queries[g])
                weights = jnp.where(allowed, jnp.exp2(scores * factor), 0.0)
                sum_acc[g] += jnp.sum(weights, axis=0, keepdims=True)
                out_acc[g] += nn(vt_s[g, :, pl.ds(base, KEYS)], weights.astype(BF16))

        for g in range(groups):
            total_weight = sum_acc[g]
            mixed = out_acc[g] / total_weight
            logs = jnp.log2(total_weight)
            for j in range(pairs):
                head = g * pairs + j
                mixed_s[here, head * width : (head + 1) * width] = mixed[:, j * QUERIES : (j + 1) * QUERIES].T.astype(BF16)
                log_ref[head : head + 1, here] = logs[:, j * QUERIES : (j + 1) * QUERIES]
        start_all(sent(block))

    @pl.loop(0, blocks)
    def _(block):
        wait_all(sent(block))


def layout_of(pieces):
    return tuple((codes, offset) for _, codes, offset in pieces), [piece for piece, _, _ in pieces]


def slots(layout):
    return sum(len(codes) for codes, _ in layout)


def forward(rep, meta, tokens, gain, head_gains, cosine, sine, doc_start, pieces, heads, groups):
    total, depth = tokens.shape
    width = head_gains.shape[1]
    cols = pieces[0][0].shape[1]
    layout, arrays = layout_of(pieces)
    wide = heads // groups * QUERIES
    blocks = total // QUERIES
    outs = [
        (total, depth),
        (heads, total, width),
        (heads + groups, total, width),
        (groups, total, width),
        (groups, width, total),
        (groups, total, width),
        (total, heads * width),
    ]
    return pl.pallas_call(
        functools.partial(forward_kernel, layout),
        in_specs=[SM, SM, ANY] + [VM] * 5 + [ANY] * len(arrays),
        out_specs=[ANY] * 7 + [VM],
        out_shape=[sds(shape, BF16) for shape in outs] + [sds((8, total), F32)],
        scratch_shapes=[pltpu.VMEM((total, depth), BF16), pltpu.VMEM((depth, cols), BF16)]
        + [pltpu.VMEM(shape, BF16) for shape in outs[:6]]
        + [
            pltpu.VMEM((groups, width, total), BF16),
            pltpu.VMEM((total, heads * width), BF16),
            pltpu.VMEM((groups, width, wide), F32),
            pltpu.VMEM((groups, 1, wide), F32),
            pltpu.SemaphoreType.DMA((blocks,)),
            pltpu.SemaphoreType.DMA((slots(layout),)),
            pltpu.SemaphoreType.DMA((7, blocks)),
        ],
        compiler_params=params(),
        cost_estimate=cost(12e9, 20e6),
        name="attention_forward",
    )(rep, meta, tokens, gain, head_gains, cosine, sine, doc_start, *arrays)


def branch_kernel(layout, rep, core, mixed_ref, *refs):
    pieces = refs[: len(layout)]
    mine_out, other_out, w_s, mixed_s, out_s, sems, w_sems, out_sems = refs[len(layout) :]
    quarter = mixed_s.shape[1]
    loads = [
        pltpu.make_async_copy(mixed_ref.at[pl.ds(at * quarter, quarter), :], mixed_s.at[at], sems.at[at]) for at in range(4)
    ]
    weights = piece_copies(rep[0], layout, pieces, w_s, w_sems)
    start_all(weights + loads)
    wait_all(weights)
    lasts = []
    for step in range(4):
        spot = step % 2
        side = 1 - step // 2
        at = 2 * spot + lax.rem(core[0] + side, 2)
        if step == 0:
            wait_all(loads)
        out_s[step] = nn(mixed_s[at], w_s[...]).astype(BF16).reshape(out_s.shape[1:])
        lasts.append(
            pltpu.make_async_copy(out_s.at[step], (mine_out, other_out)[side].at[:, spot], out_sems.at[step])
        )
        lasts[-1].start()
    wait_all(lasts)


def branch(rep, core, mixed, pieces, depth):
    total, cols = mixed.shape
    layout, arrays = layout_of(pieces)
    parts = total // 4 // PIECE
    return pl.pallas_call(
        functools.partial(branch_kernel, layout),
        in_specs=[SM, SM] + [ANY] * (1 + len(arrays)),
        out_specs=[ANY, ANY],
        out_shape=[sds((parts, 2, PIECE, depth), BF16)] * 2,
        scratch_shapes=[
            pltpu.VMEM((cols, depth), BF16),
            pltpu.VMEM((4, total // 4, cols), BF16),
            pltpu.VMEM((4, parts, PIECE, depth), BF16),
            pltpu.SemaphoreType.DMA((4,)),
            pltpu.SemaphoreType.DMA((slots(layout),)),
            pltpu.SemaphoreType.DMA((4,)),
        ],
        compiler_params=params(),
        cost_estimate=cost(2 * total * cols * depth, 6e6),
        name="branch",
    )(rep, core, mixed, *arrays)


def feed_kernel(part, core, gain_ref, fgu_ref, fd_ref, here_ref, there_ref, tok_ref, cot_ref, packed_ref, *refs):
    mine_out, other_out, sum_ref, gu_left, d_left, down_out, hid_out, act_out, dgu_out = refs[-20:-11]
    mid_s, tok_s, cot_s, wgu_s, wd_s, terms_s, down_s, hid_s, act_s, dgu_s, sems = refs[-11:]
    units = wd_s.shape[0]
    spots = [(side, spot) for side in (1, 0) for spot in range(2)]
    spare = 4 * packed_ref.shape[0]

    def natural(ref, side, spot):
        return ref.at[spot, lax.rem(core[0] + side, 2), part]

    def rows(index):
        return pl.ds(index * PIECE, PIECE)

    first, cots, lasts = [], [], []
    for index, (side, spot) in enumerate(spots):
        at = spare + 8 * index
        source = (here_ref, there_ref)[side].at[spot]
        first.append(pltpu.make_async_copy(source, mid_s.at[rows(index), :], sems.at[at]))
        first.append(pltpu.make_async_copy(natural(tok_ref, side, spot), tok_s.at[rows(index), :], sems.at[at + 1]))
        cots.append(pltpu.make_async_copy(natural(cot_ref, side, spot), cot_s.at[rows(index), :], sems.at[at + 2]))
    gateups, downs = feed_copies(packed_ref, wgu_s, wd_s, sems)
    start_all(first + gateups + cots + downs)

    def send(scratch, target_of, kind):
        for index, (side, spot) in enumerate(spots):
            lasts.append(
                pltpu.make_async_copy(
                    scratch.at[rows(index), :], target_of(side, spot), sems.at[spare + 8 * index + 3 + kind]
                )
            )
            lasts[-1].start()

    wait_all(first)
    unit, _ = unit_of(tok_s[...].astype(F32) + mid_s[...].astype(F32))
    hid_s[...] = (unit * gain_ref[...]).astype(BF16)
    send(hid_s, lambda side, spot: natural(hid_out, side, spot), 0)
    wait_all(gateups)
    both = nn(hid_s[...], wgu_s[...])
    wait_all(cots + downs)
    grad_active = nt(cot_s[...], wd_s[...])
    gate, up = both[:, :units], both[:, units:]
    sig = jax.nn.sigmoid(gate)
    lit = gate * sig
    act_s[...] = (lit * up).astype(BF16)
    send(act_s, lambda side, spot: natural(act_out, side, spot), 1)
    dgu_s[:, :units] = (grad_active * up * sig * (1.0 + gate * (1.0 - sig))).astype(BF16)
    dgu_s[:, units:] = (grad_active * lit).astype(BF16)
    send(dgu_s, lambda side, spot: natural(dgu_out, side, spot), 2)
    terms = nt(dgu_s[...], wgu_s[...])
    terms_s[...] = terms.astype(BF16)
    send(terms_s, lambda side, spot: (mine_out, other_out)[side].at[spot], 3)
    down_s[...] = nn(act_s[...], wd_s[...]).astype(BF16)
    send(down_s, lambda side, spot: natural(down_out, side, spot), 4)
    sum_ref[...] = jnp.sum(terms * unit, axis=0, keepdims=True)
    gu_left[...] = tn(nn(dgu_s[...], fgu_ref[...]).astype(BF16), hid_s[...])
    d_left[...] = tn(nn(cot_s[...], fd_ref[...]).astype(BF16), act_s[...])
    wait_all(lasts)


def feed(part, parts, core, fgu, fd, here, there, tokens_cut, cot_cut, gain, packed, units, chain):
    depth = gain.shape[1]
    saved = (
        (2, 2, parts, PIECE, depth),
        (2, 2, parts, PIECE, depth),
        (2, 2, parts, PIECE, units),
        (2, 2, parts, PIECE, 2 * units),
    )
    rows = 4 * PIECE
    return pl.pallas_call(
        functools.partial(feed_kernel, part),
        in_specs=[SM, VM, VM, VM] + [ANY] * (5 + len(chain)),
        out_specs=[ANY, ANY, VM, VM, VM] + [ANY] * 4,
        out_shape=[sds((2, PIECE, depth), BF16)] * 2
        + [sds((1, depth), F32), sds((fgu.shape[1], depth), F32), sds((fd.shape[1], units), F32)]
        + [sds(shape, BF16) for shape in saved],
        scratch_shapes=[
            pltpu.VMEM((rows, depth), BF16),
            pltpu.VMEM((rows, depth), BF16),
            pltpu.VMEM((rows, depth), BF16),
            pltpu.VMEM((depth, 2 * units), BF16),
            pltpu.VMEM((units, depth), BF16),
            pltpu.VMEM((rows, depth), BF16),
            pltpu.VMEM((rows, depth), BF16),
            pltpu.VMEM((rows, depth), BF16),
            pltpu.VMEM((rows, units), BF16),
            pltpu.VMEM((rows, 2 * units), BF16),
            pltpu.SemaphoreType.DMA((4 * packed.shape[0] + 32,)),
        ],
        input_output_aliases={9 + i: 5 + i for i in range(len(chain))},
        compiler_params=params(),
        cost_estimate=cost(2 * 4 * PIECE * depth * units * 6, 12e6),
        name=f"feed_{part}",
    )(core, gain, fgu, fd, here, there, tokens_cut, cot_cut, packed, *chain)


def backward_kernel(layout, out_layout, parts, rep, meta, mid_gain, head_ref, cos_ref, sin_ref, start_ref, log_ref, fa_ref, fo_ref, *refs):
    (tok_ref, cot_ref, q_hbm, k_hbm, kt_hbm, v_hbm, raw_hbm, mixed_hbm) = refs[:8]
    mid_parts, grad_parts = refs[8 : 8 + 2 * parts], refs[8 + 2 * parts : 8 + 4 * parts]
    hid_hbm = refs[8 + 4 * parts]
    refs = refs[9 + 4 * parts :]
    pieces, out_pieces = refs[: len(layout)], refs[len(layout) : len(layout) + len(out_layout)]
    rest = refs[len(layout) + len(out_layout) :]
    (own_ref, own_mid, gb_out, grads_out, terms_out, query_sum, key_sum, first_sum, all_left, out_left) = rest[:10]
    (mid_s, grad_s, tok_s, cot_s, w_s, wo_s, q_s, k_s, kt_s, v_s, raw_s, mixed_s, hid_s, gb_s, all_s, terms_s, dk_s, dv_s, dq_acc) = rest[10:-5]
    row_sems, big_sems, w_sems, wo_sems, out_sems = rest[-5:]
    heads, total, width = q_s.shape
    groups = k_s.shape[0]
    pairs = heads // groups
    blocks, cuts = total // QUERIES, total // PIECE
    per = QUERIES // PIECE
    core, half = meta[2 * blocks + 2 * cuts], meta[2 * blocks + 2 * cuts + 1]
    root = 1.0 / math.sqrt(width)
    factor = math.log2(math.e) * root

    def row_copies(cut):
        quarter, part = cut // parts, cut % parts
        spot = quarter // 2
        here = pl.ds(cut * PIECE, PIECE)
        near = lax.rem(core + quarter, 2) == 0

        @pl.when(near)
        def _():
            pltpu.make_async_copy(mid_parts[2 * part].at[spot], mid_s.at[here, :], row_sems.at[0, cut]).start()
            pltpu.make_async_copy(grad_parts[2 * part].at[spot], grad_s.at[here, :], row_sems.at[1, cut]).start()

        @pl.when(jnp.logical_not(near))
        def _():
            pltpu.make_async_copy(mid_parts[2 * part + 1].at[spot], mid_s.at[here, :], row_sems.at[0, cut]).start()
            pltpu.make_async_copy(grad_parts[2 * part + 1].at[spot], grad_s.at[here, :], row_sems.at[1, cut]).start()

        pltpu.make_async_copy(tok_ref.at[here, :], tok_s.at[here, :], row_sems.at[2, cut]).start()
        pltpu.make_async_copy(cot_ref.at[here, :], cot_s.at[here, :], row_sems.at[3, cut]).start()

    big = [
        pltpu.make_async_copy(x, y, big_sems.at[i])
        for i, (x, y) in enumerate(
            [
                (k_hbm, k_s), (v_hbm, v_s), (q_hbm, q_s), (kt_hbm, kt_s), (mixed_hbm, mixed_s),
                (raw_hbm, raw_s), (hid_hbm, hid_s),
            ]
        )
    ]
    weights = piece_copies(rep[0], layout, pieces, w_s, w_sems)
    out_weights = piece_copies(rep[0], out_layout, out_pieces, wo_s, wo_sems)
    for cut in range(cuts - 1, cuts - 1 - per, -1):
        row_copies(cut)
    start_all(out_weights + big + weights)
    for cut in range(cuts - 1 - per, -1, -1):
        row_copies(cut)
    dk_s[...] = jnp.zeros_like(dk_s)
    dv_s[...] = jnp.zeros_like(dv_s)
    query_sum[...] = jnp.zeros_like(query_sum)
    key_sum[...] = jnp.zeros_like(key_sum)
    first_sum[...] = jnp.zeros_like(first_sum)
    all_left[...] = jnp.zeros_like(all_left)
    out_left[...] = jnp.zeros_like(out_left)
    ones = jnp.ones((8, width), F32)
    query_gain, key_gain = head_ref[0:1, :], head_ref[1:2, :]
    means = jnp.full((width, width), 1.0 / width, BF16)

    def mean_of(values):
        return nn(values.astype(BF16), means)

    def head_back(grad, raw, cosine, sine, gain):
        turned = grad * cosine - pltpu.roll(grad, width // 2, 1) * sine
        scale = lax.rsqrt(mean_of(raw * raw) + EPSILON)
        unit = raw * scale
        weighted = turned * gain
        back = scale * (weighted - unit * mean_of(weighted * unit))
        return back.astype(BF16), jnp.sum(turned * unit, axis=0, keepdims=True)

    def out_copies(block):
        here = pl.ds(pl.multiple_of(block * QUERIES, QUERIES), QUERIES)
        pairs_of = [(gb_s, gb_out), (all_s, grads_out), (terms_s, terms_out)]
        return [
            pltpu.make_async_copy(x.at[here, :], y.at[here, :], out_sems.at[i, block]) for i, (x, y) in enumerate(pairs_of)
        ]

    @pl.loop(0, blocks)
    def _(turn_of):
        block = blocks - 1 - turn_of
        low, count = meta[block], meta[blocks + block]
        rows = pl.ds(pl.multiple_of(block * QUERIES, QUERIES), QUERIES)
        for at in range(per):
            cut = block * per + at
            here = pl.ds(pl.multiple_of(cut * PIECE, PIECE), PIECE)
            for kind, target in enumerate((mid_s, grad_s, tok_s, cot_s)):
                pltpu.make_async_copy(tok_ref.at[here, :], target.at[here, :], row_sems.at[kind, cut]).wait()
        middle = tok_s[rows, :].astype(F32) + mid_s[rows, :].astype(F32)
        unit, scale = unit_of(middle)
        result = cot_s[rows, :].astype(F32) + norm_back(grad_s[rows, :].astype(F32), unit, scale, mid_gain[...])
        low_grad = result.astype(BF16)
        gb_s[rows, :] = low_grad
        for at in range(per):
            cut = block * per + at

            @pl.when(cut // parts == 2 * half + core)
            def _():
                own_ref[lax.rem(cut, parts)] = result[at * PIECE : (at + 1) * PIECE]
                own_mid[lax.rem(cut, parts)] = middle[at * PIECE : (at + 1) * PIECE]

        @pl.when(turn_of == 0)
        def _():
            wait_all(out_weights + big)

        grad_mixed = nt(low_grad, wo_s[...]).astype(BF16)
        mixed = mixed_s[rows, :]
        start = jnp.concatenate([start_ref[:, rows]] * pairs, axis=1)
        place = block * QUERIES + lax.broadcasted_iota(jnp.int32, (1, QUERIES), 1)
        place = jnp.concatenate([place] * pairs, axis=1)
        queries, grads, logs, deltas = [], [], [], []
        for g in range(groups):
            members = range(g * pairs, (g + 1) * pairs)
            queries.append(jnp.concatenate([q_s[h, rows, :] for h in members], axis=0))
            grad = jnp.concatenate([grad_mixed[:, h * width : (h + 1) * width] for h in members], axis=0)
            out = jnp.concatenate([mixed[:, h * width : (h + 1) * width] for h in members], axis=0)
            grads.append(grad)
            logs.append(jnp.concatenate([log_ref[h : h + 1, rows] for h in members], axis=1))
            terms = lax.dot_general(
                ones,
                grad.astype(F32) * out.astype(F32),
                (((1,), (1,)), ((), ())),
                precision=lax.Precision.HIGHEST,
                preferred_element_type=F32,
            )
            deltas.append(terms[0:1, :])
        dq_acc[...] = jnp.zeros_like(dq_acc)

        @pl.loop(0, count)
        def _(turn):
            base = pl.multiple_of(low + turn * KEYS, PIECE)
            key_place = base + lax.broadcasted_iota(jnp.int32, (KEYS, 1), 0)
            allowed = (key_place >= start) & (key_place <= place)
            keys = pl.ds(base, KEYS)
            for g in range(groups):
                scores = nt(k_s[g, keys, :], queries[g])
                weights = jnp.where(allowed, jnp.exp2(scores * factor - logs[g]), 0.0)
                grad_weights = nt(v_s[g, keys, :], grads[g])
                grad_scores = (weights * (grad_weights - deltas[g])).astype(BF16)
                dv_s[g, keys, :] += nn(weights.astype(BF16), grads[g])
                dk_s[g, keys, :] += nn(grad_scores, queries[g])
                dq_acc[g] += nn(kt_s[g, :, keys], grad_scores)

        cosine, sine = cos_ref[rows, :], sin_ref[rows, :]
        sums = jnp.zeros((1, width), F32)
        columns = []
        for head in range(heads):
            j = head % pairs
            grad = dq_acc[head // pairs, :, j * QUERIES : (j + 1) * QUERIES].T * root
            back, part_sum = head_back(grad, raw_s[head, rows, :].astype(F32), cosine, sine, query_gain)
            columns.append(back)
            sums = sums + part_sum
        query_sum[...] += sums
        sums = jnp.zeros((1, width), F32)
        for g in range(groups):
            back, part_sum = head_back(
                dk_s[g, rows, :] * root, raw_s[heads + g, rows, :].astype(F32), cosine, sine, key_gain
            )
            columns.append(back)
            sums = sums + part_sum
        key_sum[...] += sums
        for g in range(groups):
            columns.append(dv_s[g, rows, :].astype(BF16))
        everything = jnp.concatenate(columns, axis=1)
        all_s[rows, :] = everything

        @pl.when(turn_of == 0)
        def _():
            wait_all(weights)

        terms = nt(everything, w_s[...])
        first_sum[...] += jnp.sum(terms * unit_of(tok_s[rows, :].astype(F32))[0], axis=0, keepdims=True)
        terms_s[rows, :] = terms.astype(BF16)
        all_left[...] += tn(nn(everything, fa_ref[...]).astype(BF16), hid_s[rows, :])
        out_left[...] += tn(nn(low_grad, fo_ref[...]).astype(BF16), mixed)
        start_all(out_copies(block))

    @pl.loop(0, blocks)
    def _(block):
        wait_all(out_copies(block))


def backward(
    rep, meta, gain, head_gains, cosine, sine, doc_start, logs, tokens, cotangent, q_rot, k_rot, k_turned, v_heads, raw,
    mixed, hidden, fa, fo, mids, grads, pieces, out_pieces
):
    heads, total, width = q_rot.shape
    groups = k_rot.shape[0]
    depth = tokens.shape[1]
    cols = pieces[0][0].shape[1]
    parts = len(grads)
    blocks = total // QUERIES
    layout, arrays = layout_of(pieces)
    out_layout, out_arrays = layout_of(out_pieces)
    flat = [one for pair in mids + grads for one in pair]
    big = (tokens, cotangent, q_rot, k_rot, k_turned, v_heads, raw, mixed)
    rows = pltpu.VMEM((total, depth), BF16)
    return pl.pallas_call(
        functools.partial(backward_kernel, layout, out_layout, parts),
        in_specs=[SM, SM] + [VM] * 8 + [ANY] * (1 + len(big) + len(flat) + len(arrays) + len(out_arrays)),
        out_specs=[VM, VM, ANY, ANY, ANY] + [VM] * 5,
        out_shape=[
            sds((parts, PIECE, depth), F32),
            sds((parts, PIECE, depth), F32),
            sds((total, depth), BF16),
            sds((total, cols), BF16),
            sds((total, depth), BF16),
            sds((1, width), F32),
            sds((1, width), F32),
            sds((1, depth), F32),
            sds((fa.shape[1], depth), F32),
            sds((fo.shape[1], heads * width), F32),
        ],
        scratch_shapes=[rows, rows, rows, rows, pltpu.VMEM((depth, cols), BF16), pltpu.VMEM((heads * width, depth), BF16)]
        + [pltpu.VMEM(one.shape, BF16) for one in (q_rot, k_rot, k_turned, v_heads, raw, mixed, hidden)]
        + [
            rows,
            pltpu.VMEM((total, cols), BF16),
            rows,
            pltpu.VMEM((groups, total, width), F32),
            pltpu.VMEM((groups, total, width), F32),
            pltpu.VMEM((groups, width, heads // groups * QUERIES), F32),
            pltpu.SemaphoreType.DMA((4, total // PIECE)),
            pltpu.SemaphoreType.DMA((7,)),
            pltpu.SemaphoreType.DMA((slots(layout),)),
            pltpu.SemaphoreType.DMA((slots(out_layout),)),
            pltpu.SemaphoreType.DMA((3, blocks)),
        ],
        compiler_params=params(),
        cost_estimate=cost(20e9, 30e6),
        name="attention_backward",
    )(rep, meta, gain, head_gains, cosine, sine, doc_start, logs, fa, fo, *big, *flat, hidden, *arrays, *out_arrays)


def shares_kernel(count, *refs):
    errors, starts, out_ref = refs[:count], refs[count:-1], refs[-1]
    blocks = []
    for error in errors:
        blocks += [error[at] for at in range(error.shape[0])] if len(error.shape) == 3 else [error[...]]
    first = 0
    for block, start in zip(blocks, starts):
        high = start[...].astype(BF16)
        low = (start[...] - high.astype(F32)).astype(BF16)
        both = nt(jnp.concatenate([high, low], axis=0), block.astype(BF16))
        ranks, rows = start.shape[0], block.shape[0]
        out_ref[:, first : first + rows] = both[:ranks] + both[ranks:]
        first += rows


def shares_of(errors, starts, rows):
    return pl.pallas_call(
        functools.partial(shares_kernel, len(errors)),
        in_specs=[VM] * (len(errors) + len(starts)),
        out_specs=VM,
        out_shape=sds((starts[0].shape[0], rows), F32),
        compiler_params=params(),
        cost_estimate=cost(1e9, 16e6),
        name="error_shares",
    )(*errors, *starts)


def feed_moment_kernel(steps, hid_ref, dgu_ref, gu_error, act_ref, cot_ref, d_error, gu_out, d_out):
    units = gu_out.shape[2]
    step = pl.program_id(0)

    @pl.when(step < steps)
    def _():
        both = tn(hid_ref[...], dgu_ref[...])
        for at in range(2):
            gu_out[at] = both[:, at * units : (at + 1) * units] + gu_error[at]

    @pl.when(step >= steps)
    def _():
        d_out[...] = tn(act_ref[...], cot_ref[...]) + d_error[...]


def feed_moments(hidden, grads, gu_error, active, cotangent, d_error):
    total, depth = hidden.shape
    units = active.shape[1]
    rows = 256
    steps, more = depth // rows, units // rows
    early = lambda i: jnp.minimum(i, steps - 1)
    late = lambda i: jnp.maximum(i - steps, 0)
    return pl.pallas_call(
        functools.partial(feed_moment_kernel, steps),
        grid=(steps + more,),
        in_specs=[
            pl.BlockSpec((total, rows), lambda i: (0, early(i))),
            pl.BlockSpec((total, 2 * units), lambda i: (0, 0)),
            pl.BlockSpec((2, rows, units), lambda i: (0, early(i), 0)),
            pl.BlockSpec((total, rows), lambda i: (0, late(i))),
            pl.BlockSpec((total, depth), lambda i: (0, 0)),
            pl.BlockSpec((rows, depth), lambda i: (late(i), 0)),
        ],
        out_specs=[
            pl.BlockSpec((2, rows, units), lambda i: (0, early(i), 0)),
            pl.BlockSpec((rows, depth), lambda i: (late(i), 0)),
        ],
        out_shape=[sds(gu_error.shape, F32), sds(d_error.shape, F32)],
        compiler_params=params(),
        cost_estimate=cost(1, 1),
        name="feed_moments",
    )(hidden, grads, gu_error, active, cotangent, d_error)


def pack_feed_kernel(ranks, parts, shares_ref, *refs):
    gu_lefts, d_lefts, out_ref = refs[:parts], refs[parts : 2 * parts], refs[-1]
    gu_left = sum(one[...] for one in gu_lefts[1:]) + gu_lefts[0][...]
    d_left = sum(one[...] for one in d_lefts[1:]) + d_lefts[0][...]
    depth = gu_left.shape[1]
    base = shares_ref.shape[1] - out_ref.shape[1]
    for at in range(2):
        piece = gu_left[at * ranks : (at + 1) * ranks, :]
        cols = slice(base + at * depth, base + (at + 1) * depth)
        out_ref[:, at * depth : (at + 1) * depth] = piece + shares_ref[:, cols]
    out_ref[:, 2 * depth :] = d_left[:ranks, :] + shares_ref[:, base + 2 * depth :]


def pack_feed_lefts(ranks, shares, lefts):
    flat = [one[0] for one in lefts] + [one[1] for one in lefts]
    cols = 2 * flat[0].shape[1] + flat[-1].shape[1]
    return pl.pallas_call(
        functools.partial(pack_feed_kernel, ranks, len(lefts)),
        in_specs=[VM] * (1 + len(flat)),
        out_specs=VM,
        out_shape=sds((ranks, cols), F32),
        compiler_params=params(),
        cost_estimate=cost(1, 1),
        name="pack_feed_lefts",
    )(shares, *flat)


def pack_kernel(ranks, shares_ref, all_left, out_left, first_ref, query_ref, key_ref, *refs):
    seconds, (left_ref, gains_ref) = refs[:-2], refs[-2:]
    depth = first_ref.shape[1]
    second = sum(one[...] for one in seconds[1:]) + seconds[0][...]
    for at in range(3):
        cols = slice(at * depth, (at + 1) * depth)
        left_ref[:, cols] = all_left[at * ranks : (at + 1) * ranks, :] + shares_ref[:, cols]
    left_ref[:, 3 * depth :] = out_left[:ranks, :] + shares_ref[:, 3 * depth : left_ref.shape[1]]
    gains_ref[...] = jnp.zeros_like(gains_ref)
    wide = depth // 4
    for at in range(4):
        gains_ref[at : at + 1, :wide] = first_ref[:, at * wide : (at + 1) * wide]
        gains_ref[4 + at : 5 + at, :wide] = second[:, at * wide : (at + 1) * wide]
    width = query_ref.shape[1]
    gains_ref[0:1, wide : wide + width] = query_ref[...]
    gains_ref[1:2, wide : wide + width] = key_ref[...]


def pack_sums(ranks, shares, all_left, out_left, first, query, key, seconds):
    depth = first.shape[1]
    cols = 3 * depth + out_left.shape[1]
    return pl.pallas_call(
        functools.partial(pack_kernel, ranks),
        in_specs=[VM] * (6 + len(seconds)),
        out_specs=[VM, VM],
        out_shape=[sds((ranks, cols), F32), sds((8, depth // 4 + query.shape[1]), F32)],
        compiler_params=params(),
        cost_estimate=cost(1, 1),
        name="pack_sums",
    )(shares, all_left, out_left, first, query, key, *seconds)


def orthonormal_panel(panel):
    ranks = panel.shape[0]
    index = lax.broadcasted_iota(jnp.int32, (ranks, 1), 0)
    for at in range(ranks):
        column = panel[at : at + 1, :]
        column = column * lax.rsqrt(jnp.sum(column * column, axis=1, keepdims=True) + EPSILON)
        dots = jnp.sum(panel * column, axis=1, keepdims=True)
        later = panel - dots * column
        panel = jnp.where(index > at, later, jnp.where(index == at, column, panel))
    return panel


def two_parts(value):
    high = value.astype(BF16)
    return high, (value - high.astype(F32)).astype(BF16)


def panels_of(refs):
    views = []
    for ref in refs:
        views += [ref.at[0], ref.at[1]] if len(ref.shape) == 3 else [ref]
    return views


def factors_kernel(count, kinds, lefts_ref, *refs):
    moments, lefts_out, rights_ref = refs[:count], refs[count : count + kinds], refs[count + kinds]
    held, sems = refs[count + kinds + 1 : -1], refs[-1]
    copies = [pltpu.make_async_copy(x, y, sems.at[i]) for i, (x, y) in enumerate(zip(panels_of(moments), panels_of(held)))]
    start_all(copies)
    done = []
    first = 0
    for source, target in zip(panels_of(held), panels_of(lefts_out)):
        rows = source.shape[0]
        done.append(orthonormal_panel(lefts_ref[:, first : first + rows]))
        target[...] = done[-1]
        first += rows
    first = 0
    for panel, source, copy in zip(done, panels_of(held), copies):
        ranks, cols = panel.shape[0], source.shape[1]
        both = jnp.concatenate(two_parts(panel), axis=0)
        copy.wait()
        result = nn(both, source[...].astype(BF16))
        rights_ref[:, first : first + cols] = result[:ranks] + result[ranks:]
        first += cols


def make_factors(label, lefts, moments, shapes, cols):
    ranks = lefts.shape[0]
    return pl.pallas_call(
        functools.partial(factors_kernel, len(moments), len(shapes)),
        in_specs=[VM] + [ANY] * len(moments),
        out_specs=[VM] * (len(shapes) + 1),
        out_shape=[sds(shape, F32) for shape in shapes] + [sds((ranks, cols), F32)],
        scratch_shapes=[pltpu.VMEM(one.shape, F32) for one in moments] + [pltpu.SemaphoreType.DMA((4,))],
        compiler_params=params(),
        cost_estimate=cost(1, 1),
        name=f"factors_{label}",
    )(lefts, *moments)


def settle_kernel(replicas, count, kinds, gained, rep, summed_ref, *refs):
    gains, refs = refs[: 4 * gained], refs[4 * gained :]
    lefts, refs = panels_of(refs[:kinds]), refs[kinds:]
    moments, refs = refs[:count], refs[count:]
    weights, velocities, outs = refs[:kinds], refs[kinds : 2 * kinds], refs[2 * kinds :]
    rights_out, outs = outs[:kinds], outs[kinds:]
    gains_out, outs = outs[: 4 * gained], outs[4 * gained :]
    errors_out, weights_out, velocities_out = outs[:kinds], outs[kinds : 2 * kinds], outs[2 * kinds : 3 * kinds]
    scratch = outs[3 * kinds :]
    held, approx = scratch[:count], scratch[count : 2 * count]
    weights_s, velocities_s = scratch[2 * count : 2 * count + kinds], scratch[2 * count + kinds : 2 * count + 2 * kinds]
    in_sems, small_sems, out_sems, last_sems = scratch[-4:]
    copies = [
        pltpu.make_async_copy(x, y, in_sems.at[i]) for i, (x, y) in enumerate(zip(panels_of(moments), panels_of(held)))
    ]
    small = [
        pltpu.make_async_copy(x, y, small_sems.at[i])
        for i, (x, y) in enumerate(zip(weights + velocities, weights_s + velocities_s))
    ]
    start_all(copies + small)
    if gained:
        bg_ref, bv_ref, hg_ref, hv_ref = gains
        wide = bg_ref.shape[1] // 4
        width = hg_ref.shape[1]
        base = summed_ref.shape[1] - wide - width
        for row in range(2):
            for at in range(4):
                cols = slice(at * wide, (at + 1) * wide)
                mean = summed_ref[4 * row + at : 4 * row + at + 1, base : base + wide] / replicas
                velocity = MOMENTUM * bv_ref[row : row + 1, cols] + mean
                gains_out[1][row : row + 1, cols] = velocity
                gains_out[0][row : row + 1, cols] = bg_ref[row : row + 1, cols] - GAIN_RATE * velocity
            mean = summed_ref[row : row + 1, base + wide : base + wide + width] / replicas
            velocity = MOMENTUM * hv_ref[row : row + 1, :] + mean
            gains_out[3][row : row + 1, :] = velocity
            gains_out[2][row : row + 1, :] = hg_ref[row : row + 1, :] - GAIN_RATE * velocity

    first = 0
    lasts = []
    everything = zip(lefts, panels_of(rights_out), panels_of(held), panels_of(approx), copies, panels_of(errors_out))
    for index, (left, right_out, moment, product, copy, target) in enumerate(everything):
        cols = moment.shape[1]
        right = summed_ref[:, first : first + cols] / replicas
        first += cols
        right_out[...] = right
        left_high, left_low = two_parts(left[...])
        right_high, right_low = two_parts(right)
        product[...] = tn(
            jnp.concatenate([left_high, left_low, left_high, left_low], axis=0),
            jnp.concatenate([right_high, right_high, right_low, right_low], axis=0),
        )
        copy.wait()
        moment[...] = moment[...] - product[...]
        lasts.append(pltpu.make_async_copy(moment, target, out_sems.at[index]))
        lasts[-1].start()
    wait_all(small)
    updates = zip(panels_of(approx), panels_of(weights_s), panels_of(velocities_s))
    for product, weight, velocity in updates:
        rows = weight.shape[0]
        mine = product[pl.ds(pl.multiple_of(rep[0] * rows, 8), rows), :]
        fresh = MOMENTUM * velocity[...] + mine
        velocity[...] = fresh
        weight[...] = weight[...] - STEP_RATE * fresh
    moves = zip(weights_s + velocities_s, weights_out + velocities_out)
    for index, (source, target) in enumerate(moves):
        lasts.append(pltpu.make_async_copy(source, target, last_sems.at[index]))
        lasts[-1].start()
    wait_all(lasts)


def settle(label, replicas, rep, summed, gains, lefts, moments, weights, velocities, rights, errors):
    small = [sds(one.shape, F32) for one in weights + velocities]
    kinds = len(lefts)
    outs = kinds + len(gains)
    results = pl.pallas_call(
        functools.partial(settle_kernel, replicas, len(moments), kinds, len(gains) // 4),
        in_specs=[SM] + [VM] * (1 + len(gains) + kinds) + [ANY] * (len(moments) + 2 * kinds),
        out_specs=[VM] * outs + [ANY] * (3 * kinds),
        out_shape=[sds(shape, F32) for shape in rights]
        + [sds(one.shape, F32) for one in gains]
        + [sds(shape, F32) for shape in errors]
        + small,
        scratch_shapes=[pltpu.VMEM(one.shape, F32) for one in moments + moments + weights + velocities]
        + [pltpu.SemaphoreType.DMA((2 * kinds,))] * 4,
        compiler_params=params(),
        cost_estimate=cost(1, 1),
        name=f"settle_{label}",
    )(rep, summed, *gains, *lefts, *moments, *weights, *velocities)
    rows = [results[outs + at * kinds : outs + (at + 1) * kinds] for at in range(3)]
    return results[:kinds], results[kinds:outs], rows


def on_device(
    tokens,
    cotangent,
    lengths,
    block_gains,
    block_velocity,
    head_gains,
    head_velocity,
    weight_query,
    velocity_query,
    error_query,
    factor_query,
    weight_keyval,
    velocity_keyval,
    error_keyval,
    factor_keyval,
    weight_out,
    velocity_out,
    error_out,
    factor_out,
    weight_gateup,
    velocity_gateup,
    error_gateup,
    factor_gateup,
    weight_down,
    velocity_down,
    error_down,
    factor_down,
):
    total, depth = tokens.shape
    width = head_gains.shape[1]
    heads = weight_query.shape[1] // width
    groups = weight_keyval.shape[2] // width
    units = weight_gateup.shape[2]
    quarter = total // 4
    parts = quarter // PIECE
    blocks = total // PIECE
    replicas = lax.axis_size("rep")
    rep_index = lax.axis_index("rep")
    kv_index = lax.axis_index("kv")
    core = lax.rem(kv_index, 2)
    half = kv_index // 2
    rep = rep_index[None].astype(jnp.int32)
    core_at = core[None].astype(jnp.int32)

    pieces_qkv = gather_halves(
        jnp.concatenate([weight_query, weight_keyval[0], weight_keyval[1]], axis=1).astype(BF16)
    )
    pieces_out = gather_halves(weight_out.astype(BF16))
    packed = pack_feed(
        jnp.concatenate([weight_gateup[0], weight_gateup[1]], axis=1).astype(BF16), weight_down.astype(BF16)
    )
    packed = lax.all_gather(packed, "rep", axis=0)

    own_lengths = lengths[0]
    docs = own_lengths.shape[0]
    before = jnp.arange(docs)[:, None] >= jnp.arange(docs)[None, :]
    ends = jnp.sum(jnp.where(before, own_lengths[None, :], 0), axis=1)
    places = jnp.arange(total, dtype=jnp.int32)
    passed = places[None, :] >= ends[:, None]
    doc_start = jnp.sum(jnp.where(passed, own_lengths[:, None], 0), axis=0, keepdims=True).astype(jnp.int32)
    position = (places[None, :] - doc_start)[0]
    meta = []
    for rows in (QUERIES, PIECE):
        block_ends = (jnp.arange(total // rows, dtype=jnp.int32) + 1) * rows
        turns = (block_ends - doc_start[0, ::rows] + KEYS - 1) // KEYS
        meta += [jnp.maximum(block_ends - turns * KEYS, 0), turns]
    meta = jnp.concatenate(meta + [core[None], half[None]]).astype(jnp.int32)

    half_index = jnp.arange(width // 2, dtype=F32)
    frequency = ROPE_BASE ** (-2.0 * half_index / width)
    angles = position.astype(F32)[:, None] * frequency[None, :]
    cosine, sine = jnp.cos(angles), jnp.sin(angles)
    cosine = jnp.concatenate([cosine, cosine], axis=1)
    sine = jnp.concatenate([-sine, sine], axis=1)

    tokens_cut = tokens.reshape(2, 2, parts, PIECE, depth)
    cot_cut = cotangent.reshape(2, 2, parts, PIECE, depth)

    def chip_sum(mine, theirs):
        return (mine.astype(F32) + theirs.astype(F32)).astype(BF16)

    def cross_sum(own, *earlier):
        theirs = flip_kv(own, 2)
        summed = (after(own, *earlier).astype(F32) + theirs.astype(F32)).astype(BF16)
        return summed, flip_kv(summed, 1)

    factors = [factor_query, factor_keyval[0], factor_keyval[1], factor_out[0], factor_gateup[0], factor_gateup[1]]
    factors = [one.T for one in factors + [factor_down[0]]]
    tied = (error_query[0], error_keyval[0], error_out[0], error_gateup[0], error_down[0])
    tied = lax.optimization_barrier((*tied, pieces_qkv[0][0], pieces_qkv[2 % len(pieces_qkv)][0]))[:5]
    query_rows, group_cols = heads * width, groups * width
    shares = shares_of(tied, factors, 5 * depth + query_rows + units)
    doc_start = after(doc_start, shares)
    ranks = factor_query.shape[1]

    def laid(parts_of):
        rows = []
        for at, one in enumerate(parts_of):
            pads = (at * ranks, 128 - (at + 1) * ranks)
            rows.append(jnp.pad(one.T, ((0, 0), pads)))
        return jnp.concatenate(rows, axis=0).astype(BF16)

    laid_attn, laid_feed = laid(factors[:3]), laid(factors[4:6])
    laid_out, laid_down = laid(factors[3:4]), laid(factors[6:7])
    doc_start = after(doc_start, laid_attn, laid_feed, laid_out, laid_down)

    hidden_first, q_rot, raw, k_rot, k_turned, v_heads, mixed, logs = forward(
        rep, meta, tokens, block_gains[0:1], head_gains, cosine, sine, doc_start, pieces_qkv, heads, groups
    )
    mine, other = branch(rep, core_at, mixed, pieces_out, depth)
    theirs = flip_kv(other, 1)
    owns = [chip_sum(mine[p], theirs[p]) for p in range(parts)]

    mids, chain, terms_parts, second_parts, left_parts, term_owns = [], [], [], [], [], []
    earlier = ()
    for part in range(parts):
        mids.append(cross_sum(owns[part], *earlier))
        here = mids[part][0]
        if part >= 2:
            mine, theirs = terms_parts[part - 2]
            term_owns.append(chip_sum(mine, after(theirs, terms_parts[part - 1][0])))
            here = after(here, term_owns[-1])
        mine, other, second, gu_left, d_left, *chain = feed(
            part, parts, core_at, laid_feed, laid_down, here, mids[part][1], tokens_cut, cot_cut, block_gains[1:2],
            packed, units, chain,
        )
        earlier = (mine,)
        terms_parts.append((mine, flip_kv(other, 1)))
        second_parts.append(second)
        left_parts.append((gu_left, d_left))
    down_terms = chain[0].reshape(total, depth)

    down_terms = chain[0].reshape(total, depth)
    last = terms_parts[parts - 1][0]
    bits = rep_bits()
    feed_lefts = pack_feed_lefts(ranks, shares, left_parts)
    pending = begin_sum(feed_lefts, bits[0])
    grads = [cross_sum(term_owns[0], last)]
    term_owns.append(chip_sum(terms_parts[1][0], after(terms_parts[1][1], grads[0][0])))
    term_owns.append(chip_sum(terms_parts[2][0], after(terms_parts[2][1], term_owns[1])))
    feed_lefts = end_sum(pending, term_owns[2])
    pending = begin_sum(feed_lefts, bits[1])
    *chain, _, _ = lax.optimization_barrier((*chain[1:], term_owns[2], feed_lefts))
    hid_full, act_full, dgu_full = [one.reshape(total, -1) for one in chain]
    moment_gateup, moment_down = feed_moments(
        hid_full, dgu_full, error_gateup[0], act_full, cotangent, error_down[0]
    )
    feed_lefts = end_sum(pending, moment_down)
    pending = begin_sum(feed_lefts, bits[2])
    grads.append(cross_sum(term_owns[1], moment_down))
    grads.append(cross_sum(term_owns[2], moment_down))
    feed_own = lax.psum_scatter(after(down_terms, grads[2][0]), "kv", scatter_dimension=0, tiled=True)

    own_grad, own_middle, gb_full, grads_qkv, input_terms, head_query, head_key, first_gain, all_left, out_left = backward(
        rep, meta, block_gains[1:2], head_gains, cosine, sine, doc_start, logs, tokens, cotangent, q_rot, k_rot,
        k_turned, v_heads, raw, mixed, hidden_first, laid_attn, laid_out, mids, grads, pieces_qkv, pieces_out,
    )

    attn_lefts, gains = pack_sums(
        ranks, shares, after(all_left, feed_own), out_left, first_gain, head_query, head_key, second_parts
    )
    feed_lefts = end_sum(pending, own_grad)
    for bit in bits[3:]:
        feed_lefts = end_sum(begin_sum(feed_lefts, bit))
    pending = begin_sum(attn_lefts, bits[0])
    *left_feed, right_feed = make_factors(
        "feed", after(feed_lefts, attn_lefts), [moment_gateup, moment_down],
        [(2, ranks, depth), (ranks, units)], 2 * units + depth,
    )
    gains = gains + flip_kv(gains, 1)
    attn_lefts = end_sum(pending, right_feed)
    pending, feed_pending = begin_sum(attn_lefts, bits[1]), begin_sum(right_feed, bits[0])
    grads_qkv = after(grads_qkv, attn_lefts)
    moment_query = tn(hidden_first, grads_qkv[:, :query_rows]) + error_query[0]
    attn_lefts, right_feed = end_sum(pending, moment_query), end_sum(feed_pending, moment_query)
    pending, feed_pending = begin_sum(attn_lefts, bits[2]), begin_sum(right_feed, bits[1])
    gains = gains + flip_kv(gains, 2)
    moment_out = tn(mixed, after(gb_full, attn_lefts, right_feed)) + error_out[0]
    attn_lefts, right_feed = end_sum(pending, moment_out), end_sum(feed_pending, moment_out)
    feed_pending = begin_sum(right_feed, bits[2])
    for bit in bits[3:]:
        attn_lefts = end_sum(begin_sum(attn_lefts, bit))
    grads_qkv = after(grads_qkv, attn_lefts, right_feed)
    moment_key = tn(hidden_first, grads_qkv[:, query_rows : query_rows + group_cols]) + error_keyval[0, 0]
    moment_value = tn(hidden_first, grads_qkv[:, query_rows + group_cols :]) + error_keyval[0, 1]
    right_feed = end_sum(feed_pending, moment_key, moment_value)
    for bit in bits[3:]:
        right_feed = end_sum(begin_sum(right_feed, bit))
    attn_moments = [moment_query, moment_key, moment_value, moment_out]
    *left_attn, right_attn = make_factors(
        "attn", after(attn_lefts, right_feed), attn_moments,
        [(ranks, depth), (2, ranks, depth), (ranks, query_rows)], query_rows + 2 * group_cols + depth,
    )
    summed = jnp.concatenate([right_attn, gains], axis=1)
    pending = begin_sum(summed, bits[0])
    feed_rights, _, feed_rest = settle(
        "feed", replicas, rep, after(right_feed, right_attn), [], left_feed, [moment_gateup, moment_down],
        [weight_gateup, weight_down], [velocity_gateup, velocity_down],
        [(2, ranks, units), (ranks, depth)], [moment_gateup.shape, moment_down.shape],
    )
    summed = end_sum(pending, feed_rights[1])
    pending = begin_sum(summed, bits[1])

    grad_first = lax.psum_scatter(input_terms, "kv", scatter_dimension=0, tiled=True)
    own_middle, own_grad, feed_own, _ = lax.optimization_barrier((own_middle, own_grad, feed_own, summed))
    layer_out = (own_middle.reshape(quarter, depth) + feed_own.astype(F32)).astype(BF16)
    summed = end_sum(pending, layer_out)
    pending = begin_sum(summed, bits[2])
    own_tokens = lax.dynamic_slice_in_dim(tokens, kv_index * quarter, quarter, 0).astype(F32)
    unit, scale = unit_of(own_tokens)
    grad_first = after(grad_first, summed).astype(F32)
    input_grad = own_grad.reshape(quarter, depth) + norm_back(grad_first, unit, scale, block_gains[0])
    summed = end_sum(pending, input_grad)
    for bit in bits[3:]:
        summed = end_sum(begin_sum(summed, bit))
    attn_rights, gains, attn_rest = settle(
        "attn", replicas, rep, summed, [block_gains, block_velocity, head_gains, head_velocity], left_attn, attn_moments,
        [weight_query, weight_keyval, weight_out], [velocity_query, velocity_keyval, velocity_out],
        [(ranks, query_rows), (2, ranks, group_cols), (ranks, depth)],
        [moment_query.shape, (2,) + moment_key.shape, moment_out.shape],
    )

    def turned_over(value):
        return jnp.swapaxes(value, -1, -2)

    def five(rest, at, left, right):
        errors, weights, velocities = rest
        return [weights[at], velocities[at], errors[at][None], turned_over(left), turned_over(right)]

    outputs = [layer_out, input_grad, *gains]
    outputs += five(attn_rest, 0, left_attn[0][None], attn_rights[0])
    outputs += five(attn_rest, 1, left_attn[1][:, None], attn_rights[1])
    outputs += five(attn_rest, 2, left_attn[2], attn_rights[2][None])
    outputs += five(feed_rest, 0, left_feed[0][:, None], feed_rights[0])
    outputs += five(feed_rest, 1, left_feed[1], feed_rights[1][None])
    return tuple(outputs)


def solution(mesh):
    placed = (
        P("rep", None),
        P("rep", None),
        P("rep", None),
        P(),
        P(),
        P(),
        P(),
        P("rep", "kv"),
        P("rep", "kv"),
        P("rep", None, "kv"),
        P("kv", None),
        P(None, "rep", "kv"),
        P(None, "rep", "kv"),
        P("rep", None, None, "kv"),
        P(None, "kv", None),
        P(("kv", "rep"), None),
        P(("kv", "rep"), None),
        P("rep", "kv", None),
        P("kv", None, None),
        P(None, "rep", "kv"),
        P(None, "rep", "kv"),
        P("rep", None, None, "kv"),
        P(None, "kv", None),
        P(("kv", "rep"), None),
        P(("kv", "rep"), None),
        P("rep", "kv", None),
        P("kv", None, None),
    )
    return jax.shard_map(
        on_device,
        mesh=mesh,
        in_specs=placed,
        out_specs=(
            P(("rep", "kv"), None),
            P(("rep", "kv"), None),
            P(),
            P(),
            P(),
            P(),
            P("rep", "kv"),
            P("rep", "kv"),
            P("rep", None, "kv"),
            P("kv", None, None),
            P("kv", None),
            P(None, "rep", "kv"),
            P(None, "rep", "kv"),
            P("rep", None, None, "kv"),
            P(None, "kv", None, None),
            P(None, "kv", None),
            P(("kv", "rep"), None),
            P(("kv", "rep"), None),
            P("rep", "kv", None),
            P("kv", None),
            P("kv", None, None),
            P(None, "rep", "kv"),
            P(None, "rep", "kv"),
            P("rep", None, None, "kv"),
            P(None, "kv", None, None),
            P(None, "kv", None),
            P(("kv", "rep"), None),
            P(("kv", "rep"), None),
            P("rep", "kv", None),
            P("kv", None),
            P("kv", None, None),
        ),
        check_vma=False,
    )
```

```python
import functools
import math

import jax
import jax.numpy as jnp
from jax import lax
from jax.experimental import pallas as pl
from jax.experimental.pallas import tpu as pltpu
from jax.sharding import PartitionSpec as P

EPSILON = 1e-06
ROPE_BASE = 1000000.0
MOMENTUM = 0.9
STEP_RATE = 0.04
GAIN_RATE = 0.005
PIECE = 128
QUERIES = 256
KEYS = 512
KEYS_BACK = 256
F32 = jnp.float32
BF16 = jnp.bfloat16
VMEM_LIMIT = 56 * 1024 * 1024


def nn(left, right):
    return lax.dot_general(left, right, (((1,), (0,)), ((), ())), preferred_element_type=F32)


def nt(left, right):
    return lax.dot_general(left, right, (((1,), (1,)), ((), ())), preferred_element_type=F32)


def tn(left, right):
    return lax.dot_general(left, right, (((0,), (0,)), ((), ())), preferred_element_type=F32)


def params(limit=VMEM_LIMIT):
    return pltpu.CompilerParams(vmem_limit_bytes=limit)


def cost(flops, moved, exps=0):
    return pl.CostEstimate(flops=int(flops / 8), bytes_accessed=int(moved / 8), transcendentals=0)


def sds(shape, dtype):
    return jax.ShapeDtypeStruct(shape, dtype)


VM = pl.BlockSpec(memory_space=pltpu.VMEM)
SM = pl.BlockSpec(memory_space=pltpu.SMEM)
ANY = pl.BlockSpec(memory_space=pl.ANY)


def flip_kv(value, bit):
    size = lax.axis_size("kv")
    return lax.ppermute(value, "kv", [(i, i ^ bit) for i in range(size)])


def flip_rep(value, bit):
    size = lax.axis_size("rep")
    return lax.ppermute(value, "rep", [(i, i ^ bit) for i in range(size)])


def after(value, *earlier):
    return lax.optimization_barrier((value, *earlier))[0]


def rounded(value):
    return lax.reduce_precision(value, exponent_bits=8, mantissa_bits=7)


def rep_bits():
    return [1 << i for i in range(lax.axis_size("rep").bit_length() - 1)]


def begin_sum(value, bit):
    held = rounded(value.astype(F32))
    return held, flip_rep(held.astype(BF16), bit)


def end_sum(pair, *earlier):
    return after(pair[0], *earlier) + pair[1].astype(F32)


def xor_codes(bits):
    codes = (0,)
    for bit in bits:
        codes = codes + tuple(code ^ bit for code in codes)
    return codes


def spread(value, bits):
    for bit in bits[:-1]:
        value = jnp.concatenate([value, flip_rep(value, bit)], axis=0)
    codes = xor_codes(bits)
    middle = len(codes) // 2
    return [(value, codes[:middle]), (flip_rep(value, bits[-1]), codes[middle:])]


def gather_halves(chunk):
    replicas = lax.axis_size("rep")
    falling = [1 << i for i in range(replicas.bit_length() - 2, -1, -1)]
    rows = chunk.shape[0]
    if rows % 32 != 0:
        return [part + (0,) for part in spread(chunk, falling)]
    rising = falling[-1:] + falling[:-1]
    first = [part + (0,) for part in spread(chunk[: rows // 2], falling)]
    return first + [part + (rows // 2,) for part in spread(chunk[rows // 2 :], rising)]


def piece_copies(rep, layout, refs, target, sems):
    share = target.shape[0] // sum(len(codes) for codes, offset in layout if offset == 0)
    copies = []
    for (codes, offset), ref in zip(layout, refs):
        rows = ref.shape[0] // len(codes)
        for at, code in enumerate(codes):
            first = pl.multiple_of(lax.bitwise_xor(rep, code) * share + offset, 8)
            copies.append(
                pltpu.make_async_copy(
                    ref.at[pl.ds(at * rows, rows), :], target.at[pl.ds(first, rows), :], sems.at[len(copies)]
                )
            )
    return copies


def pack_feed(gateup, down):
    depth = down.shape[1]
    rows = gateup.shape[0]
    rest = gateup[:, depth:]
    rest = jnp.concatenate([rest[: rows // 2], rest[rows // 2 :]], axis=1)
    return jnp.concatenate([gateup[:, :depth], rest, down], axis=0)


def feed_copies(packed, gateup, down, sems):
    replicas = packed.shape[0]
    depth = down.shape[1]
    rows, low_rows = gateup.shape[0] // replicas, down.shape[0] // replicas
    half = rows // 2
    rest = gateup.shape[1] - depth
    first, second = [], []
    for at in range(replicas):
        top = at * rows
        pairs = [
            (packed.at[at, 0:rows, :], gateup.at[top : top + rows, 0:depth]),
            (packed.at[at, rows : rows + half, 0:rest], gateup.at[top : top + half, depth : depth + rest]),
            (packed.at[at, rows : rows + half, rest : 2 * rest], gateup.at[top + half : top + rows, depth : depth + rest]),
        ]
        first += [pltpu.make_async_copy(x, y, sems.at[at * 4 + i]) for i, (x, y) in enumerate(pairs)]
        second.append(
            pltpu.make_async_copy(
                packed.at[at, rows + half : rows + half + low_rows, :],
                down.at[at * low_rows : (at + 1) * low_rows, :],
                sems.at[at * 4 + 3],
            )
        )
    return first, second


def start_all(copies):
    for copy in copies:
        copy.start()


def wait_all(copies):
    for copy in copies:
        copy.wait()


def unit_of(values):
    scale = lax.rsqrt(jnp.mean(values * values, axis=-1, keepdims=True) + EPSILON)
    return values * scale, scale


def norm_back(grad, unit, scale, gain):
    weighted = grad * gain
    return scale * (weighted - unit * jnp.mean(weighted * unit, axis=-1, keepdims=True))


def forward_kernel(layout, rep, meta, tok_ref, gain_ref, head_ref, cos_ref, sin_ref, start_ref, *refs):
    pieces = refs[: len(layout)]
    hid_out, q_out, raw_out, k_out, kt_out, v_out, mixed_out, log_ref = refs[len(layout) : len(layout) + 8]
    (tok_s, w_s, hid_s, q_s, raw_s, k_s, kt_s, v_s, vt_s, mixed_s, out_acc, sum_acc) = refs[len(layout) + 8 : -3]
    in_sems, w_sems, out_sems = refs[-3:]
    heads, total, width = q_s.shape
    groups = k_s.shape[0]
    pairs = heads // groups
    blocks = total // QUERIES
    factor = math.log2(math.e) / math.sqrt(width)

    def token_copy(block):
        here = pl.ds(pl.multiple_of(block * QUERIES, QUERIES), QUERIES)
        return pltpu.make_async_copy(tok_ref.at[here, :], tok_s.at[here, :], in_sems.at[block])

    def sent(block):
        here = pl.ds(pl.multiple_of(block * QUERIES, QUERIES), QUERIES)
        pairs_of = [
            (hid_s.at[here, :], hid_out.at[here, :]),
            (q_s.at[:, here, :], q_out.at[:, here, :]),
            (raw_s.at[:, here, :], raw_out.at[:, here, :]),
            (k_s.at[:, here, :], k_out.at[:, here, :]),
            (kt_s.at[:, :, here], kt_out.at[:, :, here]),
            (v_s.at[:, here, :], v_out.at[:, here, :]),
            (mixed_s.at[here, :], mixed_out.at[here, :]),
        ]
        return [pltpu.make_async_copy(x, y, out_sems.at[i, block]) for i, (x, y) in enumerate(pairs_of)]

    weights = piece_copies(rep[0], layout, pieces, w_s, w_sems)
    token_copy(0).start()
    start_all(weights)
    for block in range(1, blocks):
        token_copy(block).start()
    log_ref[...] = jnp.zeros_like(log_ref)
    vt_s[...] = jnp.zeros_like(vt_s)
    wait_all(weights)

    @pl.loop(0, blocks)
    def _(block):
        low, count = meta[block], meta[blocks + block]
        here = pl.ds(pl.multiple_of(block * QUERIES, QUERIES), QUERIES)
        token_copy(block).wait()
        unit, _ = unit_of(tok_s[here, :].astype(F32))
        hidden = (unit * gain_ref[...]).astype(BF16)
        hid_s[here, :] = hidden
        projected = nn(hidden, w_s[...])
        cosine, sine = cos_ref[here, :], sin_ref[here, :]
        means = jnp.full((width, width), 1.0 / width, BF16)
        for index in range(heads + groups):
            one = projected[:, index * width : (index + 1) * width]
            raw_s[index, here, :] = one.astype(BF16)
            gain = head_ref[0:1, :] if index < heads else head_ref[1:2, :]
            normed = one * lax.rsqrt(nn((one * one).astype(BF16), means) + EPSILON) * gain
            turned = normed * cosine + pltpu.roll(normed, width // 2, 1) * sine
            if index < heads:
                q_s[index, here, :] = turned.astype(BF16)
            else:
                k_s[index - heads, here, :] = turned.astype(BF16)
                kt_s[index - heads, :, here] = turned.T.astype(BF16)
        for index in range(groups):
            first = (heads + groups + index) * width
            one = projected[:, first : first + width]
            v_s[index, here, :] = one.astype(BF16)
            vt_s[index, :, here] = one.T.astype(BF16)

        start = jnp.concatenate([start_ref[:, here]] * pairs, axis=1)
        place = block * QUERIES + lax.broadcasted_iota(jnp.int32, (1, QUERIES), 1)
        place = jnp.concatenate([place] * pairs, axis=1)
        queries = [
            jnp.concatenate([q_s[g * pairs + j, here, :] for j in range(pairs)], axis=0) for g in range(groups)
        ]
        out_acc[...] = jnp.zeros_like(out_acc)
        sum_acc[...] = jnp.zeros_like(sum_acc)

        @pl.loop(0, count)
        def _(turn):
            base = pl.multiple_of(low + turn * KEYS, PIECE)
            key_place = base + lax.broadcasted_iota(jnp.int32, (KEYS, 1), 0)
            allowed = (key_place >= start) & (key_place <= place)
            for g in range(groups):
                scores = nt(k_s[g, pl.ds(base, KEYS), :], queries[g])
                weights = jnp.where(allowed, jnp.exp2(scores * factor), 0.0)
                sum_acc[g] += jnp.sum(weights, axis=0, keepdims=True)
                out_acc[g] += nn(vt_s[g, :, pl.ds(base, KEYS)], weights.astype(BF16))

        for g in range(groups):
            total_weight = sum_acc[g]
            mixed = out_acc[g] / total_weight
            logs = jnp.log2(total_weight)
            for j in range(pairs):
                head = g * pairs + j
                mixed_s[here, head * width : (head + 1) * width] = mixed[:, j * QUERIES : (j + 1) * QUERIES].T.astype(BF16)
                log_ref[head : head + 1, here] = logs[:, j * QUERIES : (j + 1) * QUERIES]
        start_all(sent(block))

    @pl.loop(0, blocks)
    def _(block):
        wait_all(sent(block))


def layout_of(pieces):
    return tuple((codes, offset) for _, codes, offset in pieces), [piece for piece, _, _ in pieces]


def slots(layout):
    return sum(len(codes) for codes, _ in layout)


def forward(rep, meta, tokens, gain, head_gains, cosine, sine, doc_start, pieces, heads, groups):
    total, depth = tokens.shape
    width = head_gains.shape[1]
    cols = pieces[0][0].shape[1]
    layout, arrays = layout_of(pieces)
    wide = heads // groups * QUERIES
    blocks = total // QUERIES
    outs = [
        (total, depth),
        (heads, total, width),
        (heads + groups, total, width),
        (groups, total, width),
        (groups, width, total),
        (groups, total, width),
        (total, heads * width),
    ]
    return pl.pallas_call(
        functools.partial(forward_kernel, layout),
        in_specs=[SM, SM, ANY] + [VM] * 5 + [ANY] * len(arrays),
        out_specs=[ANY] * 7 + [VM],
        out_shape=[sds(shape, BF16) for shape in outs] + [sds((8, total), F32)],
        scratch_shapes=[pltpu.VMEM((total, depth), BF16), pltpu.VMEM((depth, cols), BF16)]
        + [pltpu.VMEM(shape, BF16) for shape in outs[:6]]
        + [
            pltpu.VMEM((groups, width, total), BF16),
            pltpu.VMEM((total, heads * width), BF16),
            pltpu.VMEM((groups, width, wide), F32),
            pltpu.VMEM((groups, 1, wide), F32),
            pltpu.SemaphoreType.DMA((blocks,)),
            pltpu.SemaphoreType.DMA((slots(layout),)),
            pltpu.SemaphoreType.DMA((7, blocks)),
        ],
        compiler_params=params(),
        cost_estimate=cost(12e9, 20e6),
        name="attention_forward",
    )(rep, meta, tokens, gain, head_gains, cosine, sine, doc_start, *arrays)


def branch_kernel(layout, rep, core, mixed_ref, *refs):
    pieces = refs[: len(layout)]
    mine_out, other_out, w_s, mixed_s, out_s, sems, w_sems, out_sems = refs[len(layout) :]
    quarter = mixed_s.shape[1]
    loads = [
        pltpu.make_async_copy(mixed_ref.at[pl.ds(at * quarter, quarter), :], mixed_s.at[at], sems.at[at]) for at in range(4)
    ]
    weights = piece_copies(rep[0], layout, pieces, w_s, w_sems)
    start_all(weights + loads)
    wait_all(weights)
    lasts = []
    for step in range(4):
        spot = step % 2
        side = 1 - step // 2
        at = 2 * spot + lax.rem(core[0] + side, 2)
        if step == 0:
            wait_all(loads)
        out_s[step] = nn(mixed_s[at], w_s[...]).astype(BF16).reshape(out_s.shape[1:])
        lasts.append(
            pltpu.make_async_copy(out_s.at[step], (mine_out, other_out)[side].at[:, spot], out_sems.at[step])
        )
        lasts[-1].start()
    wait_all(lasts)


def branch(rep, core, mixed, pieces, depth):
    total, cols = mixed.shape
    layout, arrays = layout_of(pieces)
    parts = total // 4 // PIECE
    return pl.pallas_call(
        functools.partial(branch_kernel, layout),
        in_specs=[SM, SM] + [ANY] * (1 + len(arrays)),
        out_specs=[ANY, ANY],
        out_shape=[sds((parts, 2, PIECE, depth), BF16)] * 2,
        scratch_shapes=[
            pltpu.VMEM((cols, depth), BF16),
            pltpu.VMEM((4, total // 4, cols), BF16),
            pltpu.VMEM((4, parts, PIECE, depth), BF16),
            pltpu.SemaphoreType.DMA((4,)),
            pltpu.SemaphoreType.DMA((slots(layout),)),
            pltpu.SemaphoreType.DMA((4,)),
        ],
        compiler_params=params(),
        cost_estimate=cost(2 * total * cols * depth, 6e6),
        name="branch",
    )(rep, core, mixed, *arrays)


def feed_kernel(part, core, gain_ref, here_ref, there_ref, tok_ref, cot_ref, packed_ref, *refs):
    mine_out, other_out, sum_ref, down_out, hid_out, act_out, dgu_out = refs[-18:-11]
    mid_s, tok_s, cot_s, wgu_s, wd_s, terms_s, down_s, hid_s, act_s, dgu_s, sems = refs[-11:]
    units = wd_s.shape[0]
    spots = [(side, spot) for side in (1, 0) for spot in range(2)]
    spare = 4 * packed_ref.shape[0]

    def natural(ref, side, spot):
        return ref.at[spot, lax.rem(core[0] + side, 2), part]

    def rows(index):
        return pl.ds(index * PIECE, PIECE)

    first, cots, lasts = [], [], []
    for index, (side, spot) in enumerate(spots):
        at = spare + 8 * index
        source = (here_ref, there_ref)[side].at[spot]
        first.append(pltpu.make_async_copy(source, mid_s.at[rows(index), :], sems.at[at]))
        first.append(pltpu.make_async_copy(natural(tok_ref, side, spot), tok_s.at[rows(index), :], sems.at[at + 1]))
        cots.append(pltpu.make_async_copy(natural(cot_ref, side, spot), cot_s.at[rows(index), :], sems.at[at + 2]))
    gateups, downs = feed_copies(packed_ref, wgu_s, wd_s, sems)
    start_all(first + gateups + cots + downs)

    def send(scratch, target_of, kind):
        for index, (side, spot) in enumerate(spots):
            lasts.append(
                pltpu.make_async_copy(
                    scratch.at[rows(index), :], target_of(side, spot), sems.at[spare + 8 * index + 3 + kind]
                )
            )
            lasts[-1].start()

    wait_all(first)
    unit, _ = unit_of(tok_s[...].astype(F32) + mid_s[...].astype(F32))
    hid_s[...] = (unit * gain_ref[...]).astype(BF16)
    send(hid_s, lambda side, spot: natural(hid_out, side, spot), 0)
    wait_all(gateups)
    both = nn(hid_s[...], wgu_s[...])
    wait_all(cots + downs)
    grad_active = nt(cot_s[...], wd_s[...])
    gate, up = both[:, :units], both[:, units:]
    sig = jax.nn.sigmoid(gate)
    lit = gate * sig
    act_s[...] = (lit * up).astype(BF16)
    send(act_s, lambda side, spot: natural(act_out, side, spot), 1)
    dgu_s[:, :units] = (grad_active * up * sig * (1.0 + gate * (1.0 - sig))).astype(BF16)
    dgu_s[:, units:] = (grad_active * lit).astype(BF16)
    send(dgu_s, lambda side, spot: natural(dgu_out, side, spot), 2)
    terms = nt(dgu_s[...], wgu_s[...])
    terms_s[...] = terms.astype(BF16)
    send(terms_s, lambda side, spot: (mine_out, other_out)[side].at[spot], 3)
    down_s[...] = nn(act_s[...], wd_s[...]).astype(BF16)
    send(down_s, lambda side, spot: natural(down_out, side, spot), 4)
    sum_ref[...] = jnp.sum(terms * unit, axis=0, keepdims=True)
    wait_all(lasts)


def feed(part, parts, core, here, there, tokens_cut, cot_cut, gain, packed, units, chain):
    depth = gain.shape[1]
    saved = (
        (2, 2, parts, PIECE, depth),
        (2, 2, parts, PIECE, depth),
        (2, 2, parts, PIECE, units),
        (2, 2, parts, PIECE, 2 * units),
    )
    rows = 4 * PIECE
    return pl.pallas_call(
        functools.partial(feed_kernel, part),
        in_specs=[SM, VM] + [ANY] * (5 + len(chain)),
        out_specs=[ANY, ANY, VM] + [ANY] * 4,
        out_shape=[sds((2, PIECE, depth), BF16)] * 2
        + [sds((1, depth), F32)]
        + [sds(shape, BF16) for shape in saved],
        scratch_shapes=[
            pltpu.VMEM((rows, depth), BF16),
            pltpu.VMEM((rows, depth), BF16),
            pltpu.VMEM((rows, depth), BF16),
            pltpu.VMEM((depth, 2 * units), BF16),
            pltpu.VMEM((units, depth), BF16),
            pltpu.VMEM((rows, depth), BF16),
            pltpu.VMEM((rows, depth), BF16),
            pltpu.VMEM((rows, depth), BF16),
            pltpu.VMEM((rows, units), BF16),
            pltpu.VMEM((rows, 2 * units), BF16),
            pltpu.SemaphoreType.DMA((4 * packed.shape[0] + 32,)),
        ],
        input_output_aliases={7 + i: 3 + i for i in range(len(chain))},
        compiler_params=params(),
        cost_estimate=cost(2 * 4 * PIECE * depth * units * 6, 12e6),
        name=f"feed_{part}",
    )(core, gain, here, there, tokens_cut, cot_cut, packed, *chain)


def backward_kernel(layout, out_layout, parts, rep, meta, mid_gain, head_ref, cos_ref, sin_ref, start_ref, log_ref, fa_ref, fo_ref, *refs):
    (tok_ref, cot_ref, q_hbm, k_hbm, kt_hbm, v_hbm, raw_hbm, mixed_hbm) = refs[:8]
    mid_parts, grad_parts = refs[8 : 8 + 2 * parts], refs[8 + 2 * parts : 12 + 2 * parts]
    hid_hbm = refs[12 + 2 * parts]
    refs = refs[13 + 2 * parts :]
    pieces, out_pieces = refs[: len(layout)], refs[len(layout) : len(layout) + len(out_layout)]
    rest = refs[len(layout) + len(out_layout) :]
    (own_ref, own_mid, gb_out, grads_out, terms_out, query_sum, key_sum, first_sum, all_left, out_left) = rest[:10]
    (mid_s, grad_s, tok_s, cot_s, w_s, wo_s, q_s, k_s, kt_s, v_s, raw_s, mixed_s, hid_s, gb_s, all_s, terms_s, dk_s, dv_s, dq_acc) = rest[10:-5]
    row_sems, big_sems, w_sems, wo_sems, out_sems = rest[-5:]
    heads, total, width = q_s.shape
    groups = k_s.shape[0]
    pairs = heads // groups
    blocks, cuts = total // QUERIES, total // PIECE
    per = QUERIES // PIECE
    core, half = meta[4 * blocks], meta[4 * blocks + 1]
    root = 1.0 / math.sqrt(width)
    factor = math.log2(math.e) * root

    def grad_copy(side, part, spot, cut):
        source = grad_parts[side].at[spot] if part == 0 else grad_parts[2 + side].at[2 * part - 2 + spot]
        return pltpu.make_async_copy(source, grad_s.at[pl.ds(cut * PIECE, PIECE), :], row_sems.at[1, cut])

    def row_copies(cut):
        quarter, part = cut // parts, cut % parts
        spot = quarter // 2
        here = pl.ds(cut * PIECE, PIECE)
        near = lax.rem(core + quarter, 2) == 0

        @pl.when(near)
        def _():
            pltpu.make_async_copy(mid_parts[2 * part].at[spot], mid_s.at[here, :], row_sems.at[0, cut]).start()
            grad_copy(0, part, spot, cut).start()

        @pl.when(jnp.logical_not(near))
        def _():
            pltpu.make_async_copy(mid_parts[2 * part + 1].at[spot], mid_s.at[here, :], row_sems.at[0, cut]).start()
            grad_copy(1, part, spot, cut).start()

        pltpu.make_async_copy(tok_ref.at[here, :], tok_s.at[here, :], row_sems.at[2, cut]).start()
        pltpu.make_async_copy(cot_ref.at[here, :], cot_s.at[here, :], row_sems.at[3, cut]).start()

    big = [
        pltpu.make_async_copy(x, y, big_sems.at[i])
        for i, (x, y) in enumerate(
            [
                (k_hbm, k_s), (v_hbm, v_s), (q_hbm, q_s), (kt_hbm, kt_s), (mixed_hbm, mixed_s),
                (raw_hbm, raw_s), (hid_hbm, hid_s),
            ]
        )
    ]
    weights = piece_copies(rep[0], layout, pieces, w_s, w_sems)
    out_weights = piece_copies(rep[0], out_layout, out_pieces, wo_s, wo_sems)
    for cut in range(cuts - 1, cuts - 1 - per, -1):
        row_copies(cut)
    start_all(out_weights + big + weights)
    for cut in range(cuts - 1 - per, -1, -1):
        row_copies(cut)
    dk_s[...] = jnp.zeros_like(dk_s)
    dv_s[...] = jnp.zeros_like(dv_s)
    query_sum[...] = jnp.zeros_like(query_sum)
    key_sum[...] = jnp.zeros_like(key_sum)
    first_sum[...] = jnp.zeros_like(first_sum)
    ones = jnp.ones((8, width), F32)
    query_gain, key_gain = head_ref[0:1, :], head_ref[1:2, :]
    means = jnp.full((width, width), 1.0 / width, BF16)

    def mean_of(values):
        return nn(values.astype(BF16), means)

    def head_back(grad, raw, cosine, sine, gain):
        turned = grad * cosine - pltpu.roll(grad, width // 2, 1) * sine
        scale = lax.rsqrt(mean_of(raw * raw) + EPSILON)
        unit = raw * scale
        weighted = turned * gain
        back = scale * (weighted - unit * mean_of(weighted * unit))
        return back.astype(BF16), jnp.sum(turned * unit, axis=0, keepdims=True)

    def out_copies(block):
        here = pl.ds(pl.multiple_of(block * QUERIES, QUERIES), QUERIES)
        pairs_of = [(gb_s, gb_out), (all_s, grads_out), (terms_s, terms_out)]
        return [
            pltpu.make_async_copy(x.at[here, :], y.at[here, :], out_sems.at[i, block]) for i, (x, y) in enumerate(pairs_of)
        ]

    @pl.loop(0, blocks)
    def _(turn_of):
        block = blocks - 1 - turn_of
        low, count = meta[2 * blocks + block], meta[3 * blocks + block]
        rows = pl.ds(pl.multiple_of(block * QUERIES, QUERIES), QUERIES)
        for at in range(per):
            cut = block * per + at
            here = pl.ds(pl.multiple_of(cut * PIECE, PIECE), PIECE)
            for kind, target in enumerate((mid_s, grad_s, tok_s, cot_s)):
                pltpu.make_async_copy(tok_ref.at[here, :], target.at[here, :], row_sems.at[kind, cut]).wait()
        middle = tok_s[rows, :].astype(F32) + mid_s[rows, :].astype(F32)
        unit, scale = unit_of(middle)
        result = cot_s[rows, :].astype(F32) + norm_back(grad_s[rows, :].astype(F32), unit, scale, mid_gain[...])
        low_grad = result.astype(BF16)
        gb_s[rows, :] = low_grad
        for at in range(per):
            cut = block * per + at

            @pl.when(cut // parts == 2 * half + core)
            def _():
                own_ref[lax.rem(cut, parts)] = result[at * PIECE : (at + 1) * PIECE]
                own_mid[lax.rem(cut, parts)] = middle[at * PIECE : (at + 1) * PIECE]

        @pl.when(turn_of == 0)
        def _():
            wait_all(out_weights + big)

        grad_mixed = nt(low_grad, wo_s[...]).astype(BF16)
        mixed = mixed_s[rows, :]
        start = jnp.concatenate([start_ref[:, rows]] * pairs, axis=1)
        place = block * QUERIES + lax.broadcasted_iota(jnp.int32, (1, QUERIES), 1)
        place = jnp.concatenate([place] * pairs, axis=1)
        queries, grads, logs, deltas = [], [], [], []
        for g in range(groups):
            members = range(g * pairs, (g + 1) * pairs)
            queries.append(jnp.concatenate([q_s[h, rows, :] for h in members], axis=0))
            grad = jnp.concatenate([grad_mixed[:, h * width : (h + 1) * width] for h in members], axis=0)
            out = jnp.concatenate([mixed[:, h * width : (h + 1) * width] for h in members], axis=0)
            grads.append(grad)
            logs.append(jnp.concatenate([log_ref[h : h + 1, rows] for h in members], axis=1))
            terms = lax.dot_general(
                ones,
                grad.astype(F32) * out.astype(F32),
                (((1,), (1,)), ((), ())),
                precision=lax.Precision.HIGHEST,
                preferred_element_type=F32,
            )
            deltas.append(terms[0:1, :])
        dq_acc[...] = jnp.zeros_like(dq_acc)

        @pl.loop(0, count)
        def _(turn):
            base = pl.multiple_of(low + turn * KEYS_BACK, PIECE)
            key_place = base + lax.broadcasted_iota(jnp.int32, (KEYS_BACK, 1), 0)
            allowed = (key_place >= start) & (key_place <= place)
            keys = pl.ds(base, KEYS_BACK)
            for g in range(groups):
                scores = nt(k_s[g, keys, :], queries[g])
                weights = jnp.where(allowed, jnp.exp2(scores * factor - logs[g]), 0.0)
                grad_weights = nt(v_s[g, keys, :], grads[g])
                grad_scores = (weights * (grad_weights - deltas[g])).astype(BF16)
                dv_s[g, keys, :] += nn(weights.astype(BF16), grads[g])
                dk_s[g, keys, :] += nn(grad_scores, queries[g])
                dq_acc[g] += nn(kt_s[g, :, keys], grad_scores)

        cosine, sine = cos_ref[rows, :], sin_ref[rows, :]
        sums = jnp.zeros((1, width), F32)
        columns = []
        for head in range(heads):
            j = head % pairs
            grad = dq_acc[head // pairs, :, j * QUERIES : (j + 1) * QUERIES].T * root
            back, part_sum = head_back(grad, raw_s[head, rows, :].astype(F32), cosine, sine, query_gain)
            columns.append(back)
            sums = sums + part_sum
        query_sum[...] += sums
        sums = jnp.zeros((1, width), F32)
        for g in range(groups):
            back, part_sum = head_back(
                dk_s[g, rows, :] * root, raw_s[heads + g, rows, :].astype(F32), cosine, sine, key_gain
            )
            columns.append(back)
            sums = sums + part_sum
        key_sum[...] += sums
        for g in range(groups):
            columns.append(dv_s[g, rows, :].astype(BF16))
        everything = jnp.concatenate(columns, axis=1)
        all_s[rows, :] = everything

        @pl.when(turn_of == 0)
        def _():
            wait_all(weights)

        terms = nt(everything, w_s[...])
        first_sum[...] += jnp.sum(terms * unit_of(tok_s[rows, :].astype(F32))[0], axis=0, keepdims=True)
        terms_s[rows, :] = terms.astype(BF16)
        start_all(out_copies(block))

    all_left[...] = tn(nn(all_s[...], fa_ref[...]).astype(BF16), hid_s[...])
    out_left[...] = tn(nn(gb_s[...], fo_ref[...]).astype(BF16), mixed_s[...])

    @pl.loop(0, blocks)
    def _(block):
        wait_all(out_copies(block))


def backward(
    rep, meta, gain, head_gains, cosine, sine, doc_start, logs, tokens, cotangent, q_rot, k_rot, k_turned, v_heads, raw,
    mixed, hidden, fa, fo, mids, grads, pieces, out_pieces
):
    heads, total, width = q_rot.shape
    groups = k_rot.shape[0]
    depth = tokens.shape[1]
    cols = pieces[0][0].shape[1]
    parts = len(mids)
    blocks = total // QUERIES
    layout, arrays = layout_of(pieces)
    out_layout, out_arrays = layout_of(out_pieces)
    flat = [one for pair in mids + grads for one in pair]
    big = (tokens, cotangent, q_rot, k_rot, k_turned, v_heads, raw, mixed)
    rows = pltpu.VMEM((total, depth), BF16)
    return pl.pallas_call(
        functools.partial(backward_kernel, layout, out_layout, parts),
        in_specs=[SM, SM] + [VM] * 8 + [ANY] * (1 + len(big) + len(flat) + len(arrays) + len(out_arrays)),
        out_specs=[VM, VM, ANY, ANY, ANY] + [VM] * 5,
        out_shape=[
            sds((parts, PIECE, depth), F32),
            sds((parts, PIECE, depth), F32),
            sds((total, depth), BF16),
            sds((total, cols), BF16),
            sds((total, depth), BF16),
            sds((1, width), F32),
            sds((1, width), F32),
            sds((1, depth), F32),
            sds((fa.shape[1], depth), F32),
            sds((fo.shape[1], heads * width), F32),
        ],
        scratch_shapes=[rows, rows, rows, rows, pltpu.VMEM((depth, cols), BF16), pltpu.VMEM((heads * width, depth), BF16)]
        + [pltpu.VMEM(one.shape, BF16) for one in (q_rot, k_rot, k_turned, v_heads, raw, mixed, hidden)]
        + [
            rows,
            pltpu.VMEM((total, cols), BF16),
            rows,
            pltpu.VMEM((groups, total, width), F32),
            pltpu.VMEM((groups, total, width), F32),
            pltpu.VMEM((groups, width, heads // groups * QUERIES), F32),
            pltpu.SemaphoreType.DMA((4, total // PIECE)),
            pltpu.SemaphoreType.DMA((7,)),
            pltpu.SemaphoreType.DMA((slots(layout),)),
            pltpu.SemaphoreType.DMA((slots(out_layout),)),
            pltpu.SemaphoreType.DMA((3, blocks)),
        ],
        compiler_params=params(),
        cost_estimate=cost(20e9, 30e6),
        name="attention_backward",
    )(rep, meta, gain, head_gains, cosine, sine, doc_start, logs, fa, fo, *big, *flat, hidden, *arrays, *out_arrays)


def shares_kernel(count, *refs):
    errors, starts, out_ref = refs[:count], refs[count:-1], refs[-1]
    blocks = []
    for error in errors:
        blocks += [error[at] for at in range(error.shape[0])] if len(error.shape) == 3 else [error[...]]
    first = 0
    for block, start in zip(blocks, starts):
        high = start[...].astype(BF16)
        low = (start[...] - high.astype(F32)).astype(BF16)
        both = nt(jnp.concatenate([high, low], axis=0), block.astype(BF16))
        ranks, rows = start.shape[0], block.shape[0]
        out_ref[:, first : first + rows] = both[:ranks] + both[ranks:]
        first += rows


def shares_of(errors, starts, rows):
    return pl.pallas_call(
        functools.partial(shares_kernel, len(errors)),
        in_specs=[VM] * (len(errors) + len(starts)),
        out_specs=VM,
        out_shape=sds((starts[0].shape[0], rows), F32),
        compiler_params=params(),
        cost_estimate=cost(1e9, 16e6),
        name="error_shares",
    )(*errors, *starts)


def feed_moment_kernel(steps, hid_ref, dgu_ref, gu_error, act_ref, cot_ref, d_error, gu_start, d_start, *outs):
    gu_out, d_out, gu_left, d_left = outs
    units = gu_out.shape[2]
    step = pl.program_id(0)

    def left_of(start, moment):
        both = nt(jnp.concatenate(two_parts(start), axis=0), moment.astype(BF16))
        ranks = start.shape[0]
        return both[:ranks] + both[ranks:]

    @pl.when(step < steps)
    def _():
        both = tn(hid_ref[...], dgu_ref[...])
        for at in range(2):
            moment = both[:, at * units : (at + 1) * units] + gu_error[at]
            gu_out[at] = moment
            gu_left[at] = left_of(gu_start[at], moment)

    @pl.when(step >= steps)
    def _():
        moment = tn(act_ref[...], cot_ref[...]) + d_error[...]
        d_out[...] = moment
        d_left[...] = left_of(d_start[...], moment)


def feed_moments(hidden, grads, gu_error, active, cotangent, d_error, gu_start, d_start):
    total, depth = hidden.shape
    units = active.shape[1]
    ranks = d_start.shape[0]
    rows, low_rows = 512, 384
    steps, more = depth // rows, units // low_rows
    early = lambda i: jnp.minimum(i, steps - 1)
    late = lambda i: jnp.maximum(i - steps, 0)
    return pl.pallas_call(
        functools.partial(feed_moment_kernel, steps),
        grid=(steps + more,),
        in_specs=[
            pl.BlockSpec((total, rows), lambda i: (0, early(i))),
            pl.BlockSpec((total, 2 * units), lambda i: (0, 0)),
            pl.BlockSpec((2, rows, units), lambda i: (0, early(i), 0)),
            pl.BlockSpec((total, low_rows), lambda i: (0, late(i))),
            pl.BlockSpec((total, depth), lambda i: (0, 0)),
            pl.BlockSpec((low_rows, depth), lambda i: (late(i), 0)),
            pl.BlockSpec((2, ranks, units), lambda i: (0, 0, 0)),
            pl.BlockSpec((ranks, depth), lambda i: (0, 0)),
        ],
        out_specs=[
            pl.BlockSpec((2, rows, units), lambda i: (0, early(i), 0)),
            pl.BlockSpec((low_rows, depth), lambda i: (late(i), 0)),
            pl.BlockSpec((2, ranks, rows), lambda i: (0, 0, early(i))),
            pl.BlockSpec((ranks, low_rows), lambda i: (0, late(i))),
        ],
        out_shape=[
            sds(gu_error.shape, F32),
            sds(d_error.shape, F32),
            sds((2, ranks, depth), F32),
            sds((ranks, units), F32),
        ],
        compiler_params=params(),
        cost_estimate=cost(1, 1),
        name="feed_moments",
    )(hidden, grads, gu_error, active, cotangent, d_error, gu_start, d_start)


def pack_kernel(ranks, shares_ref, all_left, out_left, first_ref, query_ref, key_ref, *refs):
    seconds, (left_ref, gains_ref) = refs[:-2], refs[-2:]
    depth = first_ref.shape[1]
    second = sum(one[...] for one in seconds[1:]) + seconds[0][...]
    for at in range(3):
        cols = slice(at * depth, (at + 1) * depth)
        left_ref[:, cols] = all_left[at * ranks : (at + 1) * ranks, :] + shares_ref[:, cols]
    left_ref[:, 3 * depth :] = out_left[:ranks, :] + shares_ref[:, 3 * depth : left_ref.shape[1]]
    gains_ref[...] = jnp.zeros_like(gains_ref)
    wide = depth // 4
    for at in range(4):
        gains_ref[at : at + 1, :wide] = first_ref[:, at * wide : (at + 1) * wide]
        gains_ref[4 + at : 5 + at, :wide] = second[:, at * wide : (at + 1) * wide]
    width = query_ref.shape[1]
    gains_ref[0:1, wide : wide + width] = query_ref[...]
    gains_ref[1:2, wide : wide + width] = key_ref[...]


def pack_sums(ranks, shares, all_left, out_left, first, query, key, seconds):
    depth = first.shape[1]
    cols = 3 * depth + out_left.shape[1]
    return pl.pallas_call(
        functools.partial(pack_kernel, ranks),
        in_specs=[VM] * (6 + len(seconds)),
        out_specs=[VM, VM],
        out_shape=[sds((ranks, cols), F32), sds((8, depth // 4 + query.shape[1]), F32)],
        compiler_params=params(),
        cost_estimate=cost(1, 1),
        name="pack_sums",
    )(shares, all_left, out_left, first, query, key, *seconds)


def orthonormal_panel(panel):
    ranks = panel.shape[0]
    index = lax.broadcasted_iota(jnp.int32, (ranks, 1), 0)
    for at in range(ranks):
        column = panel[at : at + 1, :]
        column = column * lax.rsqrt(jnp.sum(column * column, axis=1, keepdims=True) + EPSILON)
        dots = jnp.sum(panel * column, axis=1, keepdims=True)
        later = panel - dots * column
        panel = jnp.where(index > at, later, jnp.where(index == at, column, panel))
    return panel


def two_parts(value):
    high = value.astype(BF16)
    return high, (value - high.astype(F32)).astype(BF16)


def panels_of(refs):
    views = []
    for ref in refs:
        views += [ref.at[0], ref.at[1]] if len(ref.shape) == 3 else [ref]
    return views


def factors_kernel(count, kinds, lefts_ref, *refs):
    moments, lefts_out, rights_ref = refs[:count], refs[count : count + kinds], refs[count + kinds]
    held, sems = refs[count + kinds + 1 : -1], refs[-1]
    copies = [pltpu.make_async_copy(x, y, sems.at[i]) for i, (x, y) in enumerate(zip(panels_of(moments), panels_of(held)))]
    start_all(copies)
    done = []
    first = 0
    for source, target in zip(panels_of(held), panels_of(lefts_out)):
        rows = source.shape[0]
        done.append(orthonormal_panel(lefts_ref[:, first : first + rows]))
        target[...] = done[-1]
        first += rows
    first = 0
    for panel, source, copy in zip(done, panels_of(held), copies):
        ranks, cols = panel.shape[0], source.shape[1]
        both = jnp.concatenate(two_parts(panel), axis=0)
        copy.wait()
        result = nn(both, source[...].astype(BF16))
        rights_ref[:, first : first + cols] = result[:ranks] + result[ranks:]
        first += cols


def make_factors(label, lefts, moments, shapes, cols):
    ranks = lefts.shape[0]
    return pl.pallas_call(
        functools.partial(factors_kernel, len(moments), len(shapes)),
        in_specs=[VM] + [ANY] * len(moments),
        out_specs=[VM] * (len(shapes) + 1),
        out_shape=[sds(shape, F32) for shape in shapes] + [sds((ranks, cols), F32)],
        scratch_shapes=[pltpu.VMEM(one.shape, F32) for one in moments] + [pltpu.SemaphoreType.DMA((4,))],
        compiler_params=params(),
        cost_estimate=cost(1, 1),
        name=f"factors_{label}",
    )(lefts, *moments)


def settle_kernel(replicas, count, kinds, gained, rep, summed_ref, *refs):
    gains, refs = refs[: 4 * gained], refs[4 * gained :]
    lefts, refs = panels_of(refs[:kinds]), refs[kinds:]
    moments, refs = refs[:count], refs[count:]
    weights, velocities, outs = refs[:kinds], refs[kinds : 2 * kinds], refs[2 * kinds :]
    rights_out, outs = outs[:kinds], outs[kinds:]
    gains_out, outs = outs[: 4 * gained], outs[4 * gained :]
    errors_out, weights_out, velocities_out = outs[:kinds], outs[kinds : 2 * kinds], outs[2 * kinds : 3 * kinds]
    scratch = outs[3 * kinds :]
    held, approx = scratch[:count], scratch[count : 2 * count]
    weights_s, velocities_s = scratch[2 * count : 2 * count + kinds], scratch[2 * count + kinds : 2 * count + 2 * kinds]
    in_sems, small_sems, out_sems, last_sems = scratch[-4:]
    copies = [
        pltpu.make_async_copy(x, y, in_sems.at[i]) for i, (x, y) in enumerate(zip(panels_of(moments), panels_of(held)))
    ]
    small = [
        pltpu.make_async_copy(x, y, small_sems.at[i])
        for i, (x, y) in enumerate(zip(weights + velocities, weights_s + velocities_s))
    ]
    start_all(copies + small)
    if gained:
        bg_ref, bv_ref, hg_ref, hv_ref = gains
        wide = bg_ref.shape[1] // 4
        width = hg_ref.shape[1]
        base = summed_ref.shape[1] - wide - width
        for row in range(2):
            for at in range(4):
                cols = slice(at * wide, (at + 1) * wide)
                mean = summed_ref[4 * row + at : 4 * row + at + 1, base : base + wide] / replicas
                velocity = MOMENTUM * bv_ref[row : row + 1, cols] + mean
                gains_out[1][row : row + 1, cols] = velocity
                gains_out[0][row : row + 1, cols] = bg_ref[row : row + 1, cols] - GAIN_RATE * velocity
            mean = summed_ref[row : row + 1, base + wide : base + wide + width] / replicas
            velocity = MOMENTUM * hv_ref[row : row + 1, :] + mean
            gains_out[3][row : row + 1, :] = velocity
            gains_out[2][row : row + 1, :] = hg_ref[row : row + 1, :] - GAIN_RATE * velocity

    first = 0
    lasts = []
    everything = zip(lefts, panels_of(rights_out), panels_of(held), panels_of(approx), copies, panels_of(errors_out))
    for index, (left, right_out, moment, product, copy, target) in enumerate(everything):
        cols = moment.shape[1]
        right = summed_ref[:, first : first + cols] / replicas
        first += cols
        right_out[...] = right
        left_high, left_low = two_parts(left[...])
        right_high, right_low = two_parts(right)
        product[...] = tn(
            jnp.concatenate([left_high, left_low, left_high, left_low], axis=0),
            jnp.concatenate([right_high, right_high, right_low, right_low], axis=0),
        )
        copy.wait()
        moment[...] = moment[...] - product[...]
        lasts.append(pltpu.make_async_copy(moment, target, out_sems.at[index]))
        lasts[-1].start()
    wait_all(small)
    updates = zip(panels_of(approx), panels_of(weights_s), panels_of(velocities_s))
    for product, weight, velocity in updates:
        rows = weight.shape[0]
        mine = product[pl.ds(pl.multiple_of(rep[0] * rows, 8), rows), :]
        fresh = MOMENTUM * velocity[...] + mine
        velocity[...] = fresh
        weight[...] = weight[...] - STEP_RATE * fresh
    moves = zip(weights_s + velocities_s, weights_out + velocities_out)
    for index, (source, target) in enumerate(moves):
        lasts.append(pltpu.make_async_copy(source, target, last_sems.at[index]))
        lasts[-1].start()
    wait_all(lasts)


def settle(label, replicas, rep, summed, gains, lefts, moments, weights, velocities, rights, errors):
    small = [sds(one.shape, F32) for one in weights + velocities]
    kinds = len(lefts)
    outs = kinds + len(gains)
    results = pl.pallas_call(
        functools.partial(settle_kernel, replicas, len(moments), kinds, len(gains) // 4),
        in_specs=[SM] + [VM] * (1 + len(gains) + kinds) + [ANY] * (len(moments) + 2 * kinds),
        out_specs=[VM] * outs + [ANY] * (3 * kinds),
        out_shape=[sds(shape, F32) for shape in rights]
        + [sds(one.shape, F32) for one in gains]
        + [sds(shape, F32) for shape in errors]
        + small,
        scratch_shapes=[pltpu.VMEM(one.shape, F32) for one in moments + moments + weights + velocities]
        + [pltpu.SemaphoreType.DMA((2 * kinds,))] * 4,
        compiler_params=params(),
        cost_estimate=cost(1, 1),
        name=f"settle_{label}",
    )(rep, summed, *gains, *lefts, *moments, *weights, *velocities)
    rows = [results[outs + at * kinds : outs + (at + 1) * kinds] for at in range(3)]
    return results[:kinds], results[kinds:outs], rows


def on_device(
    tokens,
    cotangent,
    lengths,
    block_gains,
    block_velocity,
    head_gains,
    head_velocity,
    weight_query,
    velocity_query,
    error_query,
    factor_query,
    weight_keyval,
    velocity_keyval,
    error_keyval,
    factor_keyval,
    weight_out,
    velocity_out,
    error_out,
    factor_out,
    weight_gateup,
    velocity_gateup,
    error_gateup,
    factor_gateup,
    weight_down,
    velocity_down,
    error_down,
    factor_down,
):
    total, depth = tokens.shape
    width = head_gains.shape[1]
    heads = weight_query.shape[1] // width
    groups = weight_keyval.shape[2] // width
    units = weight_gateup.shape[2]
    quarter = total // 4
    parts = quarter // PIECE
    blocks = total // PIECE
    replicas = lax.axis_size("rep")
    rep_index = lax.axis_index("rep")
    kv_index = lax.axis_index("kv")
    core = lax.rem(kv_index, 2)
    half = kv_index // 2
    rep = rep_index[None].astype(jnp.int32)
    core_at = core[None].astype(jnp.int32)

    pieces_qkv = gather_halves(
        jnp.concatenate([weight_query, weight_keyval[0], weight_keyval[1]], axis=1).astype(BF16)
    )
    pieces_out = gather_halves(weight_out.astype(BF16))
    packed = pack_feed(
        jnp.concatenate([weight_gateup[0], weight_gateup[1]], axis=1).astype(BF16), weight_down.astype(BF16)
    )
    packed = lax.all_gather(packed, "rep", axis=0)

    own_lengths = lengths[0]
    docs = own_lengths.shape[0]
    before = jnp.arange(docs)[:, None] >= jnp.arange(docs)[None, :]
    ends = jnp.sum(jnp.where(before, own_lengths[None, :], 0), axis=1)
    places = jnp.arange(total, dtype=jnp.int32)
    passed = places[None, :] >= ends[:, None]
    doc_start = jnp.sum(jnp.where(passed, own_lengths[:, None], 0), axis=0, keepdims=True).astype(jnp.int32)
    position = (places[None, :] - doc_start)[0]
    meta = []
    for rows, keys in ((QUERIES, KEYS), (QUERIES, KEYS_BACK)):
        block_ends = (jnp.arange(total // rows, dtype=jnp.int32) + 1) * rows
        turns = (block_ends - doc_start[0, ::rows] + keys - 1) // keys
        meta += [jnp.maximum(block_ends - turns * keys, 0), turns]
    meta = jnp.concatenate(meta + [core[None], half[None]]).astype(jnp.int32)

    half_index = jnp.arange(width // 2, dtype=F32)
    frequency = ROPE_BASE ** (-2.0 * half_index / width)
    angles = position.astype(F32)[:, None] * frequency[None, :]
    cosine, sine = jnp.cos(angles), jnp.sin(angles)
    cosine = jnp.concatenate([cosine, cosine], axis=1)
    sine = jnp.concatenate([-sine, sine], axis=1)

    tokens_cut = tokens.reshape(2, 2, parts, PIECE, depth)
    cot_cut = cotangent.reshape(2, 2, parts, PIECE, depth)

    def chip_sum(mine, theirs):
        return (mine.astype(F32) + theirs.astype(F32)).astype(BF16)

    def cross_sum(own, *earlier):
        theirs = flip_kv(own, 2)
        summed = (after(own, *earlier).astype(F32) + theirs.astype(F32)).astype(BF16)
        return summed, flip_kv(summed, 1)

    factors = [one.T for one in (factor_query, factor_keyval[0], factor_keyval[1], factor_out[0])]
    tied = (error_query[0], error_keyval[0], error_out[0])
    tied = lax.optimization_barrier((*tied, pieces_qkv[0][0], pieces_qkv[2 % len(pieces_qkv)][0]))[:3]
    query_rows, group_cols = heads * width, groups * width
    shares = shares_of(tied, factors, 3 * depth + query_rows)
    doc_start = after(doc_start, shares)
    ranks = factor_query.shape[1]

    def laid(parts_of):
        rows = []
        for at, one in enumerate(parts_of):
            pads = (at * ranks, 128 - (at + 1) * ranks)
            rows.append(jnp.pad(one.T, ((0, 0), pads)))
        return jnp.concatenate(rows, axis=0).astype(BF16)

    laid_attn, laid_out = laid(factors[:3]), laid(factors[3:4])
    doc_start = after(doc_start, laid_attn, laid_out)

    hidden_first, q_rot, raw, k_rot, k_turned, v_heads, mixed, logs = forward(
        rep, meta, tokens, block_gains[0:1], head_gains, cosine, sine, doc_start, pieces_qkv, heads, groups
    )
    mine, other = branch(rep, core_at, mixed, pieces_out, depth)
    owns = [chip_sum(mine[0], flip_kv(other[0], 1))]
    theirs = flip_kv(after(other[1:], owns[0]), 1)
    owns += [chip_sum(mine[p + 1], theirs[p]) for p in range(parts - 1)]

    mids, chain, terms_parts, second_parts, term_owns = [], [], [], [], []
    earlier = ()
    for part in range(parts):
        mids.append(cross_sum(owns[part], *earlier))
        here = mids[part][0]
        if part >= 2:
            mine, theirs = terms_parts[part - 2]
            term_owns.append(chip_sum(mine, after(theirs, terms_parts[part - 1][0])))
            here = after(here, term_owns[-1])
        mine, other, second, *chain = feed(
            part, parts, core_at, here, mids[part][1], tokens_cut, cot_cut, block_gains[1:2],
            packed, units, chain,
        )
        earlier = (mine,)
        terms_parts.append((mine, flip_kv(other, 1)))
        second_parts.append(second)
    down_terms = chain[0].reshape(total, depth)

    down_terms = chain[0].reshape(total, depth)
    last = terms_parts[parts - 1][0]
    bits = rep_bits()
    grads = [cross_sum(term_owns[0], last)]
    term_owns.append(chip_sum(terms_parts[1][0], after(terms_parts[1][1], grads[0][0])))
    term_owns.append(chip_sum(terms_parts[2][0], after(terms_parts[2][1], term_owns[1])))
    both_owns = jnp.concatenate(term_owns[1:], axis=0)
    *chain, _ = lax.optimization_barrier((*chain[1:], both_owns))
    hid_full, act_full, dgu_full = [one.reshape(total, -1) for one in chain]
    moment_gateup, moment_down, gu_left, d_left = feed_moments(
        hid_full, dgu_full, error_gateup[0], act_full, cotangent, error_down[0], jnp.swapaxes(factor_gateup, 1, 2),
        factor_down[0].T,
    )
    feed_lefts = jnp.concatenate([gu_left[0], gu_left[1], d_left], axis=1)
    pending = begin_sum(feed_lefts, bits[0])
    grads.append(cross_sum(both_owns, moment_down))
    feed_lefts = end_sum(pending, grads[1][0])
    pending = begin_sum(feed_lefts, bits[1])
    feed_own = lax.psum_scatter(after(down_terms, grads[1][0]), "kv", scatter_dimension=0, tiled=True)

    own_grad, own_middle, gb_full, grads_qkv, input_terms, head_query, head_key, first_gain, all_left, out_left = backward(
        rep, meta, block_gains[1:2], head_gains, cosine, sine, doc_start, logs, tokens, cotangent, q_rot, k_rot,
        k_turned, v_heads, raw, mixed, hidden_first, laid_attn, laid_out, mids, grads, pieces_qkv, pieces_out,
    )

    attn_lefts, gains = pack_sums(
        ranks, shares, after(all_left, feed_own), out_left, first_gain, head_query, head_key, second_parts
    )
    feed_lefts = end_sum(pending, own_grad)
    pending, feed_pending = begin_sum(attn_lefts, bits[0]), begin_sum(feed_lefts, bits[2])
    grads_qkv = after(grads_qkv, attn_lefts, feed_lefts)
    moment_query = tn(hidden_first, grads_qkv[:, :query_rows]) + error_query[0]
    gains = gains + flip_kv(gains, 1)
    attn_lefts, feed_lefts = end_sum(pending, moment_query), end_sum(feed_pending, moment_query)
    for bit in bits[3:]:
        feed_lefts = end_sum(begin_sum(feed_lefts, bit))
    pending = begin_sum(attn_lefts, bits[1])
    *left_feed, right_feed = make_factors(
        "feed", after(feed_lefts, attn_lefts), [moment_gateup, moment_down],
        [(2, ranks, depth), (ranks, units)], 2 * units + depth,
    )
    gains = gains + flip_kv(gains, 2)
    attn_lefts = end_sum(pending, right_feed)
    pending, feed_pending = begin_sum(attn_lefts, bits[2]), begin_sum(right_feed, bits[0])
    moment_out = tn(mixed, after(gb_full, attn_lefts, right_feed)) + error_out[0]
    attn_lefts, right_feed = end_sum(pending, moment_out), end_sum(feed_pending, moment_out)
    feed_pending = begin_sum(right_feed, bits[1])
    for bit in bits[3:]:
        attn_lefts = end_sum(begin_sum(attn_lefts, bit))
    grads_qkv = after(grads_qkv, attn_lefts, right_feed)
    moment_key = tn(hidden_first, grads_qkv[:, query_rows : query_rows + group_cols]) + error_keyval[0, 0]
    moment_value = tn(hidden_first, grads_qkv[:, query_rows + group_cols :]) + error_keyval[0, 1]
    right_feed = end_sum(feed_pending, moment_key, moment_value)
    feed_pending = begin_sum(right_feed, bits[2])
    attn_moments = [moment_query, moment_key, moment_value, moment_out]
    *left_attn, right_attn = make_factors(
        "attn", after(attn_lefts, right_feed), attn_moments,
        [(ranks, depth), (2, ranks, depth), (ranks, query_rows)], query_rows + 2 * group_cols + depth,
    )
    right_feed = end_sum(feed_pending, right_attn)
    for bit in bits[3:]:
        right_feed = end_sum(begin_sum(right_feed, bit))
    summed = jnp.concatenate([right_attn, gains], axis=1)
    pending = begin_sum(summed, bits[0])
    feed_rights, _, feed_rest = settle(
        "feed", replicas, rep, after(right_feed, right_attn), [], left_feed, [moment_gateup, moment_down],
        [weight_gateup, weight_down], [velocity_gateup, velocity_down],
        [(2, ranks, units), (ranks, depth)], [moment_gateup.shape, moment_down.shape],
    )
    summed = end_sum(pending, feed_rights[1])
    pending = begin_sum(summed, bits[1])

    grad_first = lax.psum_scatter(input_terms, "kv", scatter_dimension=0, tiled=True)
    own_middle, own_grad, feed_own, _ = lax.optimization_barrier((own_middle, own_grad, feed_own, summed))
    layer_out = (own_middle.reshape(quarter, depth) + feed_own.astype(F32)).astype(BF16)
    summed = end_sum(pending, layer_out)
    pending = begin_sum(summed, bits[2])
    own_tokens = lax.dynamic_slice_in_dim(tokens, kv_index * quarter, quarter, 0).astype(F32)
    unit, scale = unit_of(own_tokens)
    grad_first = after(grad_first, summed).astype(F32)
    input_grad = own_grad.reshape(quarter, depth) + norm_back(grad_first, unit, scale, block_gains[0])
    summed = end_sum(pending, input_grad)
    for bit in bits[3:]:
        summed = end_sum(begin_sum(summed, bit))
    attn_rights, gains, attn_rest = settle(
        "attn", replicas, rep, summed, [block_gains, block_velocity, head_gains, head_velocity], left_attn, attn_moments,
        [weight_query, weight_keyval, weight_out], [velocity_query, velocity_keyval, velocity_out],
        [(ranks, query_rows), (2, ranks, group_cols), (ranks, depth)],
        [moment_query.shape, (2,) + moment_key.shape, moment_out.shape],
    )

    def turned_over(value):
        return jnp.swapaxes(value, -1, -2)

    def five(rest, at, left, right):
        errors, weights, velocities = rest
        return [weights[at], velocities[at], errors[at][None], turned_over(left), turned_over(right)]

    outputs = [layer_out, input_grad, *gains]
    outputs += five(attn_rest, 0, left_attn[0][None], attn_rights[0])
    outputs += five(attn_rest, 1, left_attn[1][:, None], attn_rights[1])
    outputs += five(attn_rest, 2, left_attn[2], attn_rights[2][None])
    outputs += five(feed_rest, 0, left_feed[0][:, None], feed_rights[0])
    outputs += five(feed_rest, 1, left_feed[1], feed_rights[1][None])
    return tuple(outputs)


def solution(mesh):
    placed = (
        P("rep", None),
        P("rep", None),
        P("rep", None),
        P(),
        P(),
        P(),
        P(),
        P("rep", "kv"),
        P("rep", "kv"),
        P("rep", None, "kv"),
        P("kv", None),
        P(None, "rep", "kv"),
        P(None, "rep", "kv"),
        P("rep", None, None, "kv"),
        P(None, "kv", None),
        P(("kv", "rep"), None),
        P(("kv", "rep"), None),
        P("rep", "kv", None),
        P("kv", None, None),
        P(None, "rep", "kv"),
        P(None, "rep", "kv"),
        P("rep", None, None, "kv"),
        P(None, "kv", None),
        P(("kv", "rep"), None),
        P(("kv", "rep"), None),
        P("rep", "kv", None),
        P("kv", None, None),
    )
    return jax.shard_map(
        on_device,
        mesh=mesh,
        in_specs=placed,
        out_specs=(
            P(("rep", "kv"), None),
            P(("rep", "kv"), None),
            P(),
            P(),
            P(),
            P(),
            P("rep", "kv"),
            P("rep", "kv"),
            P("rep", None, "kv"),
            P("kv", None, None),
            P("kv", None),
            P(None, "rep", "kv"),
            P(None, "rep", "kv"),
            P("rep", None, None, "kv"),
            P(None, "kv", None, None),
            P(None, "kv", None),
            P(("kv", "rep"), None),
            P(("kv", "rep"), None),
            P("rep", "kv", None),
            P("kv", None),
            P("kv", None, None),
            P(None, "rep", "kv"),
            P(None, "rep", "kv"),
            P("rep", None, None, "kv"),
            P(None, "kv", None, None),
            P(None, "kv", None),
            P(("kv", "rep"), None),
            P(("kv", "rep"), None),
            P("rep", "kv", None),
            P("kv", None),
            P("kv", None, None),
        ),
        check_vma=False,
    )
```

```python
import functools
import math

import jax
import jax.numpy as jnp
from jax import lax
from jax.experimental import pallas as pl
from jax.experimental.pallas import tpu as pltpu
from jax.sharding import PartitionSpec as P

EPSILON = 1e-06
ROPE_BASE = 1000000.0
MOMENTUM = 0.9
STEP_RATE = 0.04
GAIN_RATE = 0.005
PIECE = 128
QUERIES = 256
KEYS = 512
KEYS_BACK = 256
F32 = jnp.float32
BF16 = jnp.bfloat16
VMEM_LIMIT = 56 * 1024 * 1024


def nn(left, right):
    return lax.dot_general(left, right, (((1,), (0,)), ((), ())), preferred_element_type=F32)


def nt(left, right):
    return lax.dot_general(left, right, (((1,), (1,)), ((), ())), preferred_element_type=F32)


def tn(left, right):
    return lax.dot_general(left, right, (((0,), (0,)), ((), ())), preferred_element_type=F32)


def params(limit=VMEM_LIMIT):
    return pltpu.CompilerParams(vmem_limit_bytes=limit)


def cost(flops, moved, exps=0):
    return pl.CostEstimate(flops=int(flops / 8), bytes_accessed=int(moved / 8), transcendentals=0)


def sds(shape, dtype):
    return jax.ShapeDtypeStruct(shape, dtype)


VM = pl.BlockSpec(memory_space=pltpu.VMEM)
SM = pl.BlockSpec(memory_space=pltpu.SMEM)
ANY = pl.BlockSpec(memory_space=pl.ANY)


def flip_kv(value, bit):
    size = lax.axis_size("kv")
    return lax.ppermute(value, "kv", [(i, i ^ bit) for i in range(size)])


def flip_rep(value, bit):
    size = lax.axis_size("rep")
    return lax.ppermute(value, "rep", [(i, i ^ bit) for i in range(size)])


def after(value, *earlier):
    return lax.optimization_barrier((value, *earlier))[0]


def rounded(value):
    return lax.reduce_precision(value, exponent_bits=8, mantissa_bits=7)


def rep_bits():
    return [1 << i for i in range(lax.axis_size("rep").bit_length() - 1)]


def begin_sum(value, bit):
    if value.dtype == BF16:
        return value.astype(F32), flip_rep(value, bit)
    held = rounded(value.astype(F32))
    return held, flip_rep(held.astype(BF16), bit)


def end_sum(pair, *earlier):
    return after(pair[0], *earlier) + pair[1].astype(F32)


def xor_codes(bits):
    codes = (0,)
    for bit in bits:
        codes = codes + tuple(code ^ bit for code in codes)
    return codes


def spread(value, bits):
    for bit in bits[:-1]:
        value = jnp.concatenate([value, flip_rep(value, bit)], axis=0)
    codes = xor_codes(bits)
    middle = len(codes) // 2
    return [(value, codes[:middle]), (flip_rep(value, bits[-1]), codes[middle:])]


def gather_halves(chunk):
    replicas = lax.axis_size("rep")
    falling = [1 << i for i in range(replicas.bit_length() - 2, -1, -1)]
    rows = chunk.shape[0]
    if rows % 32 != 0:
        return [part + (0,) for part in spread(chunk, falling)]
    rising = falling[-1:] + falling[:-1]
    first = [part + (0,) for part in spread(chunk[: rows // 2], falling)]
    return first + [part + (rows // 2,) for part in spread(chunk[rows // 2 :], rising)]


def piece_copies(rep, layout, refs, target, sems):
    share = target.shape[0] // sum(len(codes) for codes, offset in layout if offset == 0)
    copies = []
    for (codes, offset), ref in zip(layout, refs):
        rows = ref.shape[0] // len(codes)
        for at, code in enumerate(codes):
            first = pl.multiple_of(lax.bitwise_xor(rep, code) * share + offset, 8)
            copies.append(
                pltpu.make_async_copy(
                    ref.at[pl.ds(at * rows, rows), :], target.at[pl.ds(first, rows), :], sems.at[len(copies)]
                )
            )
    return copies


def pack_feed(gateup, down):
    depth = down.shape[1]
    rows = gateup.shape[0]
    rest = gateup[:, depth:]
    rest = jnp.concatenate([rest[: rows // 2], rest[rows // 2 :]], axis=1)
    return jnp.concatenate([gateup[:, :depth], rest, down], axis=0)


def feed_copies(packed, gateup, down, sems):
    replicas = packed.shape[0]
    depth = down.shape[1]
    rows, low_rows = gateup.shape[0] // replicas, down.shape[0] // replicas
    half = rows // 2
    rest = gateup.shape[1] - depth
    first, second = [], []
    for at in range(replicas):
        top = at * rows
        pairs = [
            (packed.at[at, 0:rows, :], gateup.at[top : top + rows, 0:depth]),
            (packed.at[at, rows : rows + half, 0:rest], gateup.at[top : top + half, depth : depth + rest]),
            (packed.at[at, rows : rows + half, rest : 2 * rest], gateup.at[top + half : top + rows, depth : depth + rest]),
        ]
        first += [pltpu.make_async_copy(x, y, sems.at[at * 4 + i]) for i, (x, y) in enumerate(pairs)]
        second.append(
            pltpu.make_async_copy(
                packed.at[at, rows + half : rows + half + low_rows, :],
                down.at[at * low_rows : (at + 1) * low_rows, :],
                sems.at[at * 4 + 3],
            )
        )
    return first, second


def start_all(copies):
    for copy in copies:
        copy.start()


def wait_all(copies):
    for copy in copies:
        copy.wait()


def unit_of(values):
    scale = lax.rsqrt(jnp.mean(values * values, axis=-1, keepdims=True) + EPSILON)
    return values * scale, scale


def norm_back(grad, unit, scale, gain):
    weighted = grad * gain
    return scale * (weighted - unit * jnp.mean(weighted * unit, axis=-1, keepdims=True))


def forward_kernel(layout, rep, meta, tok_ref, gain_ref, head_ref, cos_ref, sin_ref, start_ref, *refs):
    pieces = refs[: len(layout)]
    hid_out, q_out, raw_out, k_out, kt_out, v_out, mixed_out, log_ref = refs[len(layout) : len(layout) + 8]
    (tok_s, w_s, hid_s, q_s, raw_s, k_s, kt_s, v_s, vt_s, mixed_s, out_acc, sum_acc) = refs[len(layout) + 8 : -3]
    in_sems, w_sems, out_sems = refs[-3:]
    heads, total, width = q_s.shape
    groups = k_s.shape[0]
    pairs = heads // groups
    blocks = total // QUERIES
    factor = math.log2(math.e) / math.sqrt(width)

    def token_copy(block):
        here = pl.ds(pl.multiple_of(block * QUERIES, QUERIES), QUERIES)
        return pltpu.make_async_copy(tok_ref.at[here, :], tok_s.at[here, :], in_sems.at[block])

    def sent(block):
        here = pl.ds(pl.multiple_of(block * QUERIES, QUERIES), QUERIES)
        pairs_of = [
            (hid_s.at[here, :], hid_out.at[here, :]),
            (q_s.at[:, here, :], q_out.at[:, here, :]),
            (raw_s.at[:, here, :], raw_out.at[:, here, :]),
            (k_s.at[:, here, :], k_out.at[:, here, :]),
            (kt_s.at[:, :, here], kt_out.at[:, :, here]),
            (v_s.at[:, here, :], v_out.at[:, here, :]),
            (mixed_s.at[here, :], mixed_out.at[here, :]),
        ]
        return [pltpu.make_async_copy(x, y, out_sems.at[i, block]) for i, (x, y) in enumerate(pairs_of)]

    weights = piece_copies(rep[0], layout, pieces, w_s, w_sems)
    token_copy(0).start()
    start_all(weights)
    for block in range(1, blocks):
        token_copy(block).start()
    log_ref[...] = jnp.zeros_like(log_ref)
    vt_s[...] = jnp.zeros_like(vt_s)
    wait_all(weights)

    @pl.loop(0, blocks)
    def _(block):
        low, count = meta[block], meta[blocks + block]
        here = pl.ds(pl.multiple_of(block * QUERIES, QUERIES), QUERIES)
        token_copy(block).wait()
        unit, _ = unit_of(tok_s[here, :].astype(F32))
        hidden = (unit * gain_ref[...]).astype(BF16)
        hid_s[here, :] = hidden
        projected = nn(hidden, w_s[...])
        cosine, sine = cos_ref[here, :], sin_ref[here, :]
        means = jnp.full((width, width), 1.0 / width, BF16)
        for index in range(heads + groups):
            one = projected[:, index * width : (index + 1) * width]
            raw_s[index, here, :] = one.astype(BF16)
            gain = head_ref[0:1, :] if index < heads else head_ref[1:2, :]
            normed = one * lax.rsqrt(nn((one * one).astype(BF16), means) + EPSILON) * gain
            turned = normed * cosine + pltpu.roll(normed, width // 2, 1) * sine
            if index < heads:
                q_s[index, here, :] = turned.astype(BF16)
            else:
                k_s[index - heads, here, :] = turned.astype(BF16)
                kt_s[index - heads, :, here] = turned.T.astype(BF16)
        for index in range(groups):
            first = (heads + groups + index) * width
            one = projected[:, first : first + width]
            v_s[index, here, :] = one.astype(BF16)
            vt_s[index, :, here] = one.T.astype(BF16)

        start = jnp.concatenate([start_ref[:, here]] * pairs, axis=1)
        place = block * QUERIES + lax.broadcasted_iota(jnp.int32, (1, QUERIES), 1)
        place = jnp.concatenate([place] * pairs, axis=1)
        queries = [
            jnp.concatenate([q_s[g * pairs + j, here, :] for j in range(pairs)], axis=0) for g in range(groups)
        ]
        out_acc[...] = jnp.zeros_like(out_acc)
        sum_acc[...] = jnp.zeros_like(sum_acc)

        @pl.loop(0, count)
        def _(turn):
            base = pl.multiple_of(low + turn * KEYS, PIECE)
            key_place = base + lax.broadcasted_iota(jnp.int32, (KEYS, 1), 0)
            allowed = (key_place >= start) & (key_place <= place)
            for g in range(groups):
                scores = nt(k_s[g, pl.ds(base, KEYS), :], queries[g])
                weights = jnp.where(allowed, jnp.exp2(scores * factor), 0.0)
                sum_acc[g] += jnp.sum(weights, axis=0, keepdims=True)
                out_acc[g] += nn(vt_s[g, :, pl.ds(base, KEYS)], weights.astype(BF16))

        for g in range(groups):
            total_weight = sum_acc[g]
            mixed = out_acc[g] / total_weight
            logs = jnp.log2(total_weight)
            for j in range(pairs):
                head = g * pairs + j
                mixed_s[here, head * width : (head + 1) * width] = mixed[:, j * QUERIES : (j + 1) * QUERIES].T.astype(BF16)
                log_ref[head : head + 1, here] = logs[:, j * QUERIES : (j + 1) * QUERIES]
        start_all(sent(block))

    @pl.loop(0, blocks)
    def _(block):
        wait_all(sent(block))


def layout_of(pieces):
    return tuple((codes, offset) for _, codes, offset in pieces), [piece for piece, _, _ in pieces]


def slots(layout):
    return sum(len(codes) for codes, _ in layout)


def forward(rep, meta, tokens, gain, head_gains, cosine, sine, doc_start, pieces, heads, groups):
    total, depth = tokens.shape
    width = head_gains.shape[1]
    cols = pieces[0][0].shape[1]
    layout, arrays = layout_of(pieces)
    wide = heads // groups * QUERIES
    blocks = total // QUERIES
    outs = [
        (total, depth),
        (heads, total, width),
        (heads + groups, total, width),
        (groups, total, width),
        (groups, width, total),
        (groups, total, width),
        (total, heads * width),
    ]
    return pl.pallas_call(
        functools.partial(forward_kernel, layout),
        in_specs=[SM, SM, ANY] + [VM] * 5 + [ANY] * len(arrays),
        out_specs=[ANY] * 7 + [VM],
        out_shape=[sds(shape, BF16) for shape in outs] + [sds((8, total), F32)],
        scratch_shapes=[pltpu.VMEM((total, depth), BF16), pltpu.VMEM((depth, cols), BF16)]
        + [pltpu.VMEM(shape, BF16) for shape in outs[:6]]
        + [
            pltpu.VMEM((groups, width, total), BF16),
            pltpu.VMEM((total, heads * width), BF16),
            pltpu.VMEM((groups, width, wide), F32),
            pltpu.VMEM((groups, 1, wide), F32),
            pltpu.SemaphoreType.DMA((blocks,)),
            pltpu.SemaphoreType.DMA((slots(layout),)),
            pltpu.SemaphoreType.DMA((7, blocks)),
        ],
        compiler_params=params(),
        cost_estimate=cost(12e9, 20e6),
        name="attention_forward",
    )(rep, meta, tokens, gain, head_gains, cosine, sine, doc_start, *arrays)


def branch_kernel(layout, rep, core, mixed_ref, *refs):
    pieces = refs[: len(layout)]
    mine_out, other_first, other_rest, w_s, mixed_s, out_s, sems, w_sems, out_sems = refs[len(layout) :]
    quarter = mixed_s.shape[1]
    loads = [
        pltpu.make_async_copy(mixed_ref.at[pl.ds(at * quarter, quarter), :], mixed_s.at[at], sems.at[at]) for at in range(4)
    ]
    weights = piece_copies(rep[0], layout, pieces, w_s, w_sems)
    start_all(weights + loads)
    wait_all(weights)
    lasts = []
    for step in range(4):
        spot = step % 2
        side = 1 - step // 2
        at = 2 * spot + lax.rem(core[0] + side, 2)
        if step == 0:
            wait_all(loads)
        out_s[step] = nn(mixed_s[at], w_s[...]).astype(BF16).reshape(out_s.shape[1:])
        if side == 0:
            sends = [(out_s.at[step], mine_out.at[:, spot], step)]
        else:
            more = out_s.shape[1] - 1
            sends = [
                (out_s.at[step, 0], other_first.at[spot], step),
                (out_s.at[step, pl.ds(1, more)], other_rest.at[:, spot], 4 + step),
            ]
        for source, target, sem in sends:
            lasts.append(pltpu.make_async_copy(source, target, out_sems.at[sem]))
            lasts[-1].start()
    wait_all(lasts)


def branch(rep, core, mixed, pieces, depth):
    total, cols = mixed.shape
    layout, arrays = layout_of(pieces)
    parts = total // 4 // PIECE
    return pl.pallas_call(
        functools.partial(branch_kernel, layout),
        in_specs=[SM, SM] + [ANY] * (1 + len(arrays)),
        out_specs=[ANY, ANY, ANY],
        out_shape=[sds((rows, 2, PIECE, depth), BF16) if rows else sds((2, PIECE, depth), BF16) for rows in (parts, 0, parts - 1)],
        scratch_shapes=[
            pltpu.VMEM((cols, depth), BF16),
            pltpu.VMEM((4, total // 4, cols), BF16),
            pltpu.VMEM((4, parts, PIECE, depth), BF16),
            pltpu.SemaphoreType.DMA((4,)),
            pltpu.SemaphoreType.DMA((slots(layout),)),
            pltpu.SemaphoreType.DMA((8,)),
        ],
        compiler_params=params(),
        cost_estimate=cost(2 * total * cols * depth, 6e6),
        name="branch",
    )(rep, core, mixed, *arrays)


def feed_kernel(part, core, gain_ref, here_ref, there_ref, tok_ref, cot_ref, packed_ref, *refs):
    mine_out, other_out, sum_ref, down_out, hid_out, act_out, dgu_out = refs[-18:-11]
    mid_s, tok_s, cot_s, wgu_s, wd_s, terms_s, down_s, hid_s, act_s, dgu_s, sems = refs[-11:]
    units = wd_s.shape[0]
    spots = [(side, spot) for side in (1, 0) for spot in range(2)]
    spare = 4 * packed_ref.shape[0]

    def natural(ref, side, spot):
        return ref.at[spot, lax.rem(core[0] + side, 2), part]

    def rows(index):
        return pl.ds(index * PIECE, PIECE)

    first, cots, lasts = [], [], []
    for index, (side, spot) in enumerate(spots):
        at = spare + 8 * index
        source = (here_ref, there_ref)[side].at[spot]
        first.append(pltpu.make_async_copy(source, mid_s.at[rows(index), :], sems.at[at]))
        first.append(pltpu.make_async_copy(natural(tok_ref, side, spot), tok_s.at[rows(index), :], sems.at[at + 1]))
        cots.append(pltpu.make_async_copy(natural(cot_ref, side, spot), cot_s.at[rows(index), :], sems.at[at + 2]))
    gateups, downs = feed_copies(packed_ref, wgu_s, wd_s, sems)
    start_all(first + gateups + cots + downs)

    def send(scratch, target_of, kind):
        for index, (side, spot) in enumerate(spots):
            lasts.append(
                pltpu.make_async_copy(
                    scratch.at[rows(index), :], target_of(side, spot), sems.at[spare + 8 * index + 3 + kind]
                )
            )
            lasts[-1].start()

    wait_all(first)
    unit, _ = unit_of(tok_s[...].astype(F32) + mid_s[...].astype(F32))
    hid_s[...] = (unit * gain_ref[...]).astype(BF16)
    send(hid_s, lambda side, spot: natural(hid_out, side, spot), 0)
    wait_all(gateups)
    both = nn(hid_s[...], wgu_s[...])
    wait_all(cots + downs)
    grad_active = nt(cot_s[...], wd_s[...])
    gate, up = both[:, :units], both[:, units:]
    sig = jax.nn.sigmoid(gate)
    lit = gate * sig
    act_s[...] = (lit * up).astype(BF16)
    send(act_s, lambda side, spot: natural(act_out, side, spot), 1)
    dgu_s[:, :units] = (grad_active * up * sig * (1.0 + gate * (1.0 - sig))).astype(BF16)
    dgu_s[:, units:] = (grad_active * lit).astype(BF16)
    send(dgu_s, lambda side, spot: natural(dgu_out, side, spot), 2)
    terms = nt(dgu_s[...], wgu_s[...])
    terms_s[...] = terms.astype(BF16)
    send(terms_s, lambda side, spot: (mine_out, other_out)[side].at[spot], 3)
    down_s[...] = nn(act_s[...], wd_s[...]).astype(BF16)
    send(down_s, lambda side, spot: natural(down_out, side, spot), 4)
    sum_ref[...] = jnp.sum(terms * unit, axis=0, keepdims=True)
    wait_all(lasts)


def feed(part, parts, core, here, there, tokens_cut, cot_cut, gain, packed, units, chain):
    depth = gain.shape[1]
    saved = (
        (2, 2, parts, PIECE, depth),
        (2, 2, parts, PIECE, depth),
        (2, 2, parts, PIECE, units),
        (2, 2, parts, PIECE, 2 * units),
    )
    rows = 4 * PIECE
    return pl.pallas_call(
        functools.partial(feed_kernel, part),
        in_specs=[SM, VM] + [ANY] * (5 + len(chain)),
        out_specs=[ANY, ANY, VM] + [ANY] * 4,
        out_shape=[sds((2, PIECE, depth), BF16)] * 2
        + [sds((1, depth), F32)]
        + [sds(shape, BF16) for shape in saved],
        scratch_shapes=[
            pltpu.VMEM((rows, depth), BF16),
            pltpu.VMEM((rows, depth), BF16),
            pltpu.VMEM((rows, depth), BF16),
            pltpu.VMEM((depth, 2 * units), BF16),
            pltpu.VMEM((units, depth), BF16),
            pltpu.VMEM((rows, depth), BF16),
            pltpu.VMEM((rows, depth), BF16),
            pltpu.VMEM((rows, depth), BF16),
            pltpu.VMEM((rows, units), BF16),
            pltpu.VMEM((rows, 2 * units), BF16),
            pltpu.SemaphoreType.DMA((4 * packed.shape[0] + 32,)),
        ],
        input_output_aliases={7 + i: 3 + i for i in range(len(chain))},
        compiler_params=params(),
        cost_estimate=cost(2 * 4 * PIECE * depth * units * 6, 12e6),
        name=f"feed_{part}",
    )(core, gain, here, there, tokens_cut, cot_cut, packed, *chain)


def backward_kernel(layout, out_layout, parts, rep, meta, mid_gain, head_ref, cos_ref, sin_ref, start_ref, log_ref, fa_ref, fo_ref, shares_ref, *refs):
    seconds, refs = refs[:parts], refs[parts:]
    (tok_ref, cot_ref, q_hbm, k_hbm, kt_hbm, v_hbm, raw_hbm, mixed_hbm) = refs[:8]
    mid_parts, grad_parts = refs[8 : 8 + 2 * parts], refs[8 + 2 * parts : 12 + 2 * parts]
    hid_hbm = refs[12 + 2 * parts]
    refs = refs[13 + 2 * parts :]
    pieces, out_pieces = refs[: len(layout)], refs[len(layout) : len(layout) + len(out_layout)]
    rest = refs[len(layout) + len(out_layout) :]
    own_ref, own_mid, gb_out, grads_out, terms_out, left_ref, gains_ref = rest[:7]
    (mid_s, grad_s, tok_s, cot_s, w_s, wo_s, q_s, k_s, kt_s, v_s, raw_s, mixed_s, hid_s, gb_s, all_s, terms_s, dk_s, dv_s, dq_acc, query_sum, key_sum, first_sum) = rest[7:-5]
    row_sems, big_sems, w_sems, wo_sems, out_sems = rest[-5:]
    heads, total, width = q_s.shape
    groups = k_s.shape[0]
    pairs = heads // groups
    blocks, cuts = total // QUERIES, total // PIECE
    per = QUERIES // PIECE
    core, half = meta[4 * blocks], meta[4 * blocks + 1]
    root = 1.0 / math.sqrt(width)
    factor = math.log2(math.e) * root

    def grad_copy(side, part, spot, cut):
        source = grad_parts[side].at[spot] if part == 0 else grad_parts[2 + side].at[2 * part - 2 + spot]
        return pltpu.make_async_copy(source, grad_s.at[pl.ds(cut * PIECE, PIECE), :], row_sems.at[1, cut])

    def row_copies(cut):
        quarter, part = cut // parts, cut % parts
        spot = quarter // 2
        here = pl.ds(cut * PIECE, PIECE)
        near = lax.rem(core + quarter, 2) == 0

        @pl.when(near)
        def _():
            pltpu.make_async_copy(mid_parts[2 * part].at[spot], mid_s.at[here, :], row_sems.at[0, cut]).start()
            grad_copy(0, part, spot, cut).start()

        @pl.when(jnp.logical_not(near))
        def _():
            pltpu.make_async_copy(mid_parts[2 * part + 1].at[spot], mid_s.at[here, :], row_sems.at[0, cut]).start()
            grad_copy(1, part, spot, cut).start()

        pltpu.make_async_copy(tok_ref.at[here, :], tok_s.at[here, :], row_sems.at[2, cut]).start()
        pltpu.make_async_copy(cot_ref.at[here, :], cot_s.at[here, :], row_sems.at[3, cut]).start()

    big = [
        pltpu.make_async_copy(x, y, big_sems.at[i])
        for i, (x, y) in enumerate(
            [
                (k_hbm, k_s), (v_hbm, v_s), (q_hbm, q_s), (kt_hbm, kt_s), (mixed_hbm, mixed_s),
                (raw_hbm, raw_s), (hid_hbm, hid_s),
            ]
        )
    ]
    weights = piece_copies(rep[0], layout, pieces, w_s, w_sems)
    out_weights = piece_copies(rep[0], out_layout, out_pieces, wo_s, wo_sems)
    for cut in range(cuts - 1, cuts - 1 - per, -1):
        row_copies(cut)
    start_all(out_weights + big + weights)
    for cut in range(cuts - 1 - per, -1, -1):
        row_copies(cut)
    dk_s[...] = jnp.zeros_like(dk_s)
    dv_s[...] = jnp.zeros_like(dv_s)
    query_sum[...] = jnp.zeros_like(query_sum)
    key_sum[...] = jnp.zeros_like(key_sum)
    first_sum[...] = jnp.zeros_like(first_sum)
    ones = jnp.ones((8, width), F32)
    query_gain, key_gain = head_ref[0:1, :], head_ref[1:2, :]
    means = jnp.full((width, width), 1.0 / width, BF16)

    def mean_of(values):
        return nn(values.astype(BF16), means)

    def head_back(grad, raw, cosine, sine, gain):
        turned = grad * cosine - pltpu.roll(grad, width // 2, 1) * sine
        scale = lax.rsqrt(mean_of(raw * raw) + EPSILON)
        unit = raw * scale
        weighted = turned * gain
        back = scale * (weighted - unit * mean_of(weighted * unit))
        return back.astype(BF16), jnp.sum(turned * unit, axis=0, keepdims=True)

    def out_copies(block):
        here = pl.ds(pl.multiple_of(block * QUERIES, QUERIES), QUERIES)
        pairs_of = [(gb_s, gb_out), (all_s, grads_out), (terms_s, terms_out)]
        return [
            pltpu.make_async_copy(x.at[here, :], y.at[here, :], out_sems.at[i, block]) for i, (x, y) in enumerate(pairs_of)
        ]

    @pl.loop(0, blocks)
    def _(turn_of):
        block = blocks - 1 - turn_of
        low, count = meta[2 * blocks + block], meta[3 * blocks + block]
        rows = pl.ds(pl.multiple_of(block * QUERIES, QUERIES), QUERIES)
        for at in range(per):
            cut = block * per + at
            here = pl.ds(pl.multiple_of(cut * PIECE, PIECE), PIECE)
            for kind, target in enumerate((mid_s, grad_s, tok_s, cot_s)):
                pltpu.make_async_copy(tok_ref.at[here, :], target.at[here, :], row_sems.at[kind, cut]).wait()
        middle = tok_s[rows, :].astype(F32) + mid_s[rows, :].astype(F32)
        unit, scale = unit_of(middle)
        result = cot_s[rows, :].astype(F32) + norm_back(grad_s[rows, :].astype(F32), unit, scale, mid_gain[...])
        low_grad = result.astype(BF16)
        gb_s[rows, :] = low_grad
        for at in range(per):
            cut = block * per + at

            @pl.when(cut // parts == 2 * half + core)
            def _():
                own_ref[lax.rem(cut, parts)] = result[at * PIECE : (at + 1) * PIECE]
                own_mid[lax.rem(cut, parts)] = middle[at * PIECE : (at + 1) * PIECE]

        @pl.when(turn_of == 0)
        def _():
            wait_all(out_weights + big)

        grad_mixed = nt(low_grad, wo_s[...]).astype(BF16)
        mixed = mixed_s[rows, :]
        start = jnp.concatenate([start_ref[:, rows]] * pairs, axis=1)
        place = block * QUERIES + lax.broadcasted_iota(jnp.int32, (1, QUERIES), 1)
        place = jnp.concatenate([place] * pairs, axis=1)
        queries, grads, logs, deltas = [], [], [], []
        for g in range(groups):
            members = range(g * pairs, (g + 1) * pairs)
            queries.append(jnp.concatenate([q_s[h, rows, :] for h in members], axis=0))
            grad = jnp.concatenate([grad_mixed[:, h * width : (h + 1) * width] for h in members], axis=0)
            out = jnp.concatenate([mixed[:, h * width : (h + 1) * width] for h in members], axis=0)
            grads.append(grad)
            logs.append(jnp.concatenate([log_ref[h : h + 1, rows] for h in members], axis=1))
            terms = lax.dot_general(
                ones,
                grad.astype(F32) * out.astype(F32),
                (((1,), (1,)), ((), ())),
                precision=lax.Precision.HIGHEST,
                preferred_element_type=F32,
            )
            deltas.append(terms[0:1, :])
        dq_acc[...] = jnp.zeros_like(dq_acc)

        @pl.loop(0, count)
        def _(turn):
            base = pl.multiple_of(low + turn * KEYS_BACK, PIECE)
            key_place = base + lax.broadcasted_iota(jnp.int32, (KEYS_BACK, 1), 0)
            allowed = (key_place >= start) & (key_place <= place)
            keys = pl.ds(base, KEYS_BACK)
            for g in range(groups):
                scores = nt(k_s[g, keys, :], queries[g])
                weights = jnp.where(allowed, jnp.exp2(scores * factor - logs[g]), 0.0)
                grad_weights = nt(v_s[g, keys, :], grads[g])
                grad_scores = (weights * (grad_weights - deltas[g])).astype(BF16)
                dv_s[g, keys, :] += nn(weights.astype(BF16), grads[g])
                dk_s[g, keys, :] += nn(grad_scores, queries[g])
                dq_acc[g] += nn(kt_s[g, :, keys], grad_scores)

        cosine, sine = cos_ref[rows, :], sin_ref[rows, :]
        sums = jnp.zeros((1, width), F32)
        columns = []
        for head in range(heads):
            j = head % pairs
            grad = dq_acc[head // pairs, :, j * QUERIES : (j + 1) * QUERIES].T * root
            back, part_sum = head_back(grad, raw_s[head, rows, :].astype(F32), cosine, sine, query_gain)
            columns.append(back)
            sums = sums + part_sum
        query_sum[...] += sums
        sums = jnp.zeros((1, width), F32)
        for g in range(groups):
            back, part_sum = head_back(
                dk_s[g, rows, :] * root, raw_s[heads + g, rows, :].astype(F32), cosine, sine, key_gain
            )
            columns.append(back)
            sums = sums + part_sum
        key_sum[...] += sums
        for g in range(groups):
            columns.append(dv_s[g, rows, :].astype(BF16))
        everything = jnp.concatenate(columns, axis=1)
        all_s[rows, :] = everything

        @pl.when(turn_of == 0)
        def _():
            wait_all(weights)

        terms = nt(everything, w_s[...])
        first_sum[...] += jnp.sum(terms * unit_of(tok_s[rows, :].astype(F32))[0], axis=0, keepdims=True)
        terms_s[rows, :] = terms.astype(BF16)
        start_all(out_copies(block))

    all_left = tn(nn(all_s[...], fa_ref[...]).astype(BF16), hid_s[...])
    out_left = tn(nn(gb_s[...], fo_ref[...]).astype(BF16), mixed_s[...])
    ranks, depth = left_ref.shape[0], first_sum.shape[1]
    for at in range(3):
        cols = slice(at * depth, (at + 1) * depth)
        left_ref[:, cols] = (all_left[at * ranks : (at + 1) * ranks, :] + shares_ref[:, cols]).astype(BF16)
    left_ref[:, 3 * depth :] = (out_left[:ranks, :] + shares_ref[:, 3 * depth :]).astype(BF16)
    second = sum(one[...] for one in seconds[1:]) + seconds[0][...]
    gains_ref[...] = jnp.zeros_like(gains_ref)
    wide = depth // 4
    for at in range(4):
        gains_ref[at : at + 1, :wide] = first_sum[:, at * wide : (at + 1) * wide]
        gains_ref[4 + at : 5 + at, :wide] = second[:, at * wide : (at + 1) * wide]
    gains_ref[0:1, wide : wide + width] = query_sum[...]
    gains_ref[1:2, wide : wide + width] = key_sum[...]

    @pl.loop(0, blocks)
    def _(block):
        wait_all(out_copies(block))


def backward(
    rep, meta, gain, head_gains, cosine, sine, doc_start, logs, tokens, cotangent, q_rot, k_rot, k_turned, v_heads, raw,
    mixed, hidden, fa, fo, shares, seconds, mids, grads, pieces, out_pieces
):
    heads, total, width = q_rot.shape
    groups = k_rot.shape[0]
    depth = tokens.shape[1]
    cols = pieces[0][0].shape[1]
    parts = len(mids)
    blocks = total // QUERIES
    layout, arrays = layout_of(pieces)
    out_layout, out_arrays = layout_of(out_pieces)
    flat = [one for pair in mids + grads for one in pair]
    big = (tokens, cotangent, q_rot, k_rot, k_turned, v_heads, raw, mixed)
    rows = pltpu.VMEM((total, depth), BF16)
    return pl.pallas_call(
        functools.partial(backward_kernel, layout, out_layout, parts),
        in_specs=[SM, SM] + [VM] * (9 + parts) + [ANY] * (1 + len(big) + len(flat) + len(arrays) + len(out_arrays)),
        out_specs=[VM, VM, ANY, ANY, ANY, VM, VM],
        out_shape=[
            sds((parts, PIECE, depth), F32),
            sds((parts, PIECE, depth), F32),
            sds((total, depth), BF16),
            sds((total, cols), BF16),
            sds((total, depth), BF16),
            sds(shares.shape, BF16),
            sds((8, depth // 4 + width), F32),
        ],
        scratch_shapes=[rows, rows, rows, rows, pltpu.VMEM((depth, cols), BF16), pltpu.VMEM((heads * width, depth), BF16)]
        + [pltpu.VMEM(one.shape, BF16) for one in (q_rot, k_rot, k_turned, v_heads, raw, mixed, hidden)]
        + [
            rows,
            pltpu.VMEM((total, cols), BF16),
            rows,
            pltpu.VMEM((groups, total, width), F32),
            pltpu.VMEM((groups, total, width), F32),
            pltpu.VMEM((groups, width, heads // groups * QUERIES), F32),
            pltpu.VMEM((1, width), F32),
            pltpu.VMEM((1, width), F32),
            pltpu.VMEM((1, depth), F32),
            pltpu.SemaphoreType.DMA((4, total // PIECE)),
            pltpu.SemaphoreType.DMA((7,)),
            pltpu.SemaphoreType.DMA((slots(layout),)),
            pltpu.SemaphoreType.DMA((slots(out_layout),)),
            pltpu.SemaphoreType.DMA((3, blocks)),
        ],
        compiler_params=params(),
        cost_estimate=cost(20e9, 30e6),
        name="attention_backward",
    )(rep, meta, gain, head_gains, cosine, sine, doc_start, logs, fa, fo, shares, *seconds, *big, *flat, hidden, *arrays, *out_arrays)


def shares_kernel(count, *refs):
    errors, starts, out_ref = refs[:count], refs[count:-1], refs[-1]
    blocks = []
    for error in errors:
        blocks += [error[at] for at in range(error.shape[0])] if len(error.shape) == 3 else [error[...]]
    first = 0
    for block, start in zip(blocks, starts):
        high = start[...].astype(BF16)
        low = (start[...] - high.astype(F32)).astype(BF16)
        both = nt(jnp.concatenate([high, low], axis=0), block.astype(BF16))
        ranks, rows = start.shape[0], block.shape[0]
        out_ref[:, first : first + rows] = both[:ranks] + both[ranks:]
        first += rows


def shares_of(errors, starts, rows):
    return pl.pallas_call(
        functools.partial(shares_kernel, len(errors)),
        in_specs=[VM] * (len(errors) + len(starts)),
        out_specs=VM,
        out_shape=sds((starts[0].shape[0], rows), F32),
        compiler_params=params(),
        cost_estimate=cost(1e9, 16e6),
        name="error_shares",
    )(*errors, *starts)


def feed_moment_kernel(steps, hid_ref, dgu_ref, gu_error, act_ref, cot_ref, d_error, gu_start, d_start, *outs):
    gu_out, d_out, gu_left, d_left = outs
    units = gu_out.shape[2]
    step = pl.program_id(0)

    def left_of(start, moment):
        both = nt(jnp.concatenate(two_parts(start), axis=0), moment.astype(BF16))
        ranks = start.shape[0]
        return both[:ranks] + both[ranks:]

    @pl.when(step < steps)
    def _():
        both = tn(hid_ref[...], dgu_ref[...])
        for at in range(2):
            moment = both[:, at * units : (at + 1) * units] + gu_error[at]
            gu_out[at] = moment
            gu_left[at] = left_of(gu_start[at], moment)

    @pl.when(step >= steps)
    def _():
        moment = tn(act_ref[...], cot_ref[...]) + d_error[...]
        d_out[...] = moment
        d_left[...] = left_of(d_start[...], moment)


def feed_moments(hidden, grads, gu_error, active, cotangent, d_error, gu_start, d_start):
    total, depth = hidden.shape
    units = active.shape[1]
    ranks = d_start.shape[0]
    rows, low_rows = 512, 384
    steps, more = depth // rows, units // low_rows
    early = lambda i: jnp.minimum(i, steps - 1)
    late = lambda i: jnp.maximum(i - steps, 0)
    return pl.pallas_call(
        functools.partial(feed_moment_kernel, steps),
        grid=(steps + more,),
        in_specs=[
            pl.BlockSpec((total, rows), lambda i: (0, early(i))),
            pl.BlockSpec((total, 2 * units), lambda i: (0, 0)),
            pl.BlockSpec((2, rows, units), lambda i: (0, early(i), 0)),
            pl.BlockSpec((total, low_rows), lambda i: (0, late(i))),
            pl.BlockSpec((total, depth), lambda i: (0, 0)),
            pl.BlockSpec((low_rows, depth), lambda i: (late(i), 0)),
            pl.BlockSpec((2, ranks, units), lambda i: (0, 0, 0)),
            pl.BlockSpec((ranks, depth), lambda i: (0, 0)),
        ],
        out_specs=[
            pl.BlockSpec((2, rows, units), lambda i: (0, early(i), 0)),
            pl.BlockSpec((low_rows, depth), lambda i: (late(i), 0)),
            pl.BlockSpec((2, ranks, rows), lambda i: (0, 0, early(i))),
            pl.BlockSpec((ranks, low_rows), lambda i: (0, late(i))),
        ],
        out_shape=[
            sds(gu_error.shape, F32),
            sds(d_error.shape, F32),
            sds((2, ranks, depth), F32),
            sds((ranks, units), F32),
        ],
        compiler_params=params(),
        cost_estimate=cost(1, 1),
        name="feed_moments",
    )(hidden, grads, gu_error, active, cotangent, d_error, gu_start, d_start)


def orthonormal_panel(panel):
    ranks = panel.shape[0]
    index = lax.broadcasted_iota(jnp.int32, (ranks, 1), 0)
    for at in range(ranks):
        column = panel[at : at + 1, :]
        column = column * lax.rsqrt(jnp.sum(column * column, axis=1, keepdims=True) + EPSILON)
        dots = jnp.sum(panel * column, axis=1, keepdims=True)
        later = panel - dots * column
        panel = jnp.where(index > at, later, jnp.where(index == at, column, panel))
    return panel


def two_parts(value):
    high = value.astype(BF16)
    return high, (value - high.astype(F32)).astype(BF16)


def panels_of(refs):
    views = []
    for ref in refs:
        views += [ref.at[0], ref.at[1]] if len(ref.shape) == 3 else [ref]
    return views


def factors_kernel(count, kinds, lefts_ref, *refs):
    moments, lefts_out, rights_ref = refs[:count], refs[count : count + kinds], refs[count + kinds]
    held, sems = refs[count + kinds + 1 : -1], refs[-1]
    copies = [pltpu.make_async_copy(x, y, sems.at[i]) for i, (x, y) in enumerate(zip(panels_of(moments), panels_of(held)))]
    start_all(copies)
    done = []
    first = 0
    for source, target in zip(panels_of(held), panels_of(lefts_out)):
        rows = source.shape[0]
        done.append(orthonormal_panel(lefts_ref[:, first : first + rows]))
        target[...] = done[-1]
        first += rows
    first = 0
    for panel, source, copy in zip(done, panels_of(held), copies):
        ranks, cols = panel.shape[0], source.shape[1]
        both = jnp.concatenate(two_parts(panel), axis=0)
        copy.wait()
        result = nn(both, source[...].astype(BF16))
        rights_ref[:, first : first + cols] = (result[:ranks] + result[ranks:]).astype(BF16)
        first += cols


def make_factors(label, lefts, moments, shapes, cols):
    ranks = lefts.shape[0]
    return pl.pallas_call(
        functools.partial(factors_kernel, len(moments), len(shapes)),
        in_specs=[VM] + [ANY] * len(moments),
        out_specs=[VM] * (len(shapes) + 1),
        out_shape=[sds(shape, F32) for shape in shapes] + [sds((ranks, cols), BF16)],
        scratch_shapes=[pltpu.VMEM(one.shape, F32) for one in moments] + [pltpu.SemaphoreType.DMA((4,))],
        compiler_params=params(),
        cost_estimate=cost(1, 1),
        name=f"factors_{label}",
    )(lefts, *moments)


def settle_kernel(replicas, count, kinds, gained, rep, summed_ref, *refs):
    gains, refs = refs[: 4 * gained], refs[4 * gained :]
    lefts, refs = panels_of(refs[:kinds]), refs[kinds:]
    moments, refs = refs[:count], refs[count:]
    weights, velocities, outs = refs[:kinds], refs[kinds : 2 * kinds], refs[2 * kinds :]
    rights_out, outs = outs[:kinds], outs[kinds:]
    gains_out, outs = outs[: 4 * gained], outs[4 * gained :]
    errors_out, weights_out, velocities_out = outs[:kinds], outs[kinds : 2 * kinds], outs[2 * kinds : 3 * kinds]
    scratch = outs[3 * kinds :]
    held, approx = scratch[:count], scratch[count : 2 * count]
    weights_s, velocities_s = scratch[2 * count : 2 * count + kinds], scratch[2 * count + kinds : 2 * count + 2 * kinds]
    in_sems, small_sems, out_sems, last_sems = scratch[-4:]
    copies = [
        pltpu.make_async_copy(x, y, in_sems.at[i]) for i, (x, y) in enumerate(zip(panels_of(moments), panels_of(held)))
    ]
    small = [
        pltpu.make_async_copy(x, y, small_sems.at[i])
        for i, (x, y) in enumerate(zip(weights + velocities, weights_s + velocities_s))
    ]
    start_all(copies + small)
    if gained:
        bg_ref, bv_ref, hg_ref, hv_ref = gains
        wide = bg_ref.shape[1] // 4
        width = hg_ref.shape[1]
        base = summed_ref.shape[1] - wide - width
        for row in range(2):
            for at in range(4):
                cols = slice(at * wide, (at + 1) * wide)
                mean = summed_ref[4 * row + at : 4 * row + at + 1, base : base + wide] / replicas
                velocity = MOMENTUM * bv_ref[row : row + 1, cols] + mean
                gains_out[1][row : row + 1, cols] = velocity
                gains_out[0][row : row + 1, cols] = bg_ref[row : row + 1, cols] - GAIN_RATE * velocity
            mean = summed_ref[row : row + 1, base + wide : base + wide + width] / replicas
            velocity = MOMENTUM * hv_ref[row : row + 1, :] + mean
            gains_out[3][row : row + 1, :] = velocity
            gains_out[2][row : row + 1, :] = hg_ref[row : row + 1, :] - GAIN_RATE * velocity

    first = 0
    lasts = []
    everything = zip(lefts, panels_of(rights_out), panels_of(held), panels_of(approx), copies, panels_of(errors_out))
    for index, (left, right_out, moment, product, copy, target) in enumerate(everything):
        cols = moment.shape[1]
        right = summed_ref[:, first : first + cols] / replicas
        first += cols
        right_out[...] = right
        left_high, left_low = two_parts(left[...])
        right_high, right_low = two_parts(right)
        product[...] = tn(
            jnp.concatenate([left_high, left_low, left_high, left_low], axis=0),
            jnp.concatenate([right_high, right_high, right_low, right_low], axis=0),
        )
        copy.wait()
        moment[...] = moment[...] - product[...]
        lasts.append(pltpu.make_async_copy(moment, target, out_sems.at[index]))
        lasts[-1].start()
    wait_all(small)
    updates = zip(panels_of(approx), panels_of(weights_s), panels_of(velocities_s))
    for product, weight, velocity in updates:
        rows = weight.shape[0]
        mine = product[pl.ds(pl.multiple_of(rep[0] * rows, 8), rows), :]
        fresh = MOMENTUM * velocity[...] + mine
        velocity[...] = fresh
        weight[...] = weight[...] - STEP_RATE * fresh
    moves = zip(weights_s + velocities_s, weights_out + velocities_out)
    for index, (source, target) in enumerate(moves):
        lasts.append(pltpu.make_async_copy(source, target, last_sems.at[index]))
        lasts[-1].start()
    wait_all(lasts)


def settle(label, replicas, rep, summed, gains, lefts, moments, weights, velocities, rights, errors):
    small = [sds(one.shape, F32) for one in weights + velocities]
    kinds = len(lefts)
    outs = kinds + len(gains)
    results = pl.pallas_call(
        functools.partial(settle_kernel, replicas, len(moments), kinds, len(gains) // 4),
        in_specs=[SM] + [VM] * (1 + len(gains) + kinds) + [ANY] * (len(moments) + 2 * kinds),
        out_specs=[VM] * outs + [ANY] * (3 * kinds),
        out_shape=[sds(shape, F32) for shape in rights]
        + [sds(one.shape, F32) for one in gains]
        + [sds(shape, F32) for shape in errors]
        + small,
        scratch_shapes=[pltpu.VMEM(one.shape, F32) for one in moments + moments + weights + velocities]
        + [pltpu.SemaphoreType.DMA((2 * kinds,))] * 4,
        compiler_params=params(),
        cost_estimate=cost(1, 1),
        name=f"settle_{label}",
    )(rep, summed, *gains, *lefts, *moments, *weights, *velocities)
    rows = [results[outs + at * kinds : outs + (at + 1) * kinds] for at in range(3)]
    return results[:kinds], results[kinds:outs], rows


def on_device(
    tokens,
    cotangent,
    lengths,
    block_gains,
    block_velocity,
    head_gains,
    head_velocity,
    weight_query,
    velocity_query,
    error_query,
    factor_query,
    weight_keyval,
    velocity_keyval,
    error_keyval,
    factor_keyval,
    weight_out,
    velocity_out,
    error_out,
    factor_out,
    weight_gateup,
    velocity_gateup,
    error_gateup,
    factor_gateup,
    weight_down,
    velocity_down,
    error_down,
    factor_down,
):
    total, depth = tokens.shape
    width = head_gains.shape[1]
    heads = weight_query.shape[1] // width
    groups = weight_keyval.shape[2] // width
    units = weight_gateup.shape[2]
    quarter = total // 4
    parts = quarter // PIECE
    blocks = total // PIECE
    replicas = lax.axis_size("rep")
    rep_index = lax.axis_index("rep")
    kv_index = lax.axis_index("kv")
    core = lax.rem(kv_index, 2)
    half = kv_index // 2
    rep = rep_index[None].astype(jnp.int32)
    core_at = core[None].astype(jnp.int32)

    pieces_qkv = gather_halves(
        jnp.concatenate([weight_query, weight_keyval[0], weight_keyval[1]], axis=1).astype(BF16)
    )
    pieces_out = gather_halves(weight_out.astype(BF16))
    packed = pack_feed(
        jnp.concatenate([weight_gateup[0], weight_gateup[1]], axis=1).astype(BF16), weight_down.astype(BF16)
    )
    packed = lax.all_gather(packed, "rep", axis=0)

    own_lengths = lengths[0]
    docs = own_lengths.shape[0]
    before = jnp.arange(docs)[:, None] >= jnp.arange(docs)[None, :]
    ends = jnp.sum(jnp.where(before, own_lengths[None, :], 0), axis=1)
    places = jnp.arange(total, dtype=jnp.int32)
    passed = places[None, :] >= ends[:, None]
    doc_start = jnp.sum(jnp.where(passed, own_lengths[:, None], 0), axis=0, keepdims=True).astype(jnp.int32)
    position = (places[None, :] - doc_start)[0]
    meta = []
    for rows, keys in ((QUERIES, KEYS), (QUERIES, KEYS_BACK)):
        block_ends = (jnp.arange(total // rows, dtype=jnp.int32) + 1) * rows
        turns = (block_ends - doc_start[0, ::rows] + keys - 1) // keys
        meta += [jnp.maximum(block_ends - turns * keys, 0), turns]
    meta = jnp.concatenate(meta + [core[None], half[None]]).astype(jnp.int32)

    half_index = jnp.arange(width // 2, dtype=F32)
    frequency = ROPE_BASE ** (-2.0 * half_index / width)
    angles = position.astype(F32)[:, None] * frequency[None, :]
    cosine, sine = jnp.cos(angles), jnp.sin(angles)
    cosine = jnp.concatenate([cosine, cosine], axis=1)
    sine = jnp.concatenate([-sine, sine], axis=1)

    tokens_cut = tokens.reshape(2, 2, parts, PIECE, depth)
    cot_cut = cotangent.reshape(2, 2, parts, PIECE, depth)

    def chip_sum(mine, theirs):
        return (mine.astype(F32) + theirs.astype(F32)).astype(BF16)

    def cross_sum(own, *earlier):
        theirs = flip_kv(own, 2)
        summed = (after(own, *earlier).astype(F32) + theirs.astype(F32)).astype(BF16)
        return summed, flip_kv(summed, 1)

    factors = [one.T for one in (factor_query, factor_keyval[0], factor_keyval[1], factor_out[0])]
    tied = (error_query[0], error_keyval[0], error_out[0])
    tied = lax.optimization_barrier((*tied, pieces_qkv[0][0], pieces_qkv[2 % len(pieces_qkv)][0]))[:3]
    query_rows, group_cols = heads * width, groups * width
    shares = shares_of(tied, factors, 3 * depth + query_rows)
    doc_start = after(doc_start, shares)
    ranks = factor_query.shape[1]

    def laid(parts_of):
        rows = []
        for at, one in enumerate(parts_of):
            pads = (at * ranks, 128 - (at + 1) * ranks)
            rows.append(jnp.pad(one.T, ((0, 0), pads)))
        return jnp.concatenate(rows, axis=0).astype(BF16)

    laid_attn, laid_out = laid(factors[:3]), laid(factors[3:4])
    doc_start = after(doc_start, laid_attn, laid_out)

    hidden_first, q_rot, raw, k_rot, k_turned, v_heads, mixed, logs = forward(
        rep, meta, tokens, block_gains[0:1], head_gains, cosine, sine, doc_start, pieces_qkv, heads, groups
    )
    mine, other, later = branch(rep, core_at, mixed, pieces_out, depth)
    owns = [chip_sum(mine[0], flip_kv(other, 1))]
    theirs = flip_kv(after(later, owns[0]), 1)
    owns += [chip_sum(mine[p + 1], theirs[p]) for p in range(parts - 1)]

    mids, chain, terms_parts, second_parts, term_owns = [], [], [], [], []
    earlier = ()
    for part in range(parts):
        mids.append(cross_sum(owns[part], *earlier))
        here = mids[part][0]
        if part >= 2:
            mine, theirs = terms_parts[part - 2]
            term_owns.append(chip_sum(mine, after(theirs, terms_parts[part - 1][0])))
            here = after(here, term_owns[-1])
        mine, other, second, *chain = feed(
            part, parts, core_at, here, mids[part][1], tokens_cut, cot_cut, block_gains[1:2],
            packed, units, chain,
        )
        earlier = (mine,)
        terms_parts.append((mine, flip_kv(other, 1)))
        second_parts.append(second)
    down_terms = chain[0].reshape(total, depth)

    down_terms = chain[0].reshape(total, depth)
    last = terms_parts[parts - 1][0]
    bits = rep_bits()
    grads = [cross_sum(term_owns[0], last)]
    term_owns.append(chip_sum(terms_parts[1][0], after(terms_parts[1][1], grads[0][0])))
    term_owns.append(chip_sum(terms_parts[2][0], after(terms_parts[2][1], term_owns[1])))
    both_owns = jnp.concatenate(term_owns[1:], axis=0)
    *chain, _ = lax.optimization_barrier((*chain[1:], both_owns))
    hid_full, act_full, dgu_full = [one.reshape(total, -1) for one in chain]
    moment_gateup, moment_down, gu_left, d_left = feed_moments(
        hid_full, dgu_full, error_gateup[0], act_full, cotangent, error_down[0], jnp.swapaxes(factor_gateup, 1, 2),
        factor_down[0].T,
    )
    feed_lefts = jnp.concatenate([gu_left[0], gu_left[1], d_left], axis=1)
    pending = begin_sum(feed_lefts, bits[0])
    grads.append(cross_sum(both_owns, moment_down))
    feed_lefts = end_sum(pending, grads[1][0])
    pending = begin_sum(feed_lefts, bits[1])
    feed_own = lax.psum_scatter(after(down_terms, grads[1][0]), "kv", scatter_dimension=0, tiled=True)

    own_grad, own_middle, gb_full, grads_qkv, input_terms, attn_lefts, gains = backward(
        rep, meta, block_gains[1:2], head_gains, cosine, sine, doc_start, logs, tokens, cotangent, q_rot, k_rot,
        k_turned, v_heads, raw, mixed, hidden_first, laid_attn, laid_out, shares, second_parts, mids, grads, pieces_qkv,
        pieces_out,
    )

    attn_lefts = after(attn_lefts, feed_own)
    feed_lefts = end_sum(pending, own_grad)
    pending, feed_pending = begin_sum(attn_lefts, bits[0]), begin_sum(feed_lefts, bits[2])
    grads_qkv = after(grads_qkv, attn_lefts, feed_lefts)
    moment_query = tn(hidden_first, grads_qkv[:, :query_rows]) + error_query[0]
    gains = gains + flip_kv(gains, 1)
    attn_lefts, feed_lefts = end_sum(pending, moment_query), end_sum(feed_pending, moment_query)
    for bit in bits[3:]:
        feed_lefts = end_sum(begin_sum(feed_lefts, bit))
    pending = begin_sum(attn_lefts, bits[1])
    *left_feed, right_feed = make_factors(
        "feed", after(feed_lefts, attn_lefts), [moment_gateup, moment_down],
        [(2, ranks, depth), (ranks, units)], 2 * units + depth,
    )
    gains = gains + flip_kv(gains, 2)
    attn_lefts = end_sum(pending, right_feed)
    pending, feed_pending = begin_sum(attn_lefts, bits[2]), begin_sum(right_feed, bits[0])
    moment_out = tn(mixed, after(gb_full, attn_lefts, right_feed)) + error_out[0]
    attn_lefts, right_feed = end_sum(pending, moment_out), end_sum(feed_pending, moment_out)
    feed_pending = begin_sum(right_feed, bits[1])
    for bit in bits[3:]:
        attn_lefts = end_sum(begin_sum(attn_lefts, bit))
    grads_qkv = after(grads_qkv, attn_lefts, right_feed)
    moment_key = tn(hidden_first, grads_qkv[:, query_rows : query_rows + group_cols]) + error_keyval[0, 0]
    moment_value = tn(hidden_first, grads_qkv[:, query_rows + group_cols :]) + error_keyval[0, 1]
    right_feed = end_sum(feed_pending, moment_key, moment_value)
    feed_pending = begin_sum(right_feed, bits[2])
    attn_moments = [moment_query, moment_key, moment_value, moment_out]
    *left_attn, right_attn = make_factors(
        "attn", after(attn_lefts, right_feed), attn_moments,
        [(ranks, depth), (2, ranks, depth), (ranks, query_rows)], query_rows + 2 * group_cols + depth,
    )
    right_feed = end_sum(feed_pending, right_attn)
    for bit in bits[3:]:
        right_feed = end_sum(begin_sum(right_feed, bit))
    summed = jnp.concatenate([right_attn, gains.astype(BF16)], axis=1)
    pending = begin_sum(summed, bits[0])
    feed_rights, _, feed_rest = settle(
        "feed", replicas, rep, after(right_feed, right_attn), [], left_feed, [moment_gateup, moment_down],
        [weight_gateup, weight_down], [velocity_gateup, velocity_down],
        [(2, ranks, units), (ranks, depth)], [moment_gateup.shape, moment_down.shape],
    )
    summed = end_sum(pending, feed_rights[1])
    pending = begin_sum(summed, bits[1])

    grad_first = lax.psum_scatter(input_terms, "kv", scatter_dimension=0, tiled=True)
    own_middle, own_grad, feed_own, _ = lax.optimization_barrier((own_middle, own_grad, feed_own, summed))
    layer_out = (own_middle.reshape(quarter, depth) + feed_own.astype(F32)).astype(BF16)
    summed = end_sum(pending, layer_out)
    pending = begin_sum(summed, bits[2])
    own_tokens = lax.dynamic_slice_in_dim(tokens, kv_index * quarter, quarter, 0).astype(F32)
    unit, scale = unit_of(own_tokens)
    grad_first = after(grad_first, summed).astype(F32)
    input_grad = own_grad.reshape(quarter, depth) + norm_back(grad_first, unit, scale, block_gains[0])
    summed = end_sum(pending, input_grad)
    for bit in bits[3:]:
        summed = end_sum(begin_sum(summed, bit))
    attn_rights, gains, attn_rest = settle(
        "attn", replicas, rep, summed, [block_gains, block_velocity, head_gains, head_velocity], left_attn, attn_moments,
        [weight_query, weight_keyval, weight_out], [velocity_query, velocity_keyval, velocity_out],
        [(ranks, query_rows), (2, ranks, group_cols), (ranks, depth)],
        [moment_query.shape, (2,) + moment_key.shape, moment_out.shape],
    )

    def turned_over(value):
        return jnp.swapaxes(value, -1, -2)

    def five(rest, at, left, right):
        errors, weights, velocities = rest
        return [weights[at], velocities[at], errors[at][None], turned_over(left), turned_over(right)]

    outputs = [layer_out, input_grad, *gains]
    outputs += five(attn_rest, 0, left_attn[0][None], attn_rights[0])
    outputs += five(attn_rest, 1, left_attn[1][:, None], attn_rights[1])
    outputs += five(attn_rest, 2, left_attn[2], attn_rights[2][None])
    outputs += five(feed_rest, 0, left_feed[0][:, None], feed_rights[0])
    outputs += five(feed_rest, 1, left_feed[1], feed_rights[1][None])
    return tuple(outputs)


def solution(mesh):
    placed = (
        P("rep", None),
        P("rep", None),
        P("rep", None),
        P(),
        P(),
        P(),
        P(),
        P("rep", "kv"),
        P("rep", "kv"),
        P("rep", None, "kv"),
        P("kv", None),
        P(None, "rep", "kv"),
        P(None, "rep", "kv"),
        P("rep", None, None, "kv"),
        P(None, "kv", None),
        P(("kv", "rep"), None),
        P(("kv", "rep"), None),
        P("rep", "kv", None),
        P("kv", None, None),
        P(None, "rep", "kv"),
        P(None, "rep", "kv"),
        P("rep", None, None, "kv"),
        P(None, "kv", None),
        P(("kv", "rep"), None),
        P(("kv", "rep"), None),
        P("rep", "kv", None),
        P("kv", None, None),
    )
    return jax.shard_map(
        on_device,
        mesh=mesh,
        in_specs=placed,
        out_specs=(
            P(("rep", "kv"), None),
            P(("rep", "kv"), None),
            P(),
            P(),
            P(),
            P(),
            P("rep", "kv"),
            P("rep", "kv"),
            P("rep", None, "kv"),
            P("kv", None, None),
            P("kv", None),
            P(None, "rep", "kv"),
            P(None, "rep", "kv"),
            P("rep", None, None, "kv"),
            P(None, "kv", None, None),
            P(None, "kv", None),
            P(("kv", "rep"), None),
            P(("kv", "rep"), None),
            P("rep", "kv", None),
            P("kv", None),
            P("kv", None, None),
            P(None, "rep", "kv"),
            P(None, "rep", "kv"),
            P("rep", None, None, "kv"),
            P(None, "kv", None, None),
            P(None, "kv", None),
            P(("kv", "rep"), None),
            P(("kv", "rep"), None),
            P("rep", "kv", None),
            P("kv", None),
            P("kv", None, None),
        ),
        check_vma=False,
    )
```

```python
import functools
import math

import jax
import jax.numpy as jnp
from jax import lax
from jax.experimental import pallas as pl
from jax.experimental.pallas import tpu as pltpu
from jax.sharding import PartitionSpec as P

EPSILON = 1e-06
ROPE_BASE = 1000000.0
MOMENTUM = 0.9
STEP_RATE = 0.04
GAIN_RATE = 0.005
PIECE = 128
QUERIES = 256
KEYS = 512
KEYS_BACK = 256
F32 = jnp.float32
BF16 = jnp.bfloat16
VMEM_LIMIT = 56 * 1024 * 1024


def nn(left, right):
    return lax.dot_general(left, right, (((1,), (0,)), ((), ())), preferred_element_type=F32)


def nt(left, right):
    return lax.dot_general(left, right, (((1,), (1,)), ((), ())), preferred_element_type=F32)


def tn(left, right):
    return lax.dot_general(left, right, (((0,), (0,)), ((), ())), preferred_element_type=F32)


def params(limit=VMEM_LIMIT):
    return pltpu.CompilerParams(vmem_limit_bytes=limit)


def cost(flops, moved, exps=0):
    return pl.CostEstimate(flops=int(flops / 8), bytes_accessed=int(moved / 8), transcendentals=0)


def sds(shape, dtype):
    return jax.ShapeDtypeStruct(shape, dtype)


VM = pl.BlockSpec(memory_space=pltpu.VMEM)
SM = pl.BlockSpec(memory_space=pltpu.SMEM)
ANY = pl.BlockSpec(memory_space=pl.ANY)


def flip_kv(value, bit):
    size = lax.axis_size("kv")
    return lax.ppermute(value, "kv", [(i, i ^ bit) for i in range(size)])


def flip_rep(value, bit):
    size = lax.axis_size("rep")
    return lax.ppermute(value, "rep", [(i, i ^ bit) for i in range(size)])


def after(value, *earlier):
    return lax.optimization_barrier((value, *earlier))[0]


def rounded(value):
    return lax.reduce_precision(value, exponent_bits=8, mantissa_bits=7)


def rep_bits():
    return [1 << i for i in range(lax.axis_size("rep").bit_length() - 1)]


def begin_sum(value, bit):
    if value.dtype == BF16:
        return value.astype(F32), flip_rep(value, bit)
    held = rounded(value.astype(F32))
    return held, flip_rep(held.astype(BF16), bit)


def end_sum(pair, *earlier):
    return after(pair[0], *earlier) + pair[1].astype(F32)


def xor_codes(bits):
    codes = (0,)
    for bit in bits:
        codes = codes + tuple(code ^ bit for code in codes)
    return codes


def spread(value, bits):
    for bit in bits[:-1]:
        value = jnp.concatenate([value, flip_rep(value, bit)], axis=0)
    codes = xor_codes(bits)
    middle = len(codes) // 2
    return [(value, codes[:middle]), (flip_rep(value, bits[-1]), codes[middle:])]


def gather_halves(chunk):
    replicas = lax.axis_size("rep")
    falling = [1 << i for i in range(replicas.bit_length() - 2, -1, -1)]
    rows = chunk.shape[0]
    if rows % 32 != 0:
        return [part + (0,) for part in spread(chunk, falling)]
    rising = falling[-1:] + falling[:-1]
    first = [part + (0,) for part in spread(chunk[: rows // 2], falling)]
    return first + [part + (rows // 2,) for part in spread(chunk[rows // 2 :], rising)]


def piece_copies(rep, layout, refs, target, sems):
    share = target.shape[0] // sum(len(codes) for codes, offset in layout if offset == 0)
    copies = []
    for (codes, offset), ref in zip(layout, refs):
        rows = ref.shape[0] // len(codes)
        for at, code in enumerate(codes):
            first = pl.multiple_of(lax.bitwise_xor(rep, code) * share + offset, 8)
            copies.append(
                pltpu.make_async_copy(
                    ref.at[pl.ds(at * rows, rows), :], target.at[pl.ds(first, rows), :], sems.at[len(copies)]
                )
            )
    return copies


def pack_feed(gateup, down):
    depth = down.shape[1]
    rows = gateup.shape[0]
    rest = gateup[:, depth:]
    rest = jnp.concatenate([rest[: rows // 2], rest[rows // 2 :]], axis=1)
    return jnp.concatenate([gateup[:, :depth], rest, down], axis=0)


def feed_copies(packed, gateup, down, sems):
    replicas = packed.shape[0]
    depth = down.shape[1]
    rows, low_rows = gateup.shape[0] // replicas, down.shape[0] // replicas
    half = rows // 2
    rest = gateup.shape[1] - depth
    first, second = [], []
    for at in range(replicas):
        top = at * rows
        pairs = [
            (packed.at[at, 0:rows, :], gateup.at[top : top + rows, 0:depth]),
            (packed.at[at, rows : rows + half, 0:rest], gateup.at[top : top + half, depth : depth + rest]),
            (packed.at[at, rows : rows + half, rest : 2 * rest], gateup.at[top + half : top + rows, depth : depth + rest]),
        ]
        first += [pltpu.make_async_copy(x, y, sems.at[at * 4 + i]) for i, (x, y) in enumerate(pairs)]
        second.append(
            pltpu.make_async_copy(
                packed.at[at, rows + half : rows + half + low_rows, :],
                down.at[at * low_rows : (at + 1) * low_rows, :],
                sems.at[at * 4 + 3],
            )
        )
    return first, second


def start_all(copies):
    for copy in copies:
        copy.start()


def wait_all(copies):
    for copy in copies:
        copy.wait()


def unit_of(values):
    scale = lax.rsqrt(jnp.mean(values * values, axis=-1, keepdims=True) + EPSILON)
    return values * scale, scale


def norm_back(grad, unit, scale, gain):
    weighted = grad * gain
    return scale * (weighted - unit * jnp.mean(weighted * unit, axis=-1, keepdims=True))


def forward_kernel(layout, rep, meta, tok_ref, gain_ref, head_ref, cos_ref, sin_ref, start_ref, *refs):
    pieces = refs[: len(layout)]
    hid_out, q_out, raw_out, k_out, kt_out, v_out, mixed_out, log_ref = refs[len(layout) : len(layout) + 8]
    (tok_s, w_s, hid_s, q_s, raw_s, k_s, kt_s, v_s, vt_s, mixed_s, out_acc, sum_acc) = refs[len(layout) + 8 : -3]
    in_sems, w_sems, out_sems = refs[-3:]
    heads, total, width = q_s.shape
    groups = k_s.shape[0]
    pairs = heads // groups
    blocks = total // QUERIES
    factor = math.log2(math.e) / math.sqrt(width)

    def token_copy(block):
        here = pl.ds(pl.multiple_of(block * QUERIES, QUERIES), QUERIES)
        return pltpu.make_async_copy(tok_ref.at[here, :], tok_s.at[here, :], in_sems.at[block])

    def sent(block):
        here = pl.ds(pl.multiple_of(block * QUERIES, QUERIES), QUERIES)
        pairs_of = [
            (hid_s.at[here, :], hid_out.at[here, :]),
            (q_s.at[:, here, :], q_out.at[:, here, :]),
            (raw_s.at[:, here, :], raw_out.at[:, here, :]),
            (k_s.at[:, here, :], k_out.at[:, here, :]),
            (kt_s.at[:, :, here], kt_out.at[:, :, here]),
            (v_s.at[:, here, :], v_out.at[:, here, :]),
            (mixed_s.at[here, :], mixed_out.at[here, :]),
        ]
        return [pltpu.make_async_copy(x, y, out_sems.at[i, block]) for i, (x, y) in enumerate(pairs_of)]

    weights = piece_copies(rep[0], layout, pieces, w_s, w_sems)
    token_copy(0).start()
    start_all(weights)
    for block in range(1, blocks):
        token_copy(block).start()
    log_ref[...] = jnp.zeros_like(log_ref)
    vt_s[...] = jnp.zeros_like(vt_s)
    wait_all(weights)

    @pl.loop(0, blocks)
    def _(block):
        low, count = meta[block], meta[blocks + block]
        here = pl.ds(pl.multiple_of(block * QUERIES, QUERIES), QUERIES)
        token_copy(block).wait()
        unit, _ = unit_of(tok_s[here, :].astype(F32))
        hidden = (unit * gain_ref[...]).astype(BF16)
        hid_s[here, :] = hidden
        projected = nn(hidden, w_s[...])
        cosine, sine = cos_ref[here, :], sin_ref[here, :]
        means = jnp.full((width, width), 1.0 / width, BF16)
        for index in range(heads + groups):
            one = projected[:, index * width : (index + 1) * width]
            raw_s[index, here, :] = one.astype(BF16)
            gain = head_ref[0:1, :] if index < heads else head_ref[1:2, :]
            normed = one * lax.rsqrt(nn((one * one).astype(BF16), means) + EPSILON) * gain
            turned = normed * cosine + pltpu.roll(normed, width // 2, 1) * sine
            if index < heads:
                q_s[index, here, :] = turned.astype(BF16)
            else:
                k_s[index - heads, here, :] = turned.astype(BF16)
                kt_s[index - heads, :, here] = turned.T.astype(BF16)
        for index in range(groups):
            first = (heads + groups + index) * width
            one = projected[:, first : first + width]
            v_s[index, here, :] = one.astype(BF16)
            vt_s[index, :, here] = one.T.astype(BF16)

        start = jnp.concatenate([start_ref[:, here]] * pairs, axis=1)
        place = block * QUERIES + lax.broadcasted_iota(jnp.int32, (1, QUERIES), 1)
        place = jnp.concatenate([place] * pairs, axis=1)
        queries = [
            jnp.concatenate([q_s[g * pairs + j, here, :] for j in range(pairs)], axis=0) for g in range(groups)
        ]
        out_acc[...] = jnp.zeros_like(out_acc)
        sum_acc[...] = jnp.zeros_like(sum_acc)

        @pl.loop(0, count)
        def _(turn):
            base = pl.multiple_of(low + turn * KEYS, PIECE)
            key_place = base + lax.broadcasted_iota(jnp.int32, (KEYS, 1), 0)
            allowed = (key_place >= start) & (key_place <= place)
            for g in range(groups):
                scores = nt(k_s[g, pl.ds(base, KEYS), :], queries[g])
                weights = jnp.where(allowed, jnp.exp2(scores * factor), 0.0)
                sum_acc[g] += jnp.sum(weights, axis=0, keepdims=True)
                out_acc[g] += nn(vt_s[g, :, pl.ds(base, KEYS)], weights.astype(BF16))

        for g in range(groups):
            total_weight = sum_acc[g]
            mixed = out_acc[g] / total_weight
            logs = jnp.log2(total_weight)
            for j in range(pairs):
                head = g * pairs + j
                mixed_s[here, head * width : (head + 1) * width] = mixed[:, j * QUERIES : (j + 1) * QUERIES].T.astype(BF16)
                log_ref[head : head + 1, here] = logs[:, j * QUERIES : (j + 1) * QUERIES]
        start_all(sent(block))

    @pl.loop(0, blocks)
    def _(block):
        wait_all(sent(block))


def layout_of(pieces):
    return tuple((codes, offset) for _, codes, offset in pieces), [piece for piece, _, _ in pieces]


def slots(layout):
    return sum(len(codes) for codes, _ in layout)


def forward(rep, meta, tokens, gain, head_gains, cosine, sine, doc_start, pieces, heads, groups):
    total, depth = tokens.shape
    width = head_gains.shape[1]
    cols = pieces[0][0].shape[1]
    layout, arrays = layout_of(pieces)
    wide = heads // groups * QUERIES
    blocks = total // QUERIES
    outs = [
        (total, depth),
        (heads, total, width),
        (heads + groups, total, width),
        (groups, total, width),
        (groups, width, total),
        (groups, total, width),
        (total, heads * width),
    ]
    return pl.pallas_call(
        functools.partial(forward_kernel, layout),
        in_specs=[SM, SM, ANY] + [VM] * 5 + [ANY] * len(arrays),
        out_specs=[ANY] * 7 + [VM],
        out_shape=[sds(shape, BF16) for shape in outs] + [sds((8, total), F32)],
        scratch_shapes=[pltpu.VMEM((total, depth), BF16), pltpu.VMEM((depth, cols), BF16)]
        + [pltpu.VMEM(shape, BF16) for shape in outs[:6]]
        + [
            pltpu.VMEM((groups, width, total), BF16),
            pltpu.VMEM((total, heads * width), BF16),
            pltpu.VMEM((groups, width, wide), F32),
            pltpu.VMEM((groups, 1, wide), F32),
            pltpu.SemaphoreType.DMA((blocks,)),
            pltpu.SemaphoreType.DMA((slots(layout),)),
            pltpu.SemaphoreType.DMA((7, blocks)),
        ],
        compiler_params=params(),
        cost_estimate=cost(12e9, 20e6),
        name="attention_forward",
    )(rep, meta, tokens, gain, head_gains, cosine, sine, doc_start, *arrays)


def branch_kernel(layout, rep, core, mixed_ref, *refs):
    pieces = refs[: len(layout)]
    mine_out, other_first, other_rest, w_s, mixed_s, out_s, sems, w_sems, out_sems = refs[len(layout) :]
    quarter = mixed_s.shape[1]
    loads = [
        pltpu.make_async_copy(mixed_ref.at[pl.ds(at * quarter, quarter), :], mixed_s.at[at], sems.at[at]) for at in range(4)
    ]
    weights = piece_copies(rep[0], layout, pieces, w_s, w_sems)
    start_all(weights + loads)
    wait_all(weights)
    lasts = []
    for step in range(4):
        spot = step % 2
        side = 1 - step // 2
        at = 2 * spot + lax.rem(core[0] + side, 2)
        if step == 0:
            wait_all(loads)
        out_s[step] = nn(mixed_s[at], w_s[...]).astype(BF16).reshape(out_s.shape[1:])
        if side == 0:
            sends = [(out_s.at[step], mine_out.at[:, spot], step)]
        else:
            more = out_s.shape[1] - 1
            sends = [
                (out_s.at[step, 0], other_first.at[spot], step),
                (out_s.at[step, pl.ds(1, more)], other_rest.at[:, spot], 4 + step),
            ]
        for source, target, sem in sends:
            lasts.append(pltpu.make_async_copy(source, target, out_sems.at[sem]))
            lasts[-1].start()
    wait_all(lasts)


def branch(rep, core, mixed, pieces, depth):
    total, cols = mixed.shape
    layout, arrays = layout_of(pieces)
    parts = total // 4 // PIECE
    return pl.pallas_call(
        functools.partial(branch_kernel, layout),
        in_specs=[SM, SM] + [ANY] * (1 + len(arrays)),
        out_specs=[ANY, ANY, ANY],
        out_shape=[sds((rows, 2, PIECE, depth), BF16) if rows else sds((2, PIECE, depth), BF16) for rows in (parts, 0, parts - 1)],
        scratch_shapes=[
            pltpu.VMEM((cols, depth), BF16),
            pltpu.VMEM((4, total // 4, cols), BF16),
            pltpu.VMEM((4, parts, PIECE, depth), BF16),
            pltpu.SemaphoreType.DMA((4,)),
            pltpu.SemaphoreType.DMA((slots(layout),)),
            pltpu.SemaphoreType.DMA((8,)),
        ],
        compiler_params=params(),
        cost_estimate=cost(2 * total * cols * depth, 6e6),
        name="branch",
    )(rep, core, mixed, *arrays)


def feed_kernel(part, core, gain_ref, here_ref, there_ref, tok_ref, cot_ref, packed_ref, *refs):
    mine_out, other_out, sum_ref, down_out, hid_out, act_out, dgu_out = refs[-18:-11]
    mid_s, tok_s, cot_s, wgu_s, wd_s, terms_s, down_s, hid_s, act_s, dgu_s, sems = refs[-11:]
    units = wd_s.shape[0]
    spots = [(side, spot) for side in (1, 0) for spot in range(2)]
    spare = 4 * packed_ref.shape[0]

    def natural(ref, side, spot):
        return ref.at[spot, lax.rem(core[0] + side, 2), part]

    def rows(index):
        return pl.ds(index * PIECE, PIECE)

    first, cots, lasts = [], [], []
    for index, (side, spot) in enumerate(spots):
        at = spare + 8 * index
        source = (here_ref, there_ref)[side].at[spot]
        first.append(pltpu.make_async_copy(source, mid_s.at[rows(index), :], sems.at[at]))
        first.append(pltpu.make_async_copy(natural(tok_ref, side, spot), tok_s.at[rows(index), :], sems.at[at + 1]))
        cots.append(pltpu.make_async_copy(natural(cot_ref, side, spot), cot_s.at[rows(index), :], sems.at[at + 2]))
    gateups, downs = feed_copies(packed_ref, wgu_s, wd_s, sems)
    start_all(first + gateups + cots + downs)

    def send(scratch, target_of, kind):
        for index, (side, spot) in enumerate(spots):
            lasts.append(
                pltpu.make_async_copy(
                    scratch.at[rows(index), :], target_of(side, spot), sems.at[spare + 8 * index + 3 + kind]
                )
            )
            lasts[-1].start()

    wait_all(first)
    unit, _ = unit_of(tok_s[...].astype(F32) + mid_s[...].astype(F32))
    hid_s[...] = (unit * gain_ref[...]).astype(BF16)
    send(hid_s, lambda side, spot: natural(hid_out, side, spot), 0)
    wait_all(gateups)
    both = nn(hid_s[...], wgu_s[...])
    wait_all(cots + downs)
    grad_active = nt(cot_s[...], wd_s[...])
    gate, up = both[:, :units], both[:, units:]
    sig = jax.nn.sigmoid(gate)
    lit = gate * sig
    act_s[...] = (lit * up).astype(BF16)
    send(act_s, lambda side, spot: natural(act_out, side, spot), 1)
    dgu_s[:, :units] = (grad_active * up * sig * (1.0 + gate * (1.0 - sig))).astype(BF16)
    dgu_s[:, units:] = (grad_active * lit).astype(BF16)
    send(dgu_s, lambda side, spot: natural(dgu_out, side, spot), 2)
    terms = nt(dgu_s[...], wgu_s[...])
    terms_s[...] = terms.astype(BF16)
    send(terms_s, lambda side, spot: (mine_out, other_out)[side].at[spot], 3)
    down_s[...] = nn(act_s[...], wd_s[...]).astype(BF16)
    send(down_s, lambda side, spot: natural(down_out, side, spot), 4)
    sum_ref[...] = jnp.sum(terms * unit, axis=0, keepdims=True)
    wait_all(lasts)


def feed(part, parts, core, here, there, tokens_cut, cot_cut, gain, packed, units, chain):
    depth = gain.shape[1]
    saved = (
        (2, 2, parts, PIECE, depth),
        (2, 2, parts, PIECE, depth),
        (2, 2, parts, PIECE, units),
        (2, 2, parts, PIECE, 2 * units),
    )
    rows = 4 * PIECE
    return pl.pallas_call(
        functools.partial(feed_kernel, part),
        in_specs=[SM, VM] + [ANY] * (5 + len(chain)),
        out_specs=[ANY, ANY, VM] + [ANY] * 4,
        out_shape=[sds((2, PIECE, depth), BF16)] * 2
        + [sds((1, depth), F32)]
        + [sds(shape, BF16) for shape in saved],
        scratch_shapes=[
            pltpu.VMEM((rows, depth), BF16),
            pltpu.VMEM((rows, depth), BF16),
            pltpu.VMEM((rows, depth), BF16),
            pltpu.VMEM((depth, 2 * units), BF16),
            pltpu.VMEM((units, depth), BF16),
            pltpu.VMEM((rows, depth), BF16),
            pltpu.VMEM((rows, depth), BF16),
            pltpu.VMEM((rows, depth), BF16),
            pltpu.VMEM((rows, units), BF16),
            pltpu.VMEM((rows, 2 * units), BF16),
            pltpu.SemaphoreType.DMA((4 * packed.shape[0] + 32,)),
        ],
        input_output_aliases={7 + i: 3 + i for i in range(len(chain))},
        compiler_params=params(),
        cost_estimate=cost(2 * 4 * PIECE * depth * units * 6, 12e6),
        name=f"feed_{part}",
    )(core, gain, here, there, tokens_cut, cot_cut, packed, *chain)


def backward_kernel(layout, out_layout, parts, rep, meta, mid_gain, head_ref, cos_ref, sin_ref, start_ref, log_ref, fa_ref, fo_ref, shares_ref, *refs):
    seconds, refs = refs[:parts], refs[parts:]
    (tok_ref, cot_ref, q_hbm, k_hbm, kt_hbm, v_hbm, raw_hbm, mixed_hbm) = refs[:8]
    mid_parts, grad_parts = refs[8 : 8 + 2 * parts], refs[8 + 2 * parts : 12 + 2 * parts]
    hid_hbm = refs[12 + 2 * parts]
    refs = refs[13 + 2 * parts :]
    pieces, out_pieces = refs[: len(layout)], refs[len(layout) : len(layout) + len(out_layout)]
    rest = refs[len(layout) + len(out_layout) :]
    own_ref, own_mid, gb_out, grads_out, terms_out, left_ref, gains_ref = rest[:7]
    (mid_s, grad_s, tok_s, cot_s, w_s, wo_s, q_s, k_s, kt_s, v_s, raw_s, mixed_s, hid_s, gb_s, all_s, terms_s, dk_s, dv_s, dq_acc, query_sum, key_sum, first_sum) = rest[7:-5]
    row_sems, big_sems, w_sems, wo_sems, out_sems = rest[-5:]
    heads, total, width = q_s.shape
    groups = k_s.shape[0]
    pairs = heads // groups
    blocks, cuts = total // QUERIES, total // PIECE
    per = QUERIES // PIECE
    core, half = meta[4 * blocks], meta[4 * blocks + 1]
    root = 1.0 / math.sqrt(width)
    factor = math.log2(math.e) * root

    def grad_copy(side, part, spot, cut):
        source = grad_parts[side].at[spot] if part == 0 else grad_parts[2 + side].at[2 * part - 2 + spot]
        return pltpu.make_async_copy(source, grad_s.at[pl.ds(cut * PIECE, PIECE), :], row_sems.at[1, cut])

    def row_copies(cut):
        quarter, part = cut // parts, cut % parts
        spot = quarter // 2
        here = pl.ds(cut * PIECE, PIECE)
        near = lax.rem(core + quarter, 2) == 0

        @pl.when(near)
        def _():
            pltpu.make_async_copy(mid_parts[2 * part].at[spot], mid_s.at[here, :], row_sems.at[0, cut]).start()
            grad_copy(0, part, spot, cut).start()

        @pl.when(jnp.logical_not(near))
        def _():
            pltpu.make_async_copy(mid_parts[2 * part + 1].at[spot], mid_s.at[here, :], row_sems.at[0, cut]).start()
            grad_copy(1, part, spot, cut).start()

        pltpu.make_async_copy(tok_ref.at[here, :], tok_s.at[here, :], row_sems.at[2, cut]).start()
        pltpu.make_async_copy(cot_ref.at[here, :], cot_s.at[here, :], row_sems.at[3, cut]).start()

    big = [
        pltpu.make_async_copy(x, y, big_sems.at[i])
        for i, (x, y) in enumerate(
            [
                (k_hbm, k_s), (v_hbm, v_s), (q_hbm, q_s), (kt_hbm, kt_s), (mixed_hbm, mixed_s),
                (raw_hbm, raw_s),
            ]
        )
    ]
    weights = piece_copies(rep[0], layout, pieces, w_s, w_sems)
    out_weights = piece_copies(rep[0], out_layout, out_pieces, wo_s, wo_sems)
    for cut in range(cuts - 1, cuts - 1 - per, -1):
        row_copies(cut)
    start_all(out_weights + big + weights)
    for cut in range(cuts - 1 - per, -1, -1):
        row_copies(cut)
    hidden_copy = pltpu.make_async_copy(hid_hbm, hid_s, big_sems.at[6])
    hidden_copy.start()
    dk_s[...] = jnp.zeros_like(dk_s)
    dv_s[...] = jnp.zeros_like(dv_s)
    query_sum[...] = jnp.zeros_like(query_sum)
    key_sum[...] = jnp.zeros_like(key_sum)
    first_sum[...] = jnp.zeros_like(first_sum)
    ones = jnp.ones((8, width), F32)
    query_gain, key_gain = head_ref[0:1, :], head_ref[1:2, :]
    means = jnp.full((width, width), 1.0 / width, BF16)

    def mean_of(values):
        return nn(values.astype(BF16), means)

    def head_back(grad, raw, cosine, sine, gain):
        turned = grad * cosine - pltpu.roll(grad, width // 2, 1) * sine
        scale = lax.rsqrt(mean_of(raw * raw) + EPSILON)
        unit = raw * scale
        weighted = turned * gain
        back = scale * (weighted - unit * mean_of(weighted * unit))
        return back.astype(BF16), jnp.sum(turned * unit, axis=0, keepdims=True)

    def out_copies(block):
        here = pl.ds(pl.multiple_of(block * QUERIES, QUERIES), QUERIES)
        pairs_of = [(gb_s, gb_out), (all_s, grads_out), (terms_s, terms_out)]
        return [
            pltpu.make_async_copy(x.at[here, :], y.at[here, :], out_sems.at[i, block]) for i, (x, y) in enumerate(pairs_of)
        ]

    @pl.loop(0, blocks)
    def _(turn_of):
        block = blocks - 1 - turn_of
        low, count = meta[2 * blocks + block], meta[3 * blocks + block]
        rows = pl.ds(pl.multiple_of(block * QUERIES, QUERIES), QUERIES)
        for at in range(per):
            cut = block * per + at
            here = pl.ds(pl.multiple_of(cut * PIECE, PIECE), PIECE)
            for kind, target in enumerate((mid_s, grad_s, tok_s, cot_s)):
                pltpu.make_async_copy(tok_ref.at[here, :], target.at[here, :], row_sems.at[kind, cut]).wait()
        middle = tok_s[rows, :].astype(F32) + mid_s[rows, :].astype(F32)
        unit, scale = unit_of(middle)
        result = cot_s[rows, :].astype(F32) + norm_back(grad_s[rows, :].astype(F32), unit, scale, mid_gain[...])
        low_grad = result.astype(BF16)
        gb_s[rows, :] = low_grad
        for at in range(per):
            cut = block * per + at

            @pl.when(cut // parts == 2 * half + core)
            def _():
                own_ref[lax.rem(cut, parts)] = result[at * PIECE : (at + 1) * PIECE]
                own_mid[lax.rem(cut, parts)] = middle[at * PIECE : (at + 1) * PIECE]

        @pl.when(turn_of == 0)
        def _():
            wait_all(out_weights + big)

        grad_mixed = nt(low_grad, wo_s[...]).astype(BF16)
        mixed = mixed_s[rows, :]
        start = jnp.concatenate([start_ref[:, rows]] * pairs, axis=1)
        place = block * QUERIES + lax.broadcasted_iota(jnp.int32, (1, QUERIES), 1)
        place = jnp.concatenate([place] * pairs, axis=1)
        queries, grads, logs, deltas = [], [], [], []
        for g in range(groups):
            members = range(g * pairs, (g + 1) * pairs)
            queries.append(jnp.concatenate([q_s[h, rows, :] for h in members], axis=0))
            grad = jnp.concatenate([grad_mixed[:, h * width : (h + 1) * width] for h in members], axis=0)
            out = jnp.concatenate([mixed[:, h * width : (h + 1) * width] for h in members], axis=0)
            grads.append(grad)
            logs.append(jnp.concatenate([log_ref[h : h + 1, rows] for h in members], axis=1))
            terms = lax.dot_general(
                ones,
                grad.astype(F32) * out.astype(F32),
                (((1,), (1,)), ((), ())),
                precision=lax.Precision.HIGHEST,
                preferred_element_type=F32,
            )
            deltas.append(terms[0:1, :])
        dq_acc[...] = jnp.zeros_like(dq_acc)

        @pl.loop(0, count)
        def _(turn):
            base = pl.multiple_of(low + turn * KEYS_BACK, PIECE)
            key_place = base + lax.broadcasted_iota(jnp.int32, (KEYS_BACK, 1), 0)
            allowed = (key_place >= start) & (key_place <= place)
            keys = pl.ds(base, KEYS_BACK)
            for g in range(groups):
                scores = nt(k_s[g, keys, :], queries[g])
                weights = jnp.where(allowed, jnp.exp2(scores * factor - logs[g]), 0.0)
                grad_weights = nt(v_s[g, keys, :], grads[g])
                grad_scores = (weights * (grad_weights - deltas[g])).astype(BF16)
                dv_s[g, keys, :] += nn(weights.astype(BF16), grads[g])
                dk_s[g, keys, :] += nn(grad_scores, queries[g])
                dq_acc[g] += nn(kt_s[g, :, keys], grad_scores)

        cosine, sine = cos_ref[rows, :], sin_ref[rows, :]
        sums = jnp.zeros((1, width), F32)
        columns = []
        for head in range(heads):
            j = head % pairs
            grad = dq_acc[head // pairs, :, j * QUERIES : (j + 1) * QUERIES].T * root
            back, part_sum = head_back(grad, raw_s[head, rows, :].astype(F32), cosine, sine, query_gain)
            columns.append(back)
            sums = sums + part_sum
        query_sum[...] += sums
        sums = jnp.zeros((1, width), F32)
        for g in range(groups):
            back, part_sum = head_back(
                dk_s[g, rows, :] * root, raw_s[heads + g, rows, :].astype(F32), cosine, sine, key_gain
            )
            columns.append(back)
            sums = sums + part_sum
        key_sum[...] += sums
        for g in range(groups):
            columns.append(dv_s[g, rows, :].astype(BF16))
        everything = jnp.concatenate(columns, axis=1)
        all_s[rows, :] = everything

        @pl.when(turn_of == 0)
        def _():
            wait_all(weights)

        terms = nt(everything, w_s[...])
        first_sum[...] += jnp.sum(terms * unit_of(tok_s[rows, :].astype(F32))[0], axis=0, keepdims=True)
        terms_s[rows, :] = terms.astype(BF16)
        start_all(out_copies(block))

    hidden_copy.wait()
    all_left = tn(nn(all_s[...], fa_ref[...]).astype(BF16), hid_s[...])
    out_left = tn(nn(gb_s[...], fo_ref[...]).astype(BF16), mixed_s[...])
    ranks, depth = left_ref.shape[0], first_sum.shape[1]
    for at in range(3):
        cols = slice(at * depth, (at + 1) * depth)
        left_ref[:, cols] = (all_left[at * ranks : (at + 1) * ranks, :] + shares_ref[:, cols]).astype(BF16)
    left_ref[:, 3 * depth :] = (out_left[:ranks, :] + shares_ref[:, 3 * depth :]).astype(BF16)
    second = sum(one[...] for one in seconds[1:]) + seconds[0][...]
    gains_ref[...] = jnp.zeros_like(gains_ref)
    wide = depth // 4
    for at in range(4):
        gains_ref[at : at + 1, :wide] = first_sum[:, at * wide : (at + 1) * wide]
        gains_ref[4 + at : 5 + at, :wide] = second[:, at * wide : (at + 1) * wide]
    gains_ref[0:1, wide : wide + width] = query_sum[...]
    gains_ref[1:2, wide : wide + width] = key_sum[...]

    @pl.loop(0, blocks)
    def _(block):
        wait_all(out_copies(block))


def backward(
    rep, meta, gain, head_gains, cosine, sine, doc_start, logs, tokens, cotangent, q_rot, k_rot, k_turned, v_heads, raw,
    mixed, hidden, fa, fo, shares, seconds, mids, grads, pieces, out_pieces
):
    heads, total, width = q_rot.shape
    groups = k_rot.shape[0]
    depth = tokens.shape[1]
    cols = pieces[0][0].shape[1]
    parts = len(mids)
    blocks = total // QUERIES
    layout, arrays = layout_of(pieces)
    out_layout, out_arrays = layout_of(out_pieces)
    flat = [one for pair in mids + grads for one in pair]
    big = (tokens, cotangent, q_rot, k_rot, k_turned, v_heads, raw, mixed)
    rows = pltpu.VMEM((total, depth), BF16)
    return pl.pallas_call(
        functools.partial(backward_kernel, layout, out_layout, parts),
        in_specs=[SM, SM] + [VM] * (9 + parts) + [ANY] * (1 + len(big) + len(flat) + len(arrays) + len(out_arrays)),
        out_specs=[VM, VM, ANY, ANY, ANY, VM, VM],
        out_shape=[
            sds((parts, PIECE, depth), F32),
            sds((parts, PIECE, depth), F32),
            sds((total, depth), BF16),
            sds((total, cols), BF16),
            sds((total, depth), BF16),
            sds(shares.shape, BF16),
            sds((8, depth // 4 + width), F32),
        ],
        scratch_shapes=[rows, rows, rows, rows, pltpu.VMEM((depth, cols), BF16), pltpu.VMEM((heads * width, depth), BF16)]
        + [pltpu.VMEM(one.shape, BF16) for one in (q_rot, k_rot, k_turned, v_heads, raw, mixed, hidden)]
        + [
            rows,
            pltpu.VMEM((total, cols), BF16),
            rows,
            pltpu.VMEM((groups, total, width), F32),
            pltpu.VMEM((groups, total, width), F32),
            pltpu.VMEM((groups, width, heads // groups * QUERIES), F32),
            pltpu.VMEM((1, width), F32),
            pltpu.VMEM((1, width), F32),
            pltpu.VMEM((1, depth), F32),
            pltpu.SemaphoreType.DMA((4, total // PIECE)),
            pltpu.SemaphoreType.DMA((7,)),
            pltpu.SemaphoreType.DMA((slots(layout),)),
            pltpu.SemaphoreType.DMA((slots(out_layout),)),
            pltpu.SemaphoreType.DMA((3, blocks)),
        ],
        compiler_params=params(),
        cost_estimate=cost(20e9, 30e6),
        name="attention_backward",
    )(rep, meta, gain, head_gains, cosine, sine, doc_start, logs, fa, fo, shares, *seconds, *big, *flat, hidden, *arrays, *out_arrays)


def shares_kernel(count, *refs):
    errors, starts, out_ref = refs[:count], refs[count:-1], refs[-1]
    blocks = []
    for error in errors:
        blocks += [error[at] for at in range(error.shape[0])] if len(error.shape) == 3 else [error[...]]
    first = 0
    for block, start in zip(blocks, starts):
        high = start[...].astype(BF16)
        low = (start[...] - high.astype(F32)).astype(BF16)
        both = nt(jnp.concatenate([high, low], axis=0), block.astype(BF16))
        ranks, rows = start.shape[0], block.shape[0]
        out_ref[:, first : first + rows] = both[:ranks] + both[ranks:]
        first += rows


def shares_of(errors, starts, rows):
    return pl.pallas_call(
        functools.partial(shares_kernel, len(errors)),
        in_specs=[VM] * (len(errors) + len(starts)),
        out_specs=VM,
        out_shape=sds((starts[0].shape[0], rows), F32),
        compiler_params=params(),
        cost_estimate=cost(1e9, 16e6),
        name="error_shares",
    )(*errors, *starts)


def feed_moment_kernel(steps, hid_ref, dgu_ref, gu_error, act_ref, cot_ref, d_error, gu_start, d_start, *outs):
    gu_out, d_out, gu_left, d_left = outs
    units = gu_out.shape[2]
    step = pl.program_id(0)

    def left_of(start, moment):
        both = nt(jnp.concatenate(two_parts(start), axis=0), moment.astype(BF16))
        ranks = start.shape[0]
        return both[:ranks] + both[ranks:]

    @pl.when(step < steps)
    def _():
        both = tn(hid_ref[...], dgu_ref[...])
        for at in range(2):
            moment = both[:, at * units : (at + 1) * units] + gu_error[at]
            gu_out[at] = moment
            gu_left[at] = left_of(gu_start[at], moment)

    @pl.when(step >= steps)
    def _():
        moment = tn(act_ref[...], cot_ref[...]) + d_error[...]
        d_out[...] = moment
        d_left[...] = left_of(d_start[...], moment)


def feed_moments(hidden, grads, gu_error, active, cotangent, d_error, gu_start, d_start):
    total, depth = hidden.shape
    units = active.shape[1]
    ranks = d_start.shape[0]
    rows, low_rows = 512, 384
    steps, more = depth // rows, units // low_rows
    early = lambda i: jnp.minimum(i, steps - 1)
    late = lambda i: jnp.maximum(i - steps, 0)
    return pl.pallas_call(
        functools.partial(feed_moment_kernel, steps),
        grid=(steps + more,),
        in_specs=[
            pl.BlockSpec((total, rows), lambda i: (0, early(i))),
            pl.BlockSpec((total, 2 * units), lambda i: (0, 0)),
            pl.BlockSpec((2, rows, units), lambda i: (0, early(i), 0)),
            pl.BlockSpec((total, low_rows), lambda i: (0, late(i))),
            pl.BlockSpec((total, depth), lambda i: (0, 0)),
            pl.BlockSpec((low_rows, depth), lambda i: (late(i), 0)),
            pl.BlockSpec((2, ranks, units), lambda i: (0, 0, 0)),
            pl.BlockSpec((ranks, depth), lambda i: (0, 0)),
        ],
        out_specs=[
            pl.BlockSpec((2, rows, units), lambda i: (0, early(i), 0)),
            pl.BlockSpec((low_rows, depth), lambda i: (late(i), 0)),
            pl.BlockSpec((2, ranks, rows), lambda i: (0, 0, early(i))),
            pl.BlockSpec((ranks, low_rows), lambda i: (0, late(i))),
        ],
        out_shape=[
            sds(gu_error.shape, F32),
            sds(d_error.shape, F32),
            sds((2, ranks, depth), F32),
            sds((ranks, units), F32),
        ],
        compiler_params=params(),
        cost_estimate=cost(1, 1),
        name="feed_moments",
    )(hidden, grads, gu_error, active, cotangent, d_error, gu_start, d_start)


def orthonormal_panel(panel):
    ranks = panel.shape[0]
    index = lax.broadcasted_iota(jnp.int32, (ranks, 1), 0)
    for at in range(ranks):
        column = panel[at : at + 1, :]
        column = column * lax.rsqrt(jnp.sum(column * column, axis=1, keepdims=True) + EPSILON)
        dots = jnp.sum(panel * column, axis=1, keepdims=True)
        later = panel - dots * column
        panel = jnp.where(index > at, later, jnp.where(index == at, column, panel))
    return panel


def two_parts(value):
    high = value.astype(BF16)
    return high, (value - high.astype(F32)).astype(BF16)


def panels_of(refs):
    views = []
    for ref in refs:
        views += [ref.at[0], ref.at[1]] if len(ref.shape) == 3 else [ref]
    return views


def factors_kernel(count, kinds, lefts_ref, *refs):
    moments, lefts_out, rights_ref = refs[:count], refs[count : count + kinds], refs[count + kinds]
    held, sems = refs[count + kinds + 1 : -1], refs[-1]
    copies = [pltpu.make_async_copy(x, y, sems.at[i]) for i, (x, y) in enumerate(zip(panels_of(moments), panels_of(held)))]
    start_all(copies)
    done = []
    first = 0
    for source, target in zip(panels_of(held), panels_of(lefts_out)):
        rows = source.shape[0]
        done.append(orthonormal_panel(lefts_ref[:, first : first + rows]))
        target[...] = done[-1]
        first += rows
    first = 0
    for panel, source, copy in zip(done, panels_of(held), copies):
        ranks, cols = panel.shape[0], source.shape[1]
        both = jnp.concatenate(two_parts(panel), axis=0)
        copy.wait()
        result = nn(both, source[...].astype(BF16))
        rights_ref[:, first : first + cols] = (result[:ranks] + result[ranks:]).astype(BF16)
        first += cols


def make_factors(label, lefts, moments, shapes, cols):
    ranks = lefts.shape[0]
    return pl.pallas_call(
        functools.partial(factors_kernel, len(moments), len(shapes)),
        in_specs=[VM] + [ANY] * len(moments),
        out_specs=[VM] * (len(shapes) + 1),
        out_shape=[sds(shape, F32) for shape in shapes] + [sds((ranks, cols), BF16)],
        scratch_shapes=[pltpu.VMEM(one.shape, F32) for one in moments] + [pltpu.SemaphoreType.DMA((4,))],
        compiler_params=params(),
        cost_estimate=cost(1, 1),
        name=f"factors_{label}",
    )(lefts, *moments)


def settle_kernel(replicas, count, kinds, gained, rep, summed_ref, *refs):
    gains, refs = refs[: 4 * gained], refs[4 * gained :]
    lefts, refs = panels_of(refs[:kinds]), refs[kinds:]
    moments, refs = refs[:count], refs[count:]
    weights, velocities, outs = refs[:kinds], refs[kinds : 2 * kinds], refs[2 * kinds :]
    rights_out, outs = outs[:kinds], outs[kinds:]
    gains_out, outs = outs[: 4 * gained], outs[4 * gained :]
    errors_out, weights_out, velocities_out = outs[:kinds], outs[kinds : 2 * kinds], outs[2 * kinds : 3 * kinds]
    scratch = outs[3 * kinds :]
    held, approx = scratch[:count], scratch[count : 2 * count]
    weights_s, velocities_s = scratch[2 * count : 2 * count + kinds], scratch[2 * count + kinds : 2 * count + 2 * kinds]
    in_sems, small_sems, out_sems, last_sems = scratch[-4:]
    copies = [
        pltpu.make_async_copy(x, y, in_sems.at[i]) for i, (x, y) in enumerate(zip(panels_of(moments), panels_of(held)))
    ]
    small = [
        pltpu.make_async_copy(x, y, small_sems.at[i])
        for i, (x, y) in enumerate(zip(weights + velocities, weights_s + velocities_s))
    ]
    start_all(copies + small)
    if gained:
        bg_ref, bv_ref, hg_ref, hv_ref = gains
        wide = bg_ref.shape[1] // 4
        width = hg_ref.shape[1]
        base = summed_ref.shape[1] - wide - width
        for row in range(2):
            for at in range(4):
                cols = slice(at * wide, (at + 1) * wide)
                mean = summed_ref[4 * row + at : 4 * row + at + 1, base : base + wide] / replicas
                velocity = MOMENTUM * bv_ref[row : row + 1, cols] + mean
                gains_out[1][row : row + 1, cols] = velocity
                gains_out[0][row : row + 1, cols] = bg_ref[row : row + 1, cols] - GAIN_RATE * velocity
            mean = summed_ref[row : row + 1, base + wide : base + wide + width] / replicas
            velocity = MOMENTUM * hv_ref[row : row + 1, :] + mean
            gains_out[3][row : row + 1, :] = velocity
            gains_out[2][row : row + 1, :] = hg_ref[row : row + 1, :] - GAIN_RATE * velocity

    first = 0
    lasts = []
    everything = zip(lefts, panels_of(rights_out), panels_of(held), panels_of(approx), copies, panels_of(errors_out))
    for index, (left, right_out, moment, product, copy, target) in enumerate(everything):
        cols = moment.shape[1]
        right = summed_ref[:, first : first + cols] / replicas
        first += cols
        right_out[...] = right
        left_high, left_low = two_parts(left[...])
        right_high, right_low = two_parts(right)
        product[...] = tn(
            jnp.concatenate([left_high, left_low, left_high, left_low], axis=0),
            jnp.concatenate([right_high, right_high, right_low, right_low], axis=0),
        )
        copy.wait()
        moment[...] = moment[...] - product[...]
        lasts.append(pltpu.make_async_copy(moment, target, out_sems.at[index]))
        lasts[-1].start()
    wait_all(small)
    updates = zip(panels_of(approx), panels_of(weights_s), panels_of(velocities_s))
    for product, weight, velocity in updates:
        rows = weight.shape[0]
        mine = product[pl.ds(pl.multiple_of(rep[0] * rows, 8), rows), :]
        fresh = MOMENTUM * velocity[...] + mine
        velocity[...] = fresh
        weight[...] = weight[...] - STEP_RATE * fresh
    moves = zip(weights_s + velocities_s, weights_out + velocities_out)
    for index, (source, target) in enumerate(moves):
        lasts.append(pltpu.make_async_copy(source, target, last_sems.at[index]))
        lasts[-1].start()
    wait_all(lasts)


def settle(label, replicas, rep, summed, gains, lefts, moments, weights, velocities, rights, errors):
    small = [sds(one.shape, F32) for one in weights + velocities]
    kinds = len(lefts)
    outs = kinds + len(gains)
    results = pl.pallas_call(
        functools.partial(settle_kernel, replicas, len(moments), kinds, len(gains) // 4),
        in_specs=[SM] + [VM] * (1 + len(gains) + kinds) + [ANY] * (len(moments) + 2 * kinds),
        out_specs=[VM] * outs + [ANY] * (3 * kinds),
        out_shape=[sds(shape, F32) for shape in rights]
        + [sds(one.shape, F32) for one in gains]
        + [sds(shape, F32) for shape in errors]
        + small,
        scratch_shapes=[pltpu.VMEM(one.shape, F32) for one in moments + moments + weights + velocities]
        + [pltpu.SemaphoreType.DMA((2 * kinds,))] * 4,
        compiler_params=params(),
        cost_estimate=cost(1, 1),
        name=f"settle_{label}",
    )(rep, summed, *gains, *lefts, *moments, *weights, *velocities)
    rows = [results[outs + at * kinds : outs + (at + 1) * kinds] for at in range(3)]
    return results[:kinds], results[kinds:outs], rows


def on_device(
    tokens,
    cotangent,
    lengths,
    block_gains,
    block_velocity,
    head_gains,
    head_velocity,
    weight_query,
    velocity_query,
    error_query,
    factor_query,
    weight_keyval,
    velocity_keyval,
    error_keyval,
    factor_keyval,
    weight_out,
    velocity_out,
    error_out,
    factor_out,
    weight_gateup,
    velocity_gateup,
    error_gateup,
    factor_gateup,
    weight_down,
    velocity_down,
    error_down,
    factor_down,
):
    total, depth = tokens.shape
    width = head_gains.shape[1]
    heads = weight_query.shape[1] // width
    groups = weight_keyval.shape[2] // width
    units = weight_gateup.shape[2]
    quarter = total // 4
    parts = quarter // PIECE
    blocks = total // PIECE
    replicas = lax.axis_size("rep")
    rep_index = lax.axis_index("rep")
    kv_index = lax.axis_index("kv")
    core = lax.rem(kv_index, 2)
    half = kv_index // 2
    rep = rep_index[None].astype(jnp.int32)
    core_at = core[None].astype(jnp.int32)

    pieces_qkv = gather_halves(
        jnp.concatenate([weight_query, weight_keyval[0], weight_keyval[1]], axis=1).astype(BF16)
    )
    pieces_out = gather_halves(weight_out.astype(BF16))
    packed = pack_feed(
        jnp.concatenate([weight_gateup[0], weight_gateup[1]], axis=1).astype(BF16), weight_down.astype(BF16)
    )
    packed = lax.all_gather(packed, "rep", axis=0)

    own_lengths = lengths[0]
    docs = own_lengths.shape[0]
    before = jnp.arange(docs)[:, None] >= jnp.arange(docs)[None, :]
    ends = jnp.sum(jnp.where(before, own_lengths[None, :], 0), axis=1)
    places = jnp.arange(total, dtype=jnp.int32)
    passed = places[None, :] >= ends[:, None]
    doc_start = jnp.sum(jnp.where(passed, own_lengths[:, None], 0), axis=0, keepdims=True).astype(jnp.int32)
    position = (places[None, :] - doc_start)[0]
    meta = []
    for rows, keys in ((QUERIES, KEYS), (QUERIES, KEYS_BACK)):
        block_ends = (jnp.arange(total // rows, dtype=jnp.int32) + 1) * rows
        turns = (block_ends - doc_start[0, ::rows] + keys - 1) // keys
        meta += [jnp.maximum(block_ends - turns * keys, 0), turns]
    meta = jnp.concatenate(meta + [core[None], half[None]]).astype(jnp.int32)

    half_index = jnp.arange(width // 2, dtype=F32)
    frequency = ROPE_BASE ** (-2.0 * half_index / width)
    angles = position.astype(F32)[:, None] * frequency[None, :]
    cosine, sine = jnp.cos(angles), jnp.sin(angles)
    cosine = jnp.concatenate([cosine, cosine], axis=1)
    sine = jnp.concatenate([-sine, sine], axis=1)

    tokens_cut = tokens.reshape(2, 2, parts, PIECE, depth)
    cot_cut = cotangent.reshape(2, 2, parts, PIECE, depth)

    def chip_sum(mine, theirs):
        return (mine.astype(F32) + theirs.astype(F32)).astype(BF16)

    def cross_sum(own, *earlier):
        theirs = flip_kv(own, 2)
        summed = (after(own, *earlier).astype(F32) + theirs.astype(F32)).astype(BF16)
        return summed, flip_kv(summed, 1)

    factors = [one.T for one in (factor_query, factor_keyval[0], factor_keyval[1], factor_out[0])]
    tied = (error_query[0], error_keyval[0], error_out[0])
    tied = lax.optimization_barrier((*tied, pieces_qkv[0][0], pieces_qkv[2 % len(pieces_qkv)][0]))[:3]
    query_rows, group_cols = heads * width, groups * width
    shares = shares_of(tied, factors, 3 * depth + query_rows)
    doc_start = after(doc_start, shares)
    ranks = factor_query.shape[1]

    def laid(parts_of):
        rows = []
        for at, one in enumerate(parts_of):
            pads = (at * ranks, 128 - (at + 1) * ranks)
            rows.append(jnp.pad(one.T, ((0, 0), pads)))
        return jnp.concatenate(rows, axis=0).astype(BF16)

    laid_attn, laid_out = laid(factors[:3]), laid(factors[3:4])
    doc_start = after(doc_start, laid_attn, laid_out)

    hidden_first, q_rot, raw, k_rot, k_turned, v_heads, mixed, logs = forward(
        rep, meta, tokens, block_gains[0:1], head_gains, cosine, sine, doc_start, pieces_qkv, heads, groups
    )
    mine, other, later = branch(rep, core_at, mixed, pieces_out, depth)
    owns = [chip_sum(mine[0], flip_kv(other, 1))]
    theirs = flip_kv(after(later, owns[0]), 1)
    owns += [chip_sum(mine[p + 1], theirs[p]) for p in range(parts - 1)]

    mids, chain, terms_parts, second_parts, term_owns = [], [], [], [], []
    earlier = ()
    for part in range(parts):
        mids.append(cross_sum(owns[part], *earlier))
        here = mids[part][0]
        if part >= 2:
            mine, theirs = terms_parts[part - 2]
            term_owns.append(chip_sum(mine, after(theirs, terms_parts[part - 1][0])))
            here = after(here, term_owns[-1])
        mine, other, second, *chain = feed(
            part, parts, core_at, here, mids[part][1], tokens_cut, cot_cut, block_gains[1:2],
            packed, units, chain,
        )
        earlier = (mine,)
        terms_parts.append((mine, flip_kv(other, 1)))
        second_parts.append(second)
    down_terms = chain[0].reshape(total, depth)

    down_terms = chain[0].reshape(total, depth)
    last = terms_parts[parts - 1][0]
    bits = rep_bits()
    grads = [cross_sum(term_owns[0], last)]
    term_owns.append(chip_sum(terms_parts[1][0], after(terms_parts[1][1], grads[0][0])))
    term_owns.append(chip_sum(terms_parts[2][0], after(terms_parts[2][1], term_owns[1])))
    both_owns = jnp.concatenate(term_owns[1:], axis=0)
    *chain, _ = lax.optimization_barrier((*chain[1:], both_owns))
    hid_full, act_full, dgu_full = [one.reshape(total, -1) for one in chain]
    moment_gateup, moment_down, gu_left, d_left = feed_moments(
        hid_full, dgu_full, error_gateup[0], act_full, cotangent, error_down[0], jnp.swapaxes(factor_gateup, 1, 2),
        factor_down[0].T,
    )
    feed_lefts = jnp.concatenate([gu_left[0], gu_left[1], d_left], axis=1)
    pending = begin_sum(feed_lefts, bits[0])
    grads.append(cross_sum(both_owns, moment_down))
    feed_lefts = end_sum(pending, grads[1][0])
    pending = begin_sum(feed_lefts, bits[1])
    feed_own = lax.psum_scatter(after(down_terms, grads[1][0]), "kv", scatter_dimension=0, tiled=True)

    own_grad, own_middle, gb_full, grads_qkv, input_terms, attn_lefts, gains = backward(
        rep, meta, block_gains[1:2], head_gains, cosine, sine, doc_start, logs, tokens, cotangent, q_rot, k_rot,
        k_turned, v_heads, raw, mixed, hidden_first, laid_attn, laid_out, shares, second_parts, mids, grads, pieces_qkv,
        pieces_out,
    )

    attn_lefts = after(attn_lefts, feed_own)
    feed_lefts = end_sum(pending, own_grad)
    pending, feed_pending = begin_sum(attn_lefts, bits[0]), begin_sum(feed_lefts, bits[2])
    grads_qkv = after(grads_qkv, attn_lefts, feed_lefts)
    moment_query = tn(hidden_first, grads_qkv[:, :query_rows]) + error_query[0]
    gains = gains + flip_kv(gains, 1)
    attn_lefts, feed_lefts = end_sum(pending, moment_query), end_sum(feed_pending, moment_query)
    for bit in bits[3:]:
        feed_lefts = end_sum(begin_sum(feed_lefts, bit))
    pending = begin_sum(attn_lefts, bits[1])
    *left_feed, right_feed = make_factors(
        "feed", after(feed_lefts, attn_lefts), [moment_gateup, moment_down],
        [(2, ranks, depth), (ranks, units)], 2 * units + depth,
    )
    gains = gains + flip_kv(gains, 2)
    attn_lefts = end_sum(pending, right_feed)
    pending, feed_pending = begin_sum(attn_lefts, bits[2]), begin_sum(right_feed, bits[0])
    moment_out = tn(mixed, after(gb_full, attn_lefts, right_feed)) + error_out[0]
    attn_lefts, right_feed = end_sum(pending, moment_out), end_sum(feed_pending, moment_out)
    feed_pending = begin_sum(right_feed, bits[1])
    for bit in bits[3:]:
        attn_lefts = end_sum(begin_sum(attn_lefts, bit))
    grads_qkv = after(grads_qkv, attn_lefts, right_feed)
    moment_key = tn(hidden_first, grads_qkv[:, query_rows : query_rows + group_cols]) + error_keyval[0, 0]
    moment_value = tn(hidden_first, grads_qkv[:, query_rows + group_cols :]) + error_keyval[0, 1]
    right_feed = end_sum(feed_pending, moment_key, moment_value)
    feed_pending = begin_sum(right_feed, bits[2])
    attn_moments = [moment_query, moment_key, moment_value, moment_out]
    *left_attn, right_attn = make_factors(
        "attn", after(attn_lefts, right_feed), attn_moments,
        [(ranks, depth), (2, ranks, depth), (ranks, query_rows)], query_rows + 2 * group_cols + depth,
    )
    right_feed = end_sum(feed_pending, right_attn)
    for bit in bits[3:]:
        right_feed = end_sum(begin_sum(right_feed, bit))
    summed = jnp.concatenate([right_attn, gains.astype(BF16)], axis=1)
    pending = begin_sum(summed, bits[0])
    feed_rights, _, feed_rest = settle(
        "feed", replicas, rep, after(right_feed, right_attn), [], left_feed, [moment_gateup, moment_down],
        [weight_gateup, weight_down], [velocity_gateup, velocity_down],
        [(2, ranks, units), (ranks, depth)], [moment_gateup.shape, moment_down.shape],
    )
    summed = end_sum(pending, feed_rights[1])
    pending = begin_sum(summed, bits[1])

    grad_first = lax.psum_scatter(input_terms, "kv", scatter_dimension=0, tiled=True)
    own_middle, own_grad, feed_own, _ = lax.optimization_barrier((own_middle, own_grad, feed_own, summed))
    layer_out = (own_middle.reshape(quarter, depth) + feed_own.astype(F32)).astype(BF16)
    summed = end_sum(pending, layer_out)
    pending = begin_sum(summed, bits[2])
    own_tokens = lax.dynamic_slice_in_dim(tokens, kv_index * quarter, quarter, 0).astype(F32)
    unit, scale = unit_of(own_tokens)
    grad_first = after(grad_first, summed).astype(F32)
    input_grad = own_grad.reshape(quarter, depth) + norm_back(grad_first, unit, scale, block_gains[0])
    summed = end_sum(pending, input_grad)
    for bit in bits[3:]:
        summed = end_sum(begin_sum(summed, bit))
    attn_rights, gains, attn_rest = settle(
        "attn", replicas, rep, summed, [block_gains, block_velocity, head_gains, head_velocity], left_attn, attn_moments,
        [weight_query, weight_keyval, weight_out], [velocity_query, velocity_keyval, velocity_out],
        [(ranks, query_rows), (2, ranks, group_cols), (ranks, depth)],
        [moment_query.shape, (2,) + moment_key.shape, moment_out.shape],
    )

    def turned_over(value):
        return jnp.swapaxes(value, -1, -2)

    def five(rest, at, left, right):
        errors, weights, velocities = rest
        return [weights[at], velocities[at], errors[at][None], turned_over(left), turned_over(right)]

    outputs = [layer_out, input_grad, *gains]
    outputs += five(attn_rest, 0, left_attn[0][None], attn_rights[0])
    outputs += five(attn_rest, 1, left_attn[1][:, None], attn_rights[1])
    outputs += five(attn_rest, 2, left_attn[2], attn_rights[2][None])
    outputs += five(feed_rest, 0, left_feed[0][:, None], feed_rights[0])
    outputs += five(feed_rest, 1, left_feed[1], feed_rights[1][None])
    return tuple(outputs)


def solution(mesh):
    placed = (
        P("rep", None),
        P("rep", None),
        P("rep", None),
        P(),
        P(),
        P(),
        P(),
        P("rep", "kv"),
        P("rep", "kv"),
        P("rep", None, "kv"),
        P("kv", None),
        P(None, "rep", "kv"),
        P(None, "rep", "kv"),
        P("rep", None, None, "kv"),
        P(None, "kv", None),
        P(("kv", "rep"), None),
        P(("kv", "rep"), None),
        P("rep", "kv", None),
        P("kv", None, None),
        P(None, "rep", "kv"),
        P(None, "rep", "kv"),
        P("rep", None, None, "kv"),
        P(None, "kv", None),
        P(("kv", "rep"), None),
        P(("kv", "rep"), None),
        P("rep", "kv", None),
        P("kv", None, None),
    )
    return jax.shard_map(
        on_device,
        mesh=mesh,
        in_specs=placed,
        out_specs=(
            P(("rep", "kv"), None),
            P(("rep", "kv"), None),
            P(),
            P(),
            P(),
            P(),
            P("rep", "kv"),
            P("rep", "kv"),
            P("rep", None, "kv"),
            P("kv", None, None),
            P("kv", None),
            P(None, "rep", "kv"),
            P(None, "rep", "kv"),
            P("rep", None, None, "kv"),
            P(None, "kv", None, None),
            P(None, "kv", None),
            P(("kv", "rep"), None),
            P(("kv", "rep"), None),
            P("rep", "kv", None),
            P("kv", None),
            P("kv", None, None),
            P(None, "rep", "kv"),
            P(None, "rep", "kv"),
            P("rep", None, None, "kv"),
            P(None, "kv", None, None),
            P(None, "kv", None),
            P(("kv", "rep"), None),
            P(("kv", "rep"), None),
            P("rep", "kv", None),
            P("kv", None),
            P("kv", None, None),
        ),
        check_vma=False,
    )
```
